128 devices in a mesh: dp: 16 (over y_lo, x, core), tensor: 8 (over y_hi, z).
Axes of the slice: x: 4, y: 4 (y_hi: 2, y_lo: 2; y = y_hi * 2 + y_lo), z: 4, core: 2. Of those that a mesh axis runs over, the one named last changes fastest.
Arguments:
- tokens: bfloat16 [32768, 1152], P(('dp', 'tensor')), may hold values from -6 to 6
- picture: int32 [32768], P('dp'), may hold values from -1 to 10, as said below
- cotangent: bfloat16 [32768, 1152], P(('dp', 'tensor')), may hold values from -6 to 6
- gain_one: bfloat16 [1152], replicated, may hold values from 0.5 to 1.5
- shift_one: bfloat16 [1152], replicated, may hold values from -0.625 to 0.625
- query_weight: bfloat16 [1152, 1152], P('dp', 'tensor'), may hold values from -0.1875 to 0.1875
- query_bias: bfloat16 [1152], replicated, may hold values from -1.75 to 1.75
- key_weight: bfloat16 [1152, 1152], P('dp', 'tensor'), may hold values from -0.1875 to 0.1875
- value_weight: bfloat16 [1152, 1152], P('dp', 'tensor'), may hold values from -0.1875 to 0.1875
- value_bias: bfloat16 [1152], replicated, may hold values from -0.3125 to 0.3125
- out_weight: bfloat16 [1152, 1152], P('tensor', 'dp'), may hold values from -1 to 1
- out_bias: bfloat16 [1152], replicated, may hold values from -0.625 to 0.625
- gain_two: bfloat16 [1152], replicated, may hold values from 0.5 to 1.5
- shift_two: bfloat16 [1152], replicated, may hold values from -0.625 to 0.625
- up_weight: bfloat16 [1152, 4304], P('dp', 'tensor'), may hold values from -0.1875 to 0.1875
- up_bias: bfloat16 [4304], replicated, may hold values from -0.625 to 0.625
- down_weight: bfloat16 [4304, 1152], P('tensor', 'dp'), may hold values from -0.09375 to 0.09375
- down_bias: bfloat16 [1152], replicated, may hold values from -0.625 to 0.625
Outputs:
- result: float32 [32768, 1152], P(('dp', 'tensor'))
- grad_tokens: float32 [32768, 1152], P(('dp', 'tensor'))
- grad_query_weight: float32 [1152, 1152], P('dp', 'tensor')
- grad_key_weight: float32 [1152, 1152], P('dp', 'tensor')
- grad_value_weight: float32 [1152, 1152], P('dp', 'tensor')
- grad_out_weight: float32 [1152, 1152], P('tensor', 'dp')
- grad_up_weight: float32 [1152, 4304], P('dp', 'tensor')
- grad_down_weight: float32 [4304, 1152], P('tensor', 'dp')
- grad_query_bias: float32 [1152], replicated
- grad_value_bias: float32 [1152], replicated
- grad_up_bias: float32 [4304], replicated
- grad_out_bias: float32 [1152], replicated
- grad_down_bias: float32 [1152], replicated
- grad_gain_one: float32 [1152], replicated
- grad_shift_one: float32 [1152], replicated
- grad_gain_two: float32 [1152], replicated
- grad_shift_two: float32 [1152], replicated
- clipped_query_weight: float32 [1152, 1152], P('dp', 'tensor')
- clipped_key_weight: float32 [1152, 1152], P('dp', 'tensor')
The draws below stay inside these ranges and needn't reach their ends.
Inputs may be any that keep to these rules, and one draw needn't show every extreme that they name: Each packed row of 2048 slots holds whole pictures, contiguous runs of 100 to 1024 slots numbered 0, 1, 2, ... from the row's start, followed by padding marked -1 up to the row's end; the first picture of every row has exactly 1024 slots, and the last slot of every row is padding. Some row holds as many pictures as fit.
All inputs are finite; a program needn't handle non-finite values.
Results may differ from the reference program's by a relative error of at most 0.02.
Values may be sent and summed in bfloat16 or wider, within the bound.
A program may use at most 128 MiB of HBM per device.

```python
import jax
import jax.numpy as jnp
from jax import lax

D = 1152
HEADS = 16
HEAD_DIM = 72
FF = 4304
PIC_LEAST = 100
ROW = 2048
PIC_MOST = 1024
TOKENS = 32768


def draw_picture(key, part):
    key = jax.random.fold_in(key, 11)
    length_key = jax.random.fold_in(key, 1)
    row_key = jax.random.fold_in(key, 2)
    rows_total = TOKENS // ROW
    slots = ROW // PIC_LEAST + 1
    lengths = jax.random.randint(length_key, (rows_total, slots), PIC_LEAST, PIC_MOST + 1)
    chosen = jax.random.randint(row_key, (), 0, rows_total)
    row_index = jnp.arange(rows_total, dtype=jnp.int32)[:, None]
    column_index = jnp.arange(slots, dtype=jnp.int32)[None, :]
    lengths = jnp.where((row_index == chosen) & (column_index > 0), PIC_LEAST, lengths)
    lengths = jnp.where(column_index == 0, PIC_MOST, lengths)
    ends = jnp.cumsum(lengths, axis=1)
    positions = jnp.arange(ROW, dtype=jnp.int32)
    number = jnp.sum((ends[:, None, :] <= positions[None, :, None]).astype(jnp.int32), axis=2)
    fitting = jnp.sum((ends <= ROW - 1).astype(jnp.int32), axis=1)
    picture = jnp.where(number < fitting[:, None], number, -1)
    return picture.reshape(TOKENS).astype(jnp.int32)


def levels(rng, extent, cuts, smallest, largest):
    def one(position, shards_of):
        steps = jax.random.uniform(jax.random.fold_in(jax.random.fold_in(rng, 6), position), (shards_of,), jnp.float32, smallest / len(cuts), largest / len(cuts))
        return jnp.repeat(jnp.exp(steps), extent[position] // shards_of).reshape((-1,) + (1,) * (len(extent) - position - 1))

    level = one(*cuts[0])
    for cut in cuts[1:]:
        level = level * one(*cut)
    return level


def gaussian(key, shape, scale, bound, cuts=(), kind=jnp.bfloat16):
    array = jax.random.normal(key, shape, jnp.float32) * scale
    if len(cuts) > 0:
        array = levels(key, shape, cuts, -0.22, 0.18) * array
    return jnp.clip(array, min=-bound, max=bound).astype(kind)


def setup_inputs(seed: int = 0) -> dict:
    key_list = jax.random.split(jax.random.key(seed), 19)
    tokens = gaussian(key_list[0], (TOKENS, D), 1.0, 6.0, ((0, 128),))
    picture = draw_picture(jax.random.fold_in(key_list[18], 71), 0)
    cotangent = gaussian(key_list[2], (TOKENS, D), 1.0, 6.0, ((0, 128),))
    gain_one = jnp.clip(1.0 + 0.1 * jax.random.normal(key_list[3], (D,), jnp.float32), 0.5, 1.5).astype(jnp.bfloat16)
    shift_one = gaussian(key_list[4], (D,), 0.1, 0.625)
    query_weight = gaussian(key_list[5], (D, D), D ** -0.5, 0.1875, ((0, 16), (1, 8)))
    query_bias = gaussian(key_list[6], (D,), 0.3, 1.75)
    key_weight = gaussian(key_list[7], (D, D), D ** -0.5, 0.1875, ((0, 16), (1, 8)))
    value_weight = gaussian(key_list[8], (D, D), D ** -0.5, 0.1875, ((0, 16), (1, 8)))
    value_bias = gaussian(key_list[9], (D,), 0.05, 0.3125)
    out_weight = gaussian(key_list[10], (D, D), (max(D // 36, 16)) ** -0.5, 1.0, ((0, 8), (1, 16)))
    out_bias = gaussian(key_list[11], (D,), 0.1, 0.625)
    gain_two = jnp.clip(1.0 + 0.1 * jax.random.normal(key_list[12], (D,), jnp.float32), 0.5, 1.5).astype(jnp.bfloat16)
    shift_two = gaussian(key_list[13], (D,), 0.1, 0.625)
    up_weight = gaussian(key_list[14], (D, FF), D ** -0.5, 0.1875, ((0, 16), (1, 8)))
    up_bias = gaussian(key_list[15], (FF,), 0.1, 0.625)
    down_weight = gaussian(key_list[16], (FF, D), FF ** -0.5, 0.09375, ((0, 8), (1, 16)))
    down_bias = gaussian(key_list[17], (D,), 0.1, 0.625)
    return {"tokens": tokens, "picture": picture, "cotangent": cotangent, "gain_one": gain_one, "shift_one": shift_one, "query_weight": query_weight, "query_bias": query_bias, "key_weight": key_weight, "value_weight": value_weight, "value_bias": value_bias, "out_weight": out_weight, "out_bias": out_bias, "gain_two": gain_two, "shift_two": shift_two, "up_weight": up_weight, "up_bias": up_bias, "down_weight": down_weight, "down_bias": down_bias}


@jax.custom_vjp
def low(v):
    return lax.optimization_barrier(v.astype(jnp.bfloat16)).astype(jnp.float32)

@jax.custom_vjp
def low_back(v):
    return v

def low_keep(v):
    return (low(v), None)

def low_pass(kept, grad):
    return (grad,)

def back_keep(v):
    return (v, None)

def back_low(kept, grad):
    return (low(grad),)
low.defvjp(low_keep, low_pass)
low_back.defvjp(back_keep, back_low)
EPSILON = 1e-06
CLIP_LIMIT = 2.0

def layer_norm(values, gain, shift):
    centre = values - lax.optimization_barrier(jnp.mean(values, axis=-1, keepdims=True))
    spread = lax.optimization_barrier(jnp.mean(centre * centre, axis=-1, keepdims=True))
    return centre * lax.rsqrt(spread + EPSILON) * gain + shift

def matmul(left, right):
    return jnp.dot(left, right, preferred_element_type=jnp.float32, precision=lax.Precision.HIGHEST)

def row_attention(pieces):
    queries, keys_all, values_all, picture_row = pieces
    block_rows = min(512, ROW)
    blocks = ROW // block_rows
    positions = jnp.arange(ROW, dtype=jnp.int32)
    score_scale = HEAD_DIM ** (-0.5)

    def one_block(inner):
        query_block, query_ids, query_pos = inner
        scores = jnp.einsum('qhd,khd->hqk', query_block, keys_all, precision=lax.Precision.HIGHEST) * score_scale
        scores = low_back(scores)
        allowed = (query_ids[:, None] == picture_row[None, :]) & (query_ids[:, None] >= 0) | (query_pos[:, None] == positions[None, :])
        masked = jnp.where(allowed[None], scores, -1e+30)
        weights = jax.nn.softmax(masked, axis=-1)
        mixed = jnp.einsum('hqk,khd->qhd', low(weights), values_all, precision=lax.Precision.HIGHEST)
        real = allowed & (query_ids[:, None] >= 0)
        peak = lax.optimization_barrier(jnp.max(jnp.where(real[None], scores, -1e+30), axis=(1, 2)))
        return (mixed, peak)
    mixed, peak = lax.map(jax.checkpoint(one_block), (queries.reshape(blocks, block_rows, HEADS, HEAD_DIM), picture_row.reshape(blocks, block_rows), positions.reshape(blocks, block_rows)))
    return (mixed.reshape(ROW, HEADS, HEAD_DIM), lax.optimization_barrier(jnp.max(peak, axis=0)))

def forward(tokens, gain_one, shift_one, query_weight, query_bias, key_weight, value_weight, value_bias, out_weight, out_bias, gain_two, shift_two, up_weight, up_bias, down_weight, down_bias, picture):
    rows_total = TOKENS // ROW
    normed = low(layer_norm(tokens, gain_one, shift_one))
    queries = low_back(low(matmul(normed, query_weight) + query_bias))
    keys_all = low_back(low(matmul(normed, key_weight)))
    values_all = low_back(low(matmul(normed, value_weight) + value_bias))
    shape = (rows_total, ROW, HEADS, HEAD_DIM)
    mixed, peaks = lax.map(row_attention, (queries.reshape(shape), keys_all.reshape(shape), values_all.reshape(shape), picture.reshape(rows_total, ROW)))
    mixed = low_back(low(mixed.reshape(TOKENS, D)))
    branch = low_back(matmul(mixed, out_weight) + out_bias)
    middle = tokens + branch
    normed_two = low(layer_norm(middle, gain_two, shift_two))
    hidden = low_back(matmul(normed_two, up_weight) + up_bias)
    active = low(jax.nn.gelu(hidden, approximate=True))
    result = middle + low_back(matmul(active, down_weight) + down_bias)
    return (result, lax.optimization_barrier(jnp.max(peaks, axis=0)))

def reference(tokens, picture, cotangent, gain_one, shift_one, query_weight, query_bias, key_weight, value_weight, value_bias, out_weight, out_bias, gain_two, shift_two, up_weight, up_bias, down_weight, down_bias):
    floats = [array_item.astype(jnp.float32) for array_item in (tokens, gain_one, shift_one, query_weight, query_bias, key_weight, value_weight, value_bias, out_weight, out_bias, gain_two, shift_two, up_weight, up_bias, down_weight, down_bias)]

    def wrapped(*params):
        return forward(*params, picture)
    result, pullback, peaks = jax.vjp(wrapped, *floats, has_aux=True)
    grads = pullback(cotangent.astype(jnp.float32))
    factor = jnp.sqrt(CLIP_LIMIT / jnp.maximum(peaks, CLIP_LIMIT))
    column_factor = jnp.repeat(factor, HEAD_DIM)
    clipped_query = floats[3] * column_factor[None, :]
    clipped_key = floats[5] * column_factor[None, :]
    return (result, grads[0], grads[3], grads[5], grads[6], grads[8], grads[12], grads[14], grads[4], grads[7], grads[13], grads[9], grads[15], grads[1], grads[2], grads[10], grads[11], clipped_query, clipped_key)
```

```python
import functools

import jax
import jax.numpy as jnp
import numpy as np
from jax import lax
from jax.experimental import pallas as pl
from jax.experimental.pallas import tpu as pltpu
from jax.sharding import PartitionSpec as P

HEAD_DIM = 72
EPSILON = 1e-06
CLIP_LIMIT = 2.0
LOWEST = -1e30
SCALE = HEAD_DIM**-0.5

MESH = pl.DeviceIdType.MESH
LOW = jnp.bfloat16
FULL = jnp.float32

WIDTHS = (256, 128, 256, 256)
STARTS = (0, 256, 384, 640)
UNIT = 896
MAIN = 256
TAIL = 13
HIDDEN = 8 * MAIN + 128
PART_ROWS = 48
ORDERS = (("z", "y", "x"), ("x", "z", "y"), ("y", "x", "z"))
STEPS = (1, 3, 2)


def place():
    d, t = lax.axis_index("dp"), lax.axis_index("tensor")
    return {"x": (d // 2) % 4, "y": (t // 4) * 2 + d // 8, "z": t % 4, "core": d % 2}


def device(at):
    return ((at["y"] % 2) * 8 + at["x"] * 2 + at["core"], (at["y"] // 2) * 4 + at["z"])


def moved(at, axis, step):
    other = dict(at)
    other[axis] = 1 - at["core"] if axis == "core" else (at[axis] + step) % 4
    return other


def greet(partners):
    barrier = pltpu.get_barrier_semaphore()
    for partner in partners:
        pl.semaphore_signal(barrier, inc=1, device_id=device(partner), device_id_type=MESH)
    pl.semaphore_wait(barrier, len(partners))


class Copies:
    def __init__(self, send, receive):
        self.send, self.receive, self.used = send, receive, 0

    def start(self, source, target, partner):
        copy = pltpu.make_async_remote_copy(
            src_ref=source,
            dst_ref=target,
            send_sem=self.send.at[self.used],
            recv_sem=self.receive.at[self.used],
            device_id=device(partner),
            device_id_type=MESH,
        )
        self.used += 1
        copy.start()
        return copy


def rects(ref, width, part, have, at):
    xs = slice(None) if "x" in have else at["x"]
    if "y" in have:
        ys = slice(None)
        if "z" in have:
            lanes = [pl.ds(0, 8 * width)]
        else:
            lanes = [pl.ds(pl.multiple_of((h * 4 + at["z"]) * width, 128), width) for h in (0, 1)]
    else:
        ys = at["y"] % 2
        if "z" in have:
            lanes = [pl.ds(pl.multiple_of((at["y"] // 2) * 4 * width, 128), 4 * width)]
        else:
            lanes = [pl.ds(pl.multiple_of(((at["y"] // 2) * 4 + at["z"]) * width, 128), width)]
    return [ref.at[ys, xs, part, :, lane] for lane in lanes]


def gather_kernel(pack, n1, cot, ids, *rest):
    grids, (n1_other, cot_other, ids_other) = rest[:4], rest[4:7]
    both, unit, send, receive, local = rest[7:]
    at = place()
    core = at["core"]
    sibling = moved(at, "core", 1)
    greet([sibling] + [moved(at, axis, step) for axis in "xyz" for step in STEPS])
    copies = Copies(send, receive)
    rows = pl.ds(pl.multiple_of(core * 72, 8), 72)
    first = copies.start(pack.at[1 - core], both.at[rows], sibling)
    others = [
        copies.start(ids, ids_other, sibling),
        copies.start(n1, n1_other, sibling),
        copies.start(cot, cot_other, sibling),
    ]
    both[rows, :] = pack[core]
    first.wait_recv()
    for part in range(3):
        unit[part] = both[part * PART_ROWS : (part + 1) * PART_ROWS, :].astype(LOW)
    count = 0
    held = []
    for part in range(3):
        for grid, width, start in zip(grids, WIDTHS, STARTS):
            (target,) = rects(grid, width, part, (), at)
            copy = pltpu.make_async_copy(
                unit.at[part, :, pl.ds(start, width)], target, local.at[count]
            )
            copy.start()
            held.append(copy)
            count += 1
    for copy in held:
        copy.wait()
    sent = []
    arriving = [[], [], []]
    for phase in range(3):
        for part in range(3):
            for copy in arriving[part]:
                copy.wait_recv()
            have = ORDERS[part][:phase]
            axis = ORDERS[part][phase]
            arriving[part] = []
            for step in STEPS:
                partner = moved(at, axis, step)
                for grid, width in zip(grids, WIDTHS):
                    for view in rects(grid, width, part, have, at):
                        copy = copies.start(view, view, partner)
                        arriving[part].append(copy)
                        sent.append(copy)
    for part in range(3):
        for copy in arriving[part]:
            copy.wait_recv()
    for copy in others:
        copy.wait_recv()
    for copy in [first] + others + sent:
        copy.wait_send()


def hbm():
    return pl.BlockSpec(memory_space=pl.ANY)


def vmem():
    return pl.BlockSpec(memory_space=pltpu.VMEM)


def gather(pack, n1, cot, ids):
    count = 4 + 4 * 3 * 11
    lanes = (2048, 1024, HIDDEN, HIDDEN)
    return pl.pallas_call(
        gather_kernel,
        out_shape=[jax.ShapeDtypeStruct((2, 4, 3, PART_ROWS, lane), LOW) for lane in lanes]
        + [
            jax.ShapeDtypeStruct(n1.shape, LOW),
            jax.ShapeDtypeStruct(cot.shape, LOW),
            jax.ShapeDtypeStruct(ids.shape, FULL),
        ],
        in_specs=[vmem(), hbm(), hbm(), hbm()],
        out_specs=[hbm()] * 7,
        scratch_shapes=[
            pltpu.VMEM((144, UNIT), FULL),
            pltpu.VMEM((3, PART_ROWS, UNIT), LOW),
            pltpu.SemaphoreType.DMA((count,)),
            pltpu.SemaphoreType.DMA((count,)),
            pltpu.SemaphoreType.DMA((12,)),
        ],
        compiler_params=pltpu.CompilerParams(
            collective_id=0, has_side_effects=True, vmem_limit_bytes=16 << 20
        ),
        name="gather_weights",
    )(pack, n1, cot, ids)


def add_up(target, terms, shape):
    lead = int(np.prod(shape[:-2]))

    def index(number, ref):
        where, left = [], number
        for size in reversed(shape[:-2]):
            where.append(left % size)
            left = left // size
        return tuple(reversed(where))

    @pl.loop(0, lead * 3)
    def _(number):
        rows = pl.ds(pl.multiple_of((number % 3) * 16, 16), 16)
        spot = index(number // 3, target) + (rows, slice(None))
        total = terms[0][spot].astype(FULL)
        for term in terms[1:]:
            total = total + term[spot].astype(FULL)
        target[spot] = total.astype(target.dtype)


def first_shape(part, width):
    return ((2, 48, 8 * width), (4, 48, 4 * width), (2, 2, 4, 48, width))[part]


def second_shape(part, width):
    return ((48, 4 * width), (4, 48, width), (2, 2, 48, width))[part]


def first_views(ref, part, at):
    return [ref.at[h] for h in (0, 1)] if part == 2 else [ref]


def second_view(ref, part, width, at):
    if part == 0:
        lanes = pl.ds(pl.multiple_of((at["y"] // 2) * 4 * width, 128), 4 * width)
        return ref.at[at["y"] % 2, :, lanes]
    if part == 1:
        return ref.at[:, :, pl.ds(pl.multiple_of(at["z"] * width, 128), width)]
    return ref.at[:, :, at["x"]]


def third_view(ref, part, width, at):
    if part == 0:
        return ref.at[:, pl.ds(pl.multiple_of(at["z"] * width, 128), width)]
    if part == 1:
        return ref.at[at["x"]]
    return ref.at[at["y"] // 2, at["y"] % 2]


def scatter_kernel(*refs):
    grids, (vector, out, totals) = refs[:4], refs[4:7]
    rest = list(refs[7:])

    def take(count):
        taken, rest[:] = rest[:count], rest[count:]
        return taken

    own1 = [take(4) for _ in range(3)]
    got1 = [take(4) for _ in range(3)]
    sum1 = [take(4) for _ in range(3)]
    got2 = [take(4) for _ in range(3)]
    sum2 = [take(4) for _ in range(3)]
    got3 = [take(4) for _ in range(3)]
    whole, other, line, lines, send, receive, local = rest
    at = place()
    core = at["core"]
    sibling = moved(at, "core", 1)
    greet([sibling] + [moved(at, axis, step) for axis in "xyz" for step in STEPS])
    copies = Copies(send, receive)
    sent = []

    def send_line(phase):
        started = [
            copies.start(line.at[phase], lines.at[phase, k], moved(at, "xyz"[phase], step))
            for k, step in enumerate(STEPS)
        ]
        sent.extend(started)
        return started

    def add_line(phase, started):
        for copy in started:
            copy.wait_recv()
        parts = [line[phase]] + [lines[phase, k] for k in range(3)]
        line[phase + 1, 0:88, :] = (parts[0][:88] + parts[1][:88]) + (parts[2][:88] + parts[3][:88])
        line[phase + 1, 88:96, :] = jnp.maximum(
            jnp.maximum(parts[0][88:], parts[1][88:]), jnp.maximum(parts[2][88:], parts[3][88:])
        )

    line[0] = vector[...]
    lines_out = send_line(0)
    arriving = [[], [], []]
    held = [[], [], []]
    count = 0
    for part in range(3):
        axis, have = ORDERS[part][2], ORDERS[part][:2]
        for k, step in enumerate(STEPS):
            partner = moved(at, axis, step)
            for a in range(4):
                views = rects(grids[a], WIDTHS[a], part, have, partner)
                targets = first_views(got1[part][a].at[k], part, at)
                for view, target in zip(views, targets):
                    copy = copies.start(view, target, partner)
                    arriving[part].append(copy)
                    sent.append(copy)
        for a in range(4):
            views = rects(grids[a], WIDTHS[a], part, have, at)
            for view, target in zip(views, first_views(own1[part][a], part, at)):
                copy = pltpu.make_async_copy(view, target, local.at[count])
                copy.start()
                held[part].append(copy)
                count += 1
    add_line(0, lines_out)
    lines_out = send_line(1)
    arriving2 = [[], [], []]
    for part in range(3):
        for copy in held[part]:
            copy.wait()
        for copy in arriving[part]:
            copy.wait_recv()
        for a in range(4):
            got = got1[part][a]
            add_up(
                sum1[part][a],
                [own1[part][a]] + [got.at[k] for k in range(3)],
                first_shape(part, WIDTHS[a]),
            )
        axis = ORDERS[part][1]
        for k, step in enumerate(STEPS):
            partner = moved(at, axis, step)
            for a in range(4):
                view = second_view(sum1[part][a], part, WIDTHS[a], partner)
                copy = copies.start(view, got2[part][a].at[k], partner)
                arriving2[part].append(copy)
                sent.append(copy)
    add_line(1, lines_out)
    lines_out = send_line(2)
    arriving3 = [[], [], []]
    for part in range(3):
        for copy in arriving2[part]:
            copy.wait_recv()
        for a in range(4):
            got = got2[part][a]
            add_up(
                sum2[part][a],
                [second_view(sum1[part][a], part, WIDTHS[a], at)] + [got.at[k] for k in range(3)],
                second_shape(part, WIDTHS[a]),
            )
        axis = ORDERS[part][0]
        for k, step in enumerate(STEPS):
            partner = moved(at, axis, step)
            for a in range(4):
                view = third_view(sum2[part][a], part, WIDTHS[a], partner)
                copy = copies.start(view, got3[part][a].at[k], partner)
                arriving3[part].append(copy)
                sent.append(copy)
    add_line(2, lines_out)
    last = copies.start(line.at[3], totals.at[core], sibling)
    sent.append(last)
    for part in range(3):
        for copy in arriving3[part]:
            copy.wait_recv()
        for a in range(4):
            got = got3[part][a]
            total = third_view(sum2[part][a], part, WIDTHS[a], at)[...].astype(FULL)
            for k in range(3):
                total = total + got[k].astype(FULL)
            whole[
                part * PART_ROWS : (part + 1) * PART_ROWS, STARTS[a] : STARTS[a] + WIDTHS[a]
            ] = total
    swap = copies.start(
        whole.at[pl.ds(pl.multiple_of((1 - core) * 72, 8), 72)], other, sibling
    )
    sent.append(swap)
    totals[core] = line[3]
    out[core] = whole[pl.ds(pl.multiple_of(core * 72, 8), 72), :]
    swap.wait_recv()
    out[1 - core] = other[...]
    last.wait_recv()
    for copy in sent:
        copy.wait_send()


def scatter(grids, vector):
    count = 3 * 3 + 3 * 4 * (4 + 3 + 3) + 2
    shapes = []
    for part in range(3):
        shapes += [pltpu.VMEM(first_shape(part, w), LOW) for w in WIDTHS]
    for part in range(3):
        shapes += [pltpu.VMEM((3,) + first_shape(part, w), LOW) for w in WIDTHS]
    for part in range(3):
        shapes += [pltpu.VMEM(first_shape(part, w), LOW) for w in WIDTHS]
    for part in range(3):
        shapes += [pltpu.VMEM((3,) + second_shape(part, w), LOW) for w in WIDTHS]
    for part in range(3):
        shapes += [pltpu.VMEM(second_shape(part, w), LOW) for w in WIDTHS]
    for part in range(3):
        shapes += [pltpu.VMEM((3, 48, w), LOW) for w in WIDTHS]
    return pl.pallas_call(
        scatter_kernel,
        out_shape=[
            jax.ShapeDtypeStruct((2, 72, UNIT), FULL),
            jax.ShapeDtypeStruct((2, 96, 128), FULL),
        ],
        in_specs=[hbm()] * 4 + [vmem()],
        out_specs=[vmem()] * 2,
        scratch_shapes=shapes
        + [
            pltpu.VMEM((144, UNIT), FULL),
            pltpu.VMEM((72, UNIT), FULL),
            pltpu.VMEM((4, 96, 128), FULL),
            pltpu.VMEM((3, 3, 96, 128), FULL),
            pltpu.SemaphoreType.DMA((count,)),
            pltpu.SemaphoreType.DMA((count,)),
            pltpu.SemaphoreType.DMA((16,)),
        ],
        compiler_params=pltpu.CompilerParams(
            collective_id=1, has_side_effects=True, vmem_limit_bytes=48 << 20
        ),
        name="scatter_grads",
    )(*grids, vector)


def swap_kernel(mine, theirs, send, receive):
    sibling = moved(place(), "core", 1)
    greet([sibling])
    Copies(send, receive).start(mine, theirs, sibling).wait()


def swap(mine, number):
    return pl.pallas_call(
        swap_kernel,
        out_shape=jax.ShapeDtypeStruct(mine.shape, mine.dtype),
        in_specs=[hbm()],
        out_specs=hbm(),
        scratch_shapes=[pltpu.SemaphoreType.DMA((1,)), pltpu.SemaphoreType.DMA((1,))],
        compiler_params=pltpu.CompilerParams(collective_id=number, has_side_effects=True),
        name=f"swap_{number}",
    )(mine)


def picker(which):
    row = lax.broadcasted_iota(jnp.int32, (256, 128), 0)
    lane = lax.broadcasted_iota(jnp.int32, (256, 128), 1)
    return jnp.where((row == lane + HEAD_DIM * which) & (lane < HEAD_DIM), 1.0, 0.0).astype(LOW)


def placer(which):
    row = lax.broadcasted_iota(jnp.int32, (128, 256), 0)
    lane = lax.broadcasted_iota(jnp.int32, (128, 256), 1)
    return jnp.where((lane == row + HEAD_DIM * which) & (row < HEAD_DIM), 1.0, 0.0).astype(LOW)


def dot(left, right):
    return jnp.dot(left, right, preferred_element_type=FULL)


def dot_rows(left, right):
    return lax.dot_general(left, right, (((0,), (0,)), ((), ())), preferred_element_type=FULL)


def dot_cols(left, right):
    return lax.dot_general(left, right, (((1,), (1,)), ((), ())), preferred_element_type=FULL)


def attend_kernel(
    proj, ids_row, ids_col, mixed, qkv, logsum, peak, q_s, k_s, v_s, out_s, top_s, send, receive, local
):
    at = place()
    z = at["z"]
    partners = [moved(at, "z", step) for step in STEPS]
    greet(partners)
    copies = Copies(send, receive)

    def lanes(index, width):
        return pl.ds(pl.multiple_of(index * width, 128), width)

    started = [
        copies.start(proj.at[:, lanes(partner["z"], 512)], qkv.at[z], partner)
        for partner in partners
    ]
    own = pltpu.make_async_copy(proj.at[:, lanes(z, 512)], qkv.at[z], local.at[0])
    own.start()
    own.wait()
    for copy in started:
        copy.wait_recv()
    for r in range(2):
        for j in range(2):
            for b in range(4):
                block = qkv[b, r * 256 : (r + 1) * 256, j * 256 : (j + 1) * 256]
                spot = slice(b * 256, (b + 1) * 256)
                q_s[2 * r + j, spot, :] = dot(block, picker(0)).astype(LOW)
                k_s[2 * r + j, spot, :] = dot(block, picker(1)).astype(LOW)
                v_s[2 * r + j, spot, :] = dot(block, picker(2)).astype(LOW)
    top_s[...] = jnp.full(top_s.shape, LOWEST, FULL)
    back = []
    for step in STEPS + (0,):
        b = (z + step) % 4
        rows = pl.ds(pl.multiple_of(b * 256, 256), 256)

        @pl.loop(0, 4)
        def _(n, b=b, rows=rows):
            r, j = n // 2, n % 2
            scores = dot_cols(q_s[n, rows, :], k_s[n]) * SCALE
            mine = ids_col[r, rows, :]
            scores = jnp.where(mine == ids_row[r], scores, LOWEST)
            top = jnp.max(scores, axis=1, keepdims=True)
            expo = jnp.exp(scores - top)
            total = jnp.sum(expo, axis=1, keepdims=True)
            weights = (expo * (1.0 / total)).astype(LOW)
            out_s[n, b] = dot(weights, v_s[n]).astype(LOW)
            logsum[n, rows, :] = top + jnp.log(total)
            top_s[n] = jnp.maximum(top_s[n], jnp.where(mine >= 0.0, top, LOWEST))

        for n in range(4):
            r, j = n // 2, n % 2
            source = out_s.at[n, b]
            spot = (pl.ds(r * 256, 256), pl.ds(pl.multiple_of(z * 256 + j * 128, 128), 128))
            if step:
                back.append(copies.start(source, mixed.at[spot], moved(at, "z", step)))
            else:
                copy = pltpu.make_async_copy(source, mixed.at[spot], local.at[1 + n])
                copy.start()
                back.append(copy)
    row = lax.broadcasted_iota(jnp.int32, (8, 128), 0)
    high = [jnp.maximum(jnp.max(top_s[j]), jnp.max(top_s[2 + j])) for j in range(2)]
    peak[...] = jnp.where(row == 0, high[0], high[1])
    for copy in back[:12]:
        copy.wait_recv()
    for copy in back[12:]:
        copy.wait()
    for copy in started + back[:12]:
        copy.wait_send()


def attend(proj, ids_row, ids_col):
    return pl.pallas_call(
        attend_kernel,
        out_shape=[
            jax.ShapeDtypeStruct((512, 1024), LOW),
            jax.ShapeDtypeStruct((4, 512, 512), LOW),
            jax.ShapeDtypeStruct((4, 1024, 1), FULL),
            jax.ShapeDtypeStruct((8, 128), FULL),
        ],
        in_specs=[hbm(), vmem(), vmem()],
        out_specs=[hbm(), vmem(), vmem(), vmem()],
        scratch_shapes=[pltpu.VMEM((4, 1024, 128), LOW)] * 3
        + [
            pltpu.VMEM((4, 4, 256, 128), LOW),
            pltpu.VMEM((4, 256, 1), FULL),
            pltpu.SemaphoreType.DMA((15,)),
            pltpu.SemaphoreType.DMA((15,)),
            pltpu.SemaphoreType.DMA((5,)),
        ],
        compiler_params=pltpu.CompilerParams(
            collective_id=2, has_side_effects=True, vmem_limit_bytes=40 << 20
        ),
        name="attend",
    )(proj, ids_row, ids_col)


def attend_back_kernel(
    upstream, qkv, ids_row, ids_col, logsum, back, grad, q_s, k_s, v_s, g_s, dq_s, dk_s, dv_s, out_s,
    send, receive, local,
):
    at = place()
    z = at["z"]
    partners = [moved(at, "z", step) for step in STEPS]
    greet(partners)
    copies = Copies(send, receive)

    def lanes(index, width):
        return pl.ds(pl.multiple_of(index * width, 128), width)

    started = [
        copies.start(upstream.at[:, lanes(partner["z"], 256)], grad.at[z], partner)
        for partner in partners
    ]
    own = pltpu.make_async_copy(upstream.at[:, lanes(z, 256)], grad.at[z], local.at[0])
    own.start()
    for r in range(2):
        for j in range(2):
            for b in range(4):
                block = qkv[b, r * 256 : (r + 1) * 256, j * 256 : (j + 1) * 256]
                spot = slice(b * 256, (b + 1) * 256)
                q_s[2 * r + j, spot, :] = dot(block, picker(0)).astype(LOW)
                k_s[2 * r + j, spot, :] = dot(block, picker(1)).astype(LOW)
                v_s[2 * r + j, spot, :] = dot(block, picker(2)).astype(LOW)
    own.wait()
    for copy in started:
        copy.wait_recv()
    lane = lax.broadcasted_iota(jnp.int32, (256, 128), 1)
    for r in range(2):
        for j in range(2):
            for b in range(4):
                block = grad[b, r * 256 : (r + 1) * 256, j * 128 : (j + 1) * 128]
                g_s[2 * r + j, b * 256 : (b + 1) * 256, :] = jnp.where(
                    lane < HEAD_DIM, block.astype(FULL), 0.0
                ).astype(LOW)
    sent = []
    for r in range(2):
        for j in range(2):
            n = 2 * r + j
            dk_s[...] = jnp.zeros(dk_s.shape, FULL)
            dv_s[...] = jnp.zeros(dv_s.shape, FULL)

            @pl.loop(0, 4)
            def _(b, n=n, r=r):
                rows = pl.ds(pl.multiple_of(b * 256, 256), 256)
                query, upper = q_s[n, rows, :], g_s[n, rows, :]
                scores = dot_cols(query, k_s[n]) * SCALE
                allowed = ids_col[r, rows, :] == ids_row[r]
                probs = jnp.where(allowed, jnp.exp(scores - logsum[n, rows, :]), 0.0)
                dv_s[...] += dot_rows(probs.astype(LOW), upper)
                prob_grad = dot_cols(upper, v_s[n])
                centre = jnp.sum(probs * prob_grad, axis=1, keepdims=True)
                score_grad = (probs * (prob_grad - centre)).astype(LOW)
                dq_s[rows, :] = (dot(score_grad, k_s[n]) * SCALE).astype(LOW)
                dk_s[...] += dot_rows(score_grad, query)

            for b in range(4):
                spot = slice(b * 256, (b + 1) * 256)
                out_s[b, r * 256 : (r + 1) * 256, j * 256 : (j + 1) * 256] = (
                    dot(dq_s[spot, :], placer(0))
                    + dot((dk_s[spot, :] * SCALE).astype(LOW), placer(1))
                    + dot(dv_s[spot, :].astype(LOW), placer(2))
                ).astype(LOW)
        rows = pl.ds(r * 256, 256)
        for partner in partners:
            source = out_s.at[partner["z"], rows]
            sent.append(copies.start(source, back.at[rows, lanes(z, 512)], partner))
        copy = pltpu.make_async_copy(
            out_s.at[z, rows], back.at[rows, lanes(z, 512)], local.at[1 + r]
        )
        copy.start()
        sent.append(copy)
    for k, copy in enumerate(sent):
        copy.wait()
    for copy in started:
        copy.wait_send()


def attend_back(upstream, qkv, ids_row, ids_col, logsum):
    return pl.pallas_call(
        attend_back_kernel,
        out_shape=jax.ShapeDtypeStruct((512, 2048), LOW),
        in_specs=[hbm(), vmem(), vmem(), vmem(), vmem()],
        out_specs=hbm(),
        scratch_shapes=[pltpu.VMEM((4, 512, 256), LOW)]
        + [pltpu.VMEM((4, 1024, 128), LOW)] * 4
        + [
            pltpu.VMEM((1024, 128), LOW),
            pltpu.VMEM((1024, 128), FULL),
            pltpu.VMEM((1024, 128), FULL),
            pltpu.VMEM((4, 512, 512), LOW),
            pltpu.SemaphoreType.DMA((9,)),
            pltpu.SemaphoreType.DMA((9,)),
            pltpu.SemaphoreType.DMA((3,)),
        ],
        compiler_params=pltpu.CompilerParams(
            collective_id=3, has_side_effects=True, vmem_limit_bytes=40 << 20
        ),
        name="attend_back",
    )(upstream, qkv, ids_row, ids_col, logsum)


def normalize(values, gain, shift):
    centre = values - jnp.mean(values, axis=-1, keepdims=True)
    inverse = lax.rsqrt(jnp.mean(centre * centre, axis=-1, keepdims=True) + EPSILON)
    scaled = centre * inverse
    return (scaled * gain + shift, scaled, inverse)


def normalize_back(upstream, scaled, inverse, gain):
    along = upstream * gain
    width_mean = jnp.mean(along, axis=-1, keepdims=True)
    cross_mean = jnp.mean(along * scaled, axis=-1, keepdims=True)
    return inverse * (along - width_mean - scaled * cross_mean)


def smooth(inner):
    return jax.nn.gelu(inner, approximate=True)


def selector(offset):
    matrix = np.zeros((1024, 128), np.float32)
    for t in range(8):
        for i in range(TAIL):
            matrix[128 * t + offset + i, TAIL * t + i] = 1.0
    return jnp.asarray(matrix, LOW)


def per_device(
    tokens,
    picture,
    cotangent,
    gain_one,
    shift_one,
    query_weight,
    query_bias,
    key_weight,
    value_weight,
    value_bias,
    out_weight,
    out_bias,
    gain_two,
    shift_two,
    up_weight,
    up_bias,
    down_weight,
    down_bias,
):
    width = tokens.shape[1]
    t = lax.axis_index("tensor")
    core = lax.axis_index("dp") % 2
    z = t % 4
    gain_first = gain_one.astype(FULL)
    gain_second = gain_two.astype(FULL)

    out_t = out_weight.astype(FULL).T
    down_t = down_weight.astype(FULL).T
    up = up_weight.astype(FULL)
    halves = []
    for h in range(2):
        cols = slice(h * 72, (h + 1) * 72)
        first = h * (MAIN + TAIL)
        main, tail = slice(first, first + MAIN), slice(first + MAIN, first + MAIN + TAIL)
        halves.append(
            jnp.concatenate(
                [
                    query_weight[:, cols].astype(FULL),
                    key_weight[:, cols].astype(FULL),
                    value_weight[:, cols].astype(FULL),
                    jnp.zeros((72, 40), FULL),
                    out_t[:, cols],
                    up[:, tail],
                    down_t[:, tail],
                    jnp.zeros((72, 30), FULL),
                    up[:, main],
                    down_t[:, main],
                ],
                axis=1,
            )
        )
    pack = jnp.stack(halves)

    inputs = tokens.astype(FULL)
    normed, scaled_one, inverse_one = normalize(inputs, gain_first, shift_one.astype(FULL))
    normed_mine = normed.astype(LOW)
    half = lax.dynamic_slice_in_dim(picture, (t // 4) * 1024, 1024)
    ids = jnp.where(half >= 0, half, -1 - jnp.arange(1024, dtype=jnp.int32)).astype(FULL)
    gq, go, gu, gd, normed_other, cot_other, ids_other = gather(
        pack, normed_mine, cotangent, ids.reshape(8, 128)
    )
    gq, go = gq.reshape(width, 2048), go.reshape(width, 1024)
    select_up, select_down = selector(72), selector(72 + TAIL)
    gu = lax.dynamic_update_slice(
        gu.reshape(width, HIDDEN), dot(go, select_up).astype(LOW), (0, 2048)
    )
    gd = lax.dynamic_update_slice(
        gd.reshape(width, HIDDEN), dot(go, select_down).astype(LOW), (0, 2048)
    )
    both_ids = jnp.stack([ids, ids_other.reshape(1024)])
    ids_row, ids_col = both_ids.reshape(2, 1, 1024), both_ids.reshape(2, 1024, 1)

    def halves_of(vector, size):
        return lax.dynamic_index_in_dim(
            vector.astype(FULL).reshape(8, 2, size), core, axis=1, keepdims=False
        )

    query_b, value_b = halves_of(query_bias, 72), halves_of(value_bias, 72)
    proj_bias = jnp.concatenate(
        [query_b, jnp.zeros((8, 72), FULL), value_b, jnp.zeros((8, 40), FULL)], axis=1
    ).reshape(2048)
    up_b = halves_of(up_bias, MAIN + TAIL)
    hidden_bias = jnp.concatenate(
        [up_b[:, :MAIN].reshape(2048), up_b[:, MAIN:].reshape(8 * TAIL), jnp.zeros((24,), FULL)]
    )

    rows_one = jnp.concatenate([normed_mine, normed_other])
    proj = (dot(rows_one, gq) + proj_bias).astype(LOW)
    mixed, qkv, logsum, peak = attend(proj, ids_row, ids_col)
    part = dot_cols(mixed, go)
    branch = part[:256] + swap(part[256:].astype(LOW), 4).astype(FULL) + out_bias.astype(FULL)
    middle = inputs + branch
    normed_two, scaled_two, inverse_two = normalize(middle, gain_second, shift_two.astype(FULL))
    normed_two = normed_two.astype(LOW)
    rows_two = jnp.concatenate([normed_two, swap(normed_two, 5)])
    hidden = dot(rows_two, gu) + hidden_bias
    active = smooth(hidden).astype(LOW)
    part = dot_cols(active, gd)
    result = middle + (
        part[:256] + swap(part[256:].astype(LOW), 6).astype(FULL) + down_bias.astype(FULL)
    )

    upstream = cotangent.astype(FULL)
    cot_rows = jnp.concatenate([cotangent, cot_other])
    active_grad = dot(cot_rows, gd)
    _, gelu_back = jax.vjp(smooth, hidden)
    hidden_grad = gelu_back(active_grad)[0].astype(LOW)
    part = dot_cols(hidden_grad, gu)
    normed_two_grad = part[:256] + swap(part[256:].astype(LOW), 7).astype(FULL)
    middle_grad = upstream + normalize_back(normed_two_grad, scaled_two, inverse_two, gain_second)
    branch_low = middle_grad.astype(LOW)
    branch_rows = jnp.concatenate([branch_low, swap(branch_low, 8)])
    mixed_grad = dot(branch_rows, go).astype(LOW)
    proj_grad = attend_back(mixed_grad, qkv, ids_row, ids_col, logsum)
    part = dot_cols(proj_grad, gq)
    normed_one_grad = part[:256] + swap(part[256:].astype(LOW), 9).astype(FULL)
    input_grad = middle_grad + normalize_back(normed_one_grad, scaled_one, inverse_one, gain_first)

    grad_q = dot_rows(rows_one, proj_grad).astype(LOW)
    grad_u = dot_rows(rows_two, hidden_grad[:, :2048]).astype(LOW)
    grad_d = dot_rows(cot_rows, active[:, :2048]).astype(LOW)
    up_tail = dot_cols(hidden_grad[:, 2048:], select_up).astype(LOW)
    down_tail = dot_cols(active[:, 2048:], select_down).astype(LOW)
    grad_o = dot_rows(
        jnp.concatenate([branch_rows, rows_two, cot_rows]),
        jnp.concatenate([mixed, up_tail, down_tail]),
    ).astype(LOW)

    head = lax.broadcasted_iota(jnp.int32, (8, 128), 1)
    peaks = jnp.where(
        head == 4 * z + core,
        peak[0, 0],
        jnp.where(head == 4 * z + 2 + core, peak[1, 0], LOWEST),
    )

    def total(values):
        return jnp.sum(values.astype(FULL), axis=0)

    vector = jnp.concatenate(
        [
            total(proj_grad),
            total(hidden_grad),
            total(branch_low),
            total(upstream),
            total(normed_one_grad * scaled_one),
            total(normed_one_grad),
            total(normed_two_grad * scaled_two),
            total(normed_two_grad),
            jnp.zeros((128,), FULL),
        ]
    ).reshape(88, 128)
    vector = jnp.concatenate([vector, peaks])
    shape = (2, 4, 3, PART_ROWS)
    grads, totals = scatter(
        [
            grad_q.reshape(shape + (2048,)),
            grad_o.reshape(shape + (1024,)),
            grad_u.reshape(shape + (2048,)),
            grad_d.reshape(shape + (2048,)),
        ],
        vector,
    )

    def side(first, size):
        return jnp.concatenate([grads[0, :, first : first + size], grads[1, :, first : first + size]], axis=1)

    def hidden_side(main, tail):
        return jnp.concatenate(
            [
                grads[0, :, main : main + MAIN],
                grads[0, :, tail : tail + TAIL],
                grads[1, :, main : main + MAIN],
                grads[1, :, tail : tail + TAIL],
            ],
            axis=1,
        )

    query_w, key_w, value_w = side(0, 72), side(72, 72), side(144, 72)
    out_w = side(256, 72).T
    up_w = hidden_side(384, 256 + 72)
    down_w = hidden_side(640, 256 + 72 + TAIL).T
    flat = totals[:, :88].reshape(2, 88 * 128)
    heads = flat[:, :2048].reshape(2, 8, 256)
    query_b_grad = heads[:, :, :72].transpose(1, 0, 2).reshape(width)
    value_b_grad = heads[:, :, 144:216].transpose(1, 0, 2).reshape(width)
    up_b_grad = (
        jnp.concatenate(
            [
                flat[:, 2048:4096].reshape(2, 8, MAIN),
                flat[:, 4096 : 4096 + 8 * TAIL].reshape(2, 8, TAIL),
            ],
            axis=2,
        )
        .transpose(1, 0, 2)
        .reshape(-1)
    )
    summed = (flat[0] + flat[1])[2048 + HIDDEN : 2048 + HIDDEN + 6 * width].reshape(6, width)
    high = jnp.maximum(totals[0, 88, :16], totals[1, 88, :16])
    factor = jnp.sqrt(CLIP_LIMIT / jnp.maximum(high, CLIP_LIMIT))
    column_factor = jnp.repeat(lax.dynamic_slice_in_dim(factor, 2 * t, 2), HEAD_DIM)
    clipped_query = query_weight.astype(FULL) * column_factor[None, :]
    clipped_key = key_weight.astype(FULL) * column_factor[None, :]
    return (
        result,
        input_grad,
        query_w,
        key_w,
        value_w,
        out_w,
        up_w,
        down_w,
        query_b_grad,
        value_b_grad,
        up_b_grad,
        summed[0],
        summed[1],
        summed[2],
        summed[3],
        summed[4],
        summed[5],
        clipped_query,
        clipped_key,
    )


def solution(mesh):
    in_specs = (
        P(("dp", "tensor"), None),
        P("dp"),
        P(("dp", "tensor"), None),
        P(),
        P(),
        P("dp", "tensor"),
        P(),
        P("dp", "tensor"),
        P("dp", "tensor"),
        P(),
        P("tensor", "dp"),
        P(),
        P(),
        P(),
        P("dp", "tensor"),
        P(),
        P("tensor", "dp"),
        P(),
    )
    out_specs = (
        P(("dp", "tensor"), None),
        P(("dp", "tensor"), None),
        P("dp", "tensor"),
        P("dp", "tensor"),
        P("dp", "tensor"),
        P("tensor", "dp"),
        P("dp", "tensor"),
        P("tensor", "dp"),
        P(),
        P(),
        P(),
        P(),
        P(),
        P(),
        P(),
        P(),
        P(),
        P("dp", "tensor"),
        P("dp", "tensor"),
    )
    return jax.shard_map(
        per_device, mesh=mesh, in_specs=in_specs, out_specs=out_specs, check_vma=False
    )
```

```python
import functools

import jax
import jax.numpy as jnp
import numpy as np
from jax import lax
from jax.experimental import pallas as pl
from jax.experimental.pallas import tpu as pltpu
from jax.sharding import PartitionSpec as P

HEAD_DIM = 72
EPSILON = 1e-06
CLIP_LIMIT = 2.0
LOWEST = -1e30
SCALE = HEAD_DIM**-0.5

MESH = pl.DeviceIdType.MESH
LOW = jnp.bfloat16
FULL = jnp.float32

WIDTHS = (256, 128, 256, 256)
STARTS = (0, 256, 384, 640)
UNIT = 896
MAIN = 256
TAIL = 13
HIDDEN = 8 * MAIN + 128
PARTS = ((0, 48, "zyx"), (48, 48, "xzy"), (96, 48, "yxz"))
PARTS_BEHIND = ((0, 64, "zyx"), (64, 64, "zxy"), (128, 16, "yxz"))
STEPS = (1, 3, 2)
ALL = "xyz"


def place():
    d, t = lax.axis_index("dp"), lax.axis_index("tensor")
    return {"x": (d // 2) % 4, "y": (t // 4) * 2 + d // 8, "z": t % 4, "core": d % 2}


def device(at):
    return ((at["y"] % 2) * 8 + at["x"] * 2 + at["core"], (at["y"] // 2) * 4 + at["z"])


def moved(at, axis, step):
    other = dict(at)
    other[axis] = 1 - at["core"] if axis == "core" else (at[axis] + step) % 4
    return other


def greet(partners):
    barrier = pltpu.get_barrier_semaphore()
    for partner in partners:
        pl.semaphore_signal(barrier, inc=1, device_id=device(partner), device_id_type=MESH)
    pl.semaphore_wait(barrier, len(partners))


class Copies:
    def __init__(self, send, receive):
        self.send, self.receive, self.used = send, receive, 0

    def start(self, source, target, partner):
        copy = pltpu.make_async_remote_copy(
            src_ref=source,
            dst_ref=target,
            send_sem=self.send.at[self.used],
            recv_sem=self.receive.at[self.used],
            device_id=device(partner),
            device_id_type=MESH,
        )
        self.used += 1
        copy.start()
        return copy


def lanes(first, size):
    return pl.ds(first if isinstance(first, int) else pl.multiple_of(first, 128), size)


def spots(held, have, at, width, rows, half=None):
    zs, ys = (4 if "z" in held else 1), at["y"] if "y" in held else 0
    x_at = pl.ds(0, 4) if "x" in have else pl.ds(at["x"] if "x" in held else 0, 1)
    y_at = pl.ds(0, 2) if "y" in have else pl.ds(ys % 2, 1)
    z = at["z"] if "z" in held else 0
    if "y" in have and "z" in have:
        ranges = [(0, 8 * width)]
    elif "y" in have:
        ranges = [((h * zs + z) * width, width) for h in (0, 1)]
    elif "z" in have:
        ranges = [((ys // 2) * zs * width, 4 * width)]
    else:
        ranges = [(((ys // 2) * zs + z) * width, width)]
    if half is not None:
        if len(ranges) == 2:
            ranges = [ranges[half]]
        elif "x" in have:
            x_at = pl.ds(2 * half, 2)
        elif "y" in have:
            y_at = pl.ds(half, 1)
        else:
            ((first, size),) = ranges
            ranges = [(first + half * (size // 2), size // 2)]
    return [(y_at, x_at, pl.ds(*rows), lanes(*r)) for r in ranges]


def rect_shape(have, width, rows):
    ys, xs, zs = 2 if "y" in have else 1, 4 if "x" in have else 1, 4 if "z" in have else 1
    return (ys, xs, rows, ys * zs * width)


class Gather:
    def __init__(self, copies, at, grids, widths, part):
        self.copies, self.at, self.grids, self.widths = copies, at, grids, widths
        self.rows, self.order = part[:2], part[2]
        self.arriving, self.sent = [], []

    def views(self, grid, width, have, at, half=None):
        return [grid.at[spot] for spot in spots(ALL, have, at, width, self.rows, half)]

    def send(self, have, owner, partner, half=None):
        started = []
        for grid, width in zip(self.grids, self.widths):
            for view in self.views(grid, width, have, owner, half):
                started.append(self.copies.start(view, view, partner))
        self.sent += started
        return started

    def settle(self):
        for copy in self.arriving:
            copy.wait_recv()
        self.arriving = []

    def first(self):
        for step in STEPS:
            self.arriving += self.send("", self.at, moved(self.at, self.order[0], step))

    def ring(self, phase):
        self.settle()
        axis, have = self.order[phase], self.order[:phase]
        self.after = self.send(have, self.at, moved(self.at, axis, 1))
        self.before = self.send(have, self.at, moved(self.at, axis, 3))

    def forward(self, phase):
        axis, have = self.order[phase], self.order[:phase]
        up, down = moved(self.at, axis, 1), moved(self.at, axis, 3)
        for copy in self.after:
            copy.wait_recv()
        self.arriving += self.send(have, down, up, 0)
        for copy in self.before:
            copy.wait_recv()
        self.arriving += self.send(have, up, down, 1)


def add_into(target, terms, shape):
    @pl.loop(0, shape[0] * shape[1] * (shape[2] // 16))
    def _(n):
        block = n // (shape[2] // 16)
        spot = (
            block // shape[1],
            block % shape[1],
            pl.ds(pl.multiple_of((n % (shape[2] // 16)) * 16, 16), 16),
            slice(None),
        )
        total = terms[0][spot].astype(FULL)
        for term in terms[1:]:
            total = total + term[spot].astype(FULL)
        target[spot] = total.astype(target.dtype)


def half_shape(have, shape):
    ys, xs, rows, cols = shape
    if "y" in have and "z" not in have:
        return (ys, xs, rows, cols // 2)
    if "x" in have:
        return (ys, 2, rows, cols)
    if "y" in have:
        return (1, xs, rows, cols)
    return (ys, xs, rows, cols // 2)


class Scatter:
    BUFFERS = 5 + 5 + 1

    @staticmethod
    def shapes(widths, part):
        _, rows, order = part
        shapes = []
        for have in (order[:2], order[:1]):
            for _ in range(5):
                shapes += [pltpu.VMEM(rect_shape(have, w, rows), LOW) for w in widths]
        shapes += [pltpu.VMEM((3, 1, 1, rows, w), LOW) for w in widths]
        return shapes

    def __init__(self, copies, at, grids, widths, part, buffers, local):
        self.copies, self.at, self.grids, self.widths = copies, at, grids, widths
        self.rows, self.order = part[:2], part[2]
        n = len(widths)
        groups = [buffers[k * n : (k + 1) * n] for k in range(self.BUFFERS)]
        self.near, self.mix, self.low, self.high, self.own = (
            [groups[0], groups[5]],
            [groups[1], groups[6]],
            [groups[2], groups[7]],
            [groups[3], groups[8]],
            [groups[4], groups[9]],
        )
        self.direct = groups[10]
        self.local = local
        self.sent = []

    def source(self, phase, a, at, half=None):
        have = self.order[: 2 - phase]
        if phase == 0:
            found = spots(ALL, have, at, self.widths[a], self.rows, half)
            return [self.grids[a].at[spot] for spot in found]
        held = self.order[: 3 - phase]
        found = spots(held, have, at, self.widths[a], (0, self.rows[1]), half)
        return [self.own[phase - 1][a].at[spot] for spot in found]

    def target(self, phase, buffer, a, half=None):
        have = self.order[: 2 - phase]
        found = spots(have, have, self.at, self.widths[a], (0, self.rows[1]), half)
        return [buffer[phase][a].at[spot] for spot in found]

    def push(self, sources, targets, partner):
        started = [self.copies.start(s, t, partner) for s, t in zip(sources, targets)]
        self.sent += started
        return started

    def begin(self, phase):
        axis = self.order[2 - phase]
        up, down, far = (moved(self.at, axis, step) for step in STEPS)
        self.arriving, self.loading = [], []
        for a in range(len(self.grids)):
            for half, partner in ((0, up), (1, down)):
                self.arriving += self.push(
                    self.source(phase, a, far, half),
                    self.target(phase, self.near, a, half),
                    partner,
                )
        if phase == 0:
            for a in range(len(self.grids)):
                pairs = list(
                    zip(
                        self.source(0, a, up, 0) + self.source(0, a, down, 1),
                        self.target(0, self.mix, a, 0) + self.target(0, self.mix, a, 1),
                    )
                )
                pairs += list(zip(self.source(0, a, self.at), self.target(0, self.own, a)))
                for view, target in pairs:
                    copy = pltpu.make_async_copy(view, target, self.local[0].at[self.local[1]])
                    self.local[1] += 1
                    copy.start()
                    self.loading.append(copy)

    def relay(self, phase):
        axis = self.order[2 - phase]
        have = self.order[: 2 - phase]
        up, down, _ = (moved(self.at, axis, step) for step in STEPS)
        for copy in self.loading:
            copy.wait()
        for copy in self.arriving:
            copy.wait_recv()
        self.arriving = []
        for a in range(len(self.grids)):
            shape = half_shape(have, rect_shape(have, self.widths[a], self.rows[1]))
            for half, partner in ((0, up), (1, down)):
                (mix,) = self.target(phase, self.mix, a, half)
                (near,) = self.target(phase, self.near, a, half)
                if phase == 0:
                    add_into(mix, [mix, near], shape)
                else:
                    (view,) = self.source(phase, a, partner, half)
                    add_into(mix, [view, near], shape)
                buffer = self.low if half == 0 else self.high
                self.arriving += self.push(
                    [mix] + self.source(phase, a, partner, 1 - half),
                    self.target(phase, buffer, a, half) + self.target(phase, buffer, a, 1 - half),
                    partner,
                )

    def finish(self, phase):
        have = self.order[: 2 - phase]
        for copy in self.arriving:
            copy.wait_recv()
        for a in range(len(self.grids)):
            for low, high, own, source in zip(
                self.target(phase, self.low, a),
                self.target(phase, self.high, a),
                self.target(phase, self.own, a),
                self.source(phase, a, self.at),
            ):
                shape = rect_shape(have, self.widths[a], self.rows[1])
                if "y" in have and "z" not in have:
                    shape = half_shape(have, shape)
                add_into(own, [own if phase == 0 else source, low, high], shape)

    def last(self):
        self.arriving = []
        for k, step in enumerate(STEPS):
            partner = moved(self.at, self.order[0], step)
            for a in range(len(self.grids)):
                self.arriving += self.push(
                    self.source(2, a, partner), [self.direct[a].at[k]], partner
                )

    def result(self, out, starts):
        for copy in self.arriving:
            copy.wait_recv()
        for a, start in enumerate(starts):
            (mine,) = self.source(2, a, self.at)
            total = mine[0, 0].astype(FULL)
            for k in range(3):
                total = total + self.direct[a][k, 0, 0].astype(FULL)
            out[pl.ds(*self.rows), start : start + self.widths[a]] = total


def hbm():
    return pl.BlockSpec(memory_space=pltpu.HBM)


def anywhere():
    return pl.BlockSpec(memory_space=pl.ANY)


def vmem():
    return pl.BlockSpec(memory_space=pltpu.VMEM)


def tail_kernel(grid, unit_behind, vector, out, totals, *rest):
    buffers = rest[:-8]
    whole, other, other_behind, line, near_lines, send, receive, local = rest[-8:]
    at = place()
    core = at["core"]
    sibling = moved(at, "core", 1)
    greet([sibling] + [moved(at, axis, step) for axis in ALL for step in STEPS])
    copies = Copies(send, receive)
    sent = []

    def send_line(phase):
        started = [
            copies.start(line.at[phase], near_lines.at[phase, k], moved(at, ALL[phase], step))
            for k, step in enumerate(STEPS)
        ]
        sent.extend(started)
        return started

    def add_line(phase, started):
        for copy in started:
            copy.wait_recv()
        parts = [line[phase]] + [near_lines[phase, k] for k in range(3)]
        line[phase + 1, 0:88, :] = (parts[0][:88] + parts[1][:88]) + (parts[2][:88] + parts[3][:88])
        line[phase + 1, 88:96, :] = jnp.maximum(
            jnp.maximum(parts[0][88:], parts[1][88:]), jnp.maximum(parts[2][88:], parts[3][88:])
        )

    line[0] = vector[...]
    mine = pl.ds(pl.multiple_of(core * 72, 8), 72)
    theirs = pl.ds(pl.multiple_of((1 - core) * 72, 8), 72)
    arriving = send_line(0)
    behind = copies.start(unit_behind.at[theirs], other_behind, sibling)
    sent.append(behind)
    local = [local, 0]
    scatters = []
    for part in PARTS:
        count = len(buffers) // 3
        k = len(scatters)
        scatters.append(
            Scatter(copies, at, [grid], WIDTHS[:1], part, buffers[k * count : (k + 1) * count], local)
        )
    for s in scatters:
        s.begin(0)
    add_line(0, arriving)
    arriving = send_line(1)
    for s in scatters:
        s.relay(0)
    add_line(1, arriving)
    arriving = send_line(2)
    for phase in (0, 1):
        for s in scatters:
            s.finish(phase)
            if phase == 0:
                s.begin(1)
            else:
                s.last()
        if phase == 0:
            add_line(2, arriving)
            last = copies.start(line.at[3], totals.at[core], sibling)
            sent.append(last)
            totals[core] = line[3]
            for s in scatters:
                s.relay(1)
    for s in scatters:
        s.result(whole, [0])
    swap = copies.start(whole.at[theirs], other, sibling)
    sent.append(swap)
    out[core, :, 0:256] = whole[mine, :]
    out[core, :, 256:UNIT] = unit_behind[mine, :]
    behind.wait_recv()
    out[1 - core, :, 256:UNIT] = other_behind[...]
    swap.wait_recv()
    out[1 - core, :, 0:256] = other[...]
    last.wait_recv()
    for copy in sent + [copy for s in scatters for copy in s.sent]:
        copy.wait_send()


def tail_scatter(grid, unit_behind, vector):
    shapes = []
    for part in PARTS:
        shapes += Scatter.shapes(WIDTHS[:1], part)
    count = 12 + 3 * 15
    return pl.pallas_call(
        tail_kernel,
        out_shape=[
            jax.ShapeDtypeStruct((2, 72, UNIT), FULL),
            jax.ShapeDtypeStruct((2, 96, 128), FULL),
        ],
        in_specs=[anywhere(), vmem(), vmem()],
        out_specs=[vmem()] * 2,
        scratch_shapes=shapes
        + [
            pltpu.VMEM((144, 256), FULL),
            pltpu.VMEM((72, 256), FULL),
            pltpu.VMEM((72, UNIT - 256), FULL),
            pltpu.VMEM((4, 96, 128), FULL),
            pltpu.VMEM((3, 3, 96, 128), FULL),
            pltpu.SemaphoreType.DMA((count,)),
            pltpu.SemaphoreType.DMA((count,)),
            pltpu.SemaphoreType.DMA((12,)),
        ],
        compiler_params=pltpu.CompilerParams(
            collective_id=1, has_side_effects=True, vmem_limit_bytes=24 << 20
        ),
        name="tail_scatter",
    )(grid, unit_behind, vector)


def swap_kernel(mine, theirs, send, receive):
    sibling = moved(place(), "core", 1)
    greet([sibling])
    Copies(send, receive).start(mine, theirs, sibling).wait()


def swap(mine, number):
    return pl.pallas_call(
        swap_kernel,
        out_shape=jax.ShapeDtypeStruct(mine.shape, mine.dtype),
        in_specs=[anywhere()],
        out_specs=anywhere(),
        scratch_shapes=[pltpu.SemaphoreType.DMA((1,)), pltpu.SemaphoreType.DMA((1,))],
        compiler_params=pltpu.CompilerParams(collective_id=number, has_side_effects=True),
        name=f"swap_{number}",
    )(mine)


def picker(which):
    row = lax.broadcasted_iota(jnp.int32, (256, 128), 0)
    lane = lax.broadcasted_iota(jnp.int32, (256, 128), 1)
    return jnp.where((row == lane + HEAD_DIM * which) & (lane < HEAD_DIM), 1.0, 0.0).astype(LOW)


def placer(which):
    row = lax.broadcasted_iota(jnp.int32, (128, 256), 0)
    lane = lax.broadcasted_iota(jnp.int32, (128, 256), 1)
    return jnp.where((lane == row + HEAD_DIM * which) & (row < HEAD_DIM), 1.0, 0.0).astype(LOW)


def dot(left, right):
    return jnp.dot(left, right, preferred_element_type=FULL)


def dot_rows(left, right):
    return lax.dot_general(left, right, (((0,), (0,)), ((), ())), preferred_element_type=FULL)


def dot_cols(left, right):
    return lax.dot_general(left, right, (((1,), (1,)), ((), ())), preferred_element_type=FULL)


def set_ids(ids, r, ids_row, ids_col):
    eye = lax.broadcasted_iota(jnp.int32, (128, 128), 0) == lax.broadcasted_iota(
        jnp.int32, (128, 128), 1
    )
    for k in range(8):
        piece = ids[k : k + 1, :]
        ids_row[r, :, k * 128 : (k + 1) * 128] = piece
        ids_col[r, k * 128 : (k + 1) * 128, :] = jnp.sum(
            jnp.where(eye, piece, 0.0), axis=1, keepdims=True
        )


def forward_kernel(
    pack, n1, cot, ids, bias, go, gu, gd, gq_out, rows_one, cot_rows, ids_other, mixed, qkv, logsum, peak,
    both, unit, gq, proj, ids_row, ids_col, q_s, k_s, v_s, out_s, top_s, send, receive, local,
):
    at = place()
    core, z = at["core"], at["z"]
    sibling = moved(at, "core", 1)
    partners = [moved(at, "z", step) for step in STEPS]
    greet([sibling] + [moved(at, axis, step) for axis in ALL for step in STEPS])
    copies = Copies(send, receive)
    mine = pl.ds(pl.multiple_of(core * 72, 8), 72)
    first = copies.start(pack.at[1 - core], both.at[mine], sibling)
    ids_copy = copies.start(ids, ids_other, sibling)
    n1_copy = copies.start(n1, rows_one.at[pl.ds(256, 256)], sibling)
    cot_copy = copies.start(cot, cot_rows.at[pl.ds(256, 256)], sibling)
    n1_own = pltpu.make_async_copy(n1, rows_one.at[pl.ds(0, 256)], local.at[0])
    cot_own = pltpu.make_async_copy(cot, cot_rows.at[pl.ds(0, 256)], local.at[1])
    n1_own.start()
    cot_own.start()
    both[mine, :] = pack[core]
    first.wait_recv()
    unit[...] = both[...].astype(LOW)
    block = (at["y"] // 2) * 4 + z
    gq[at["y"] % 2, at["x"], :, lanes(block * 256, 256)] = unit[:, 0:256]
    held = []
    for k, grid in enumerate((go, gu, gd)):
        (spot,) = spots(ALL, "", at, WIDTHS[k + 1], (0, 144))
        copy = pltpu.make_async_copy(
            unit.at[:, pl.ds(STARTS[k + 1], WIDTHS[k + 1])],
            grid.at[at["y"] % 2, at["x"], :, spot[3]],
            local.at[2 + k],
        )
        copy.start()
        held.append(copy)
    ahead = [Gather(copies, at, [gq], WIDTHS[:1], part) for part in PARTS]
    behind = [Gather(copies, at, [go, gu, gd], WIDTHS[1:], part) for part in PARTS_BEHIND]
    for g in ahead:
        g.first()
    for phase in (1, 2):
        for g in ahead:
            g.ring(phase)
        for g in ahead:
            g.forward(phase)
    for copy in held:
        copy.wait()
    for g in behind:
        g.first()
    n1_own.wait()
    n1_copy.wait_recv()
    ids_copy.wait_recv()
    set_ids(ids, 0, ids_row, ids_col)
    set_ids(ids_other, 1, ids_row, ids_col)
    for g in ahead:
        g.settle()
    started = []
    for step in STEPS + (0,):
        to = (z + step) % 4
        spot = lanes(to * 512, 512)
        weights = gq[:, :, :, spot].reshape(1152, 512)
        product = (dot(rows_one[...], weights) + bias[:, spot]).astype(LOW)
        if step:
            proj[to] = product
            started.append(copies.start(proj.at[to], qkv.at[z], moved(at, "z", step)))
        else:
            qkv[z] = product
        if step == 1:
            for g in behind:
                g.ring(1)
        if step == 2:
            for g in behind:
                g.forward(1)
    for g in behind:
        g.ring(2)
    gq_copy = pltpu.make_async_copy(gq, gq_out, local.at[5])
    gq_copy.start()
    for copy in started:
        copy.wait_recv()
    for r in range(2):
        for j in range(2):
            for b in range(4):
                block = qkv[b, r * 256 : (r + 1) * 256, j * 256 : (j + 1) * 256]
                spot = slice(b * 256, (b + 1) * 256)
                q_s[2 * r + j, spot, :] = dot(block, picker(0)).astype(LOW)
                k_s[2 * r + j, spot, :] = dot(block, picker(1)).astype(LOW)
                v_s[2 * r + j, spot, :] = dot(block, picker(2)).astype(LOW)
    top_s[...] = jnp.full(top_s.shape, LOWEST, FULL)
    back = []
    for step in STEPS + (0,):
        b = (z + step) % 4
        rows = pl.ds(pl.multiple_of(b * 256, 256), 256)

        @pl.loop(0, 4)
        def _(n, b=b, rows=rows):
            r, j = n // 2, n % 2
            scores = dot_cols(q_s[n, rows, :], k_s[n]) * SCALE
            query_ids = ids_col[r, rows, :]
            scores = jnp.where(query_ids == ids_row[r], scores, LOWEST)
            top = jnp.max(scores, axis=1, keepdims=True)
            expo = jnp.exp(scores - top)
            total = jnp.sum(expo, axis=1, keepdims=True)
            weights = (expo * (1.0 / total)).astype(LOW)
            out_s[n, b] = dot(weights, v_s[n]).astype(LOW)
            logsum[n, rows, :] = top + jnp.log(total)
            top_s[n] = jnp.maximum(top_s[n], jnp.where(query_ids >= 0.0, top, LOWEST))

        for n in range(4):
            r, j = n // 2, n % 2
            source = out_s.at[n, b]
            spot = (pl.ds(r * 256, 256), lanes(z * 256 + j * 128, 128))
            if step:
                back.append(copies.start(source, mixed.at[spot], moved(at, "z", step)))
            else:
                copy = pltpu.make_async_copy(source, mixed.at[spot], local.at[6 + n])
                copy.start()
                back.append(copy)
        if step == 2:
            for g in behind:
                g.forward(2)
    row = lax.broadcasted_iota(jnp.int32, (8, 128), 0)
    high = [jnp.maximum(jnp.max(top_s[j]), jnp.max(top_s[2 + j])) for j in range(2)]
    peak[...] = jnp.where(row == 0, high[0], high[1])
    for copy in back[:12]:
        copy.wait_recv()
    for copy in back[12:]:
        copy.wait()
    cot_own.wait()
    cot_copy.wait_recv()
    gq_copy.wait()
    for g in behind:
        g.settle()
    sent = [first, ids_copy, n1_copy, cot_copy] + started + back[:12]
    for copy in sent + [copy for g in ahead + behind for copy in g.sent]:
        copy.wait_send()


def forward(pack, n1, cot, ids, bias):
    count = 4 + 3 + 12 + 4 * 45
    return pl.pallas_call(
        forward_kernel,
        out_shape=[
            jax.ShapeDtypeStruct((2, 4, 144, 1024), LOW),
            jax.ShapeDtypeStruct((2, 4, 144, HIDDEN), LOW),
            jax.ShapeDtypeStruct((2, 4, 144, HIDDEN), LOW),
            jax.ShapeDtypeStruct((2, 4, 144, 2048), LOW),
            jax.ShapeDtypeStruct((512, 1152), LOW),
            jax.ShapeDtypeStruct((512, 1152), LOW),
            jax.ShapeDtypeStruct((8, 128), FULL),
            jax.ShapeDtypeStruct((512, 1024), LOW),
            jax.ShapeDtypeStruct((4, 512, 512), LOW),
            jax.ShapeDtypeStruct((4, 1024, 1), FULL),
            jax.ShapeDtypeStruct((8, 128), FULL),
        ],
        in_specs=[vmem(), anywhere(), anywhere(), vmem(), vmem()],
        out_specs=[hbm()] * 4
        + [vmem(), hbm(), vmem(), anywhere(), vmem(), vmem(), vmem()],
        scratch_shapes=[
            pltpu.VMEM((144, UNIT), FULL),
            pltpu.VMEM((144, UNIT), LOW),
            pltpu.VMEM((2, 4, 144, 2048), LOW),
            pltpu.VMEM((4, 512, 512), LOW),
            pltpu.VMEM((2, 1, 1024), FULL),
            pltpu.VMEM((2, 1024, 1), FULL),
        ]
        + [pltpu.VMEM((4, 1024, 128), LOW)] * 3
        + [
            pltpu.VMEM((4, 4, 256, 128), LOW),
            pltpu.VMEM((4, 256, 1), FULL),
            pltpu.SemaphoreType.DMA((count,)),
            pltpu.SemaphoreType.DMA((count,)),
            pltpu.SemaphoreType.DMA((10,)),
        ],
        compiler_params=pltpu.CompilerParams(
            collective_id=0, has_side_effects=True, vmem_limit_bytes=48 << 20
        ),
        name="forward_attention",
    )(pack, n1, cot, ids, bias)


def backward_kernel(
    upstream, qkv, ids, ids_other, logsum, go, gu, gd, back, unit, *rest
):
    (
        grad, q_s, k_s, v_s, g_s, dq_s, dk_s, dv_s, out_s, ids_row, ids_col, send, receive, local,
    ) = rest[:14]
    buffers = rest[14:]
    at = place()
    z = at["z"]
    partners = [moved(at, "z", step) for step in STEPS]
    greet([moved(at, axis, step) for axis in ALL for step in STEPS])
    copies = Copies(send, receive)
    started = [
        copies.start(upstream.at[:, lanes(partner["z"] * 256, 256)], grad.at[z], partner)
        for partner in partners
    ]
    own = pltpu.make_async_copy(upstream.at[:, lanes(z * 256, 256)], grad.at[z], local.at[0])
    own.start()
    counter = [local, 3]
    scatters = []
    for k, part in enumerate(PARTS_BEHIND):
        count = len(buffers) // 3
        scatters.append(
            Scatter(
                copies, at, [go, gu, gd], WIDTHS[1:], part, buffers[k * count : (k + 1) * count], counter
            )
        )
    for s in scatters:
        s.begin(0)
    set_ids(ids, 0, ids_row, ids_col)
    set_ids(ids_other, 1, ids_row, ids_col)
    for r in range(2):
        for j in range(2):
            for b in range(4):
                block = qkv[b, r * 256 : (r + 1) * 256, j * 256 : (j + 1) * 256]
                spot = slice(b * 256, (b + 1) * 256)
                q_s[2 * r + j, spot, :] = dot(block, picker(0)).astype(LOW)
                k_s[2 * r + j, spot, :] = dot(block, picker(1)).astype(LOW)
                v_s[2 * r + j, spot, :] = dot(block, picker(2)).astype(LOW)
    own.wait()
    for copy in started:
        copy.wait_recv()
    lane = lax.broadcasted_iota(jnp.int32, (256, 128), 1)
    for r in range(2):
        for j in range(2):
            for b in range(4):
                block = grad[b, r * 256 : (r + 1) * 256, j * 128 : (j + 1) * 128]
                g_s[2 * r + j, b * 256 : (b + 1) * 256, :] = jnp.where(
                    lane < HEAD_DIM, block.astype(FULL), 0.0
                ).astype(LOW)
    sent = []
    for r in range(2):
        for j in range(2):
            n = 2 * r + j
            dk_s[...] = jnp.zeros(dk_s.shape, FULL)
            dv_s[...] = jnp.zeros(dv_s.shape, FULL)

            @pl.loop(0, 4)
            def _(b, n=n, r=r):
                rows = pl.ds(pl.multiple_of(b * 256, 256), 256)
                query, upper = q_s[n, rows, :], g_s[n, rows, :]
                scores = dot_cols(query, k_s[n]) * SCALE
                allowed = ids_col[r, rows, :] == ids_row[r]
                probs = jnp.where(allowed, jnp.exp(scores - logsum[n, rows, :]), 0.0)
                dv_s[...] += dot_rows(probs.astype(LOW), upper)
                prob_grad = dot_cols(upper, v_s[n])
                centre = jnp.sum(probs * prob_grad, axis=1, keepdims=True)
                score_grad = (probs * (prob_grad - centre)).astype(LOW)
                dq_s[rows, :] = (dot(score_grad, k_s[n]) * SCALE).astype(LOW)
                dk_s[...] += dot_rows(score_grad, query)

            for b in range(4):
                spot = slice(b * 256, (b + 1) * 256)
                out_s[b, r * 256 : (r + 1) * 256, j * 256 : (j + 1) * 256] = (
                    dot(dq_s[spot, :], placer(0))
                    + dot((dk_s[spot, :] * SCALE).astype(LOW), placer(1))
                    + dot(dv_s[spot, :].astype(LOW), placer(2))
                ).astype(LOW)
            if n == 0:
                for s in scatters:
                    s.relay(0)
        rows = pl.ds(r * 256, 256)
        for partner in partners:
            source = out_s.at[partner["z"], rows]
            sent.append(copies.start(source, back.at[rows, lanes(z * 512, 512)], partner))
        copy = pltpu.make_async_copy(
            out_s.at[z, rows], back.at[rows, lanes(z * 512, 512)], local.at[1 + r]
        )
        copy.start()
        sent.append(copy)
    for s in scatters:
        s.finish(0)
        s.begin(1)
    for s in scatters:
        s.relay(1)
    for s in scatters:
        s.finish(1)
        s.last()
    for s in scatters:
        s.result(unit, [start - 256 for start in STARTS[1:]])
    for copy in sent:
        copy.wait()
    for copy in started + [copy for s in scatters for copy in s.sent]:
        copy.wait_send()


def backward(upstream, qkv, ids, ids_other, logsum, grids):
    count = 3 + 6 + 3 * 45
    shapes = []
    for part in PARTS_BEHIND:
        shapes += Scatter.shapes(WIDTHS[1:], part)
    return pl.pallas_call(
        backward_kernel,
        out_shape=[
            jax.ShapeDtypeStruct((512, 2048), LOW),
            jax.ShapeDtypeStruct((144, UNIT - 256), FULL),
        ],
        in_specs=[anywhere(), vmem(), vmem(), vmem(), vmem()] + [anywhere()] * 3,
        out_specs=[anywhere(), vmem()],
        scratch_shapes=[pltpu.VMEM((4, 512, 256), LOW)]
        + [pltpu.VMEM((4, 1024, 128), LOW)] * 4
        + [
            pltpu.VMEM((1024, 128), LOW),
            pltpu.VMEM((1024, 128), FULL),
            pltpu.VMEM((1024, 128), FULL),
            pltpu.VMEM((4, 512, 512), LOW),
            pltpu.VMEM((2, 1, 1024), FULL),
            pltpu.VMEM((2, 1024, 1), FULL),
            pltpu.SemaphoreType.DMA((count,)),
            pltpu.SemaphoreType.DMA((count,)),
            pltpu.SemaphoreType.DMA((48,)),
        ]
        + shapes,
        compiler_params=pltpu.CompilerParams(
            collective_id=3, has_side_effects=True, vmem_limit_bytes=52 << 20
        ),
        name="backward_attention",
    )(upstream, qkv, ids, ids_other, logsum, *grids)


def normalize(values, gain, shift):
    centre = values - jnp.mean(values, axis=-1, keepdims=True)
    inverse = lax.rsqrt(jnp.mean(centre * centre, axis=-1, keepdims=True) + EPSILON)
    scaled = centre * inverse
    return (scaled * gain + shift, scaled, inverse)


def normalize_back(upstream, scaled, inverse, gain):
    along = upstream * gain
    width_mean = jnp.mean(along, axis=-1, keepdims=True)
    cross_mean = jnp.mean(along * scaled, axis=-1, keepdims=True)
    return inverse * (along - width_mean - scaled * cross_mean)


def smooth(inner):
    return jax.nn.gelu(inner, approximate=True)


def selector(offset):
    matrix = np.zeros((1024, 128), np.float32)
    for t in range(8):
        for i in range(TAIL):
            matrix[128 * t + offset + i, TAIL * t + i] = 1.0
    return jnp.asarray(matrix, LOW)


def per_device(
    tokens,
    picture,
    cotangent,
    gain_one,
    shift_one,
    query_weight,
    query_bias,
    key_weight,
    value_weight,
    value_bias,
    out_weight,
    out_bias,
    gain_two,
    shift_two,
    up_weight,
    up_bias,
    down_weight,
    down_bias,
):
    width = tokens.shape[1]
    t = lax.axis_index("tensor")
    core = lax.axis_index("dp") % 2
    z = t % 4
    gain_first = gain_one.astype(FULL)
    gain_second = gain_two.astype(FULL)

    out_t = out_weight.astype(FULL).T
    down_t = down_weight.astype(FULL).T
    up = up_weight.astype(FULL)
    halves = []
    for h in range(2):
        cols = slice(h * 72, (h + 1) * 72)
        first = h * (MAIN + TAIL)
        main, tail = slice(first, first + MAIN), slice(first + MAIN, first + MAIN + TAIL)
        halves.append(
            jnp.concatenate(
                [
                    query_weight[:, cols].astype(FULL),
                    key_weight[:, cols].astype(FULL),
                    value_weight[:, cols].astype(FULL),
                    jnp.zeros((72, 40), FULL),
                    out_t[:, cols],
                    up[:, tail],
                    down_t[:, tail],
                    jnp.zeros((72, 30), FULL),
                    up[:, main],
                    down_t[:, main],
                ],
                axis=1,
            )
        )
    pack = jnp.stack(halves)

    inputs = tokens.astype(FULL)
    normed, scaled_one, inverse_one = normalize(inputs, gain_first, shift_one.astype(FULL))
    normed_mine = normed.astype(LOW)
    half = lax.dynamic_slice_in_dim(picture, (t // 4) * 1024, 1024)
    ids = jnp.where(half >= 0, half, -1 - jnp.arange(1024, dtype=jnp.int32)).astype(FULL)
    def halves_of(vector, size):
        return lax.dynamic_index_in_dim(
            vector.astype(FULL).reshape(8, 2, size), core, axis=1, keepdims=False
        )

    query_b, value_b = halves_of(query_bias, 72), halves_of(value_bias, 72)
    proj_bias = jnp.concatenate(
        [query_b, jnp.zeros((8, 72), FULL), value_b, jnp.zeros((8, 40), FULL)], axis=1
    ).reshape(1, 2048)
    up_b = halves_of(up_bias, MAIN + TAIL)
    hidden_bias = jnp.concatenate(
        [up_b[:, :MAIN].reshape(2048), up_b[:, MAIN:].reshape(8 * TAIL), jnp.zeros((24,), FULL)]
    )

    go, gu, gd, gq, rows_one, cot_rows, ids_other, mixed, qkv, logsum, peak = forward(
        pack, normed_mine, cotangent, ids.reshape(8, 128), proj_bias
    )
    gq, go = gq.reshape(width, 2048), go.reshape(width, 1024)
    select_up, select_down = selector(72), selector(72 + TAIL)
    gu = lax.dynamic_update_slice(
        gu.reshape(width, HIDDEN), dot(go, select_up).astype(LOW), (0, 2048)
    )
    gd = lax.dynamic_update_slice(
        gd.reshape(width, HIDDEN), dot(go, select_down).astype(LOW), (0, 2048)
    )
    part = dot_cols(mixed, go)
    branch = part[:256] + swap(part[256:].astype(LOW), 4).astype(FULL) + out_bias.astype(FULL)
    middle = inputs + branch
    normed_two, scaled_two, inverse_two = normalize(middle, gain_second, shift_two.astype(FULL))
    normed_two = normed_two.astype(LOW)
    rows_two = jnp.concatenate([normed_two, swap(normed_two, 5)])
    hidden = dot(rows_two, gu) + hidden_bias
    active = smooth(hidden).astype(LOW)
    part = dot_cols(active, gd)
    result = middle + (
        part[:256] + swap(part[256:].astype(LOW), 6).astype(FULL) + down_bias.astype(FULL)
    )

    upstream = cotangent.astype(FULL)
    active_grad = dot(cot_rows, gd)
    _, gelu_back = jax.vjp(smooth, hidden)
    hidden_grad = gelu_back(active_grad)[0].astype(LOW)
    part = dot_cols(hidden_grad, gu)
    normed_two_grad = part[:256] + swap(part[256:].astype(LOW), 7).astype(FULL)
    middle_grad = upstream + normalize_back(normed_two_grad, scaled_two, inverse_two, gain_second)
    branch_low = middle_grad.astype(LOW)
    branch_rows = jnp.concatenate([branch_low, swap(branch_low, 8)])
    mixed_grad = dot(branch_rows, go).astype(LOW)

    shape = (2, 4, 144)
    grad_u = dot_rows(rows_two, hidden_grad[:, :2048]).astype(LOW)
    grad_d = dot_rows(cot_rows, active[:, :2048]).astype(LOW)
    up_tail = dot_cols(hidden_grad[:, 2048:], select_up).astype(LOW)
    down_tail = dot_cols(active[:, 2048:], select_down).astype(LOW)
    grad_o = dot_rows(
        jnp.concatenate([branch_rows, rows_two, cot_rows]),
        jnp.concatenate([mixed, up_tail, down_tail]),
    ).astype(LOW)
    proj_grad, unit_behind = backward(
        mixed_grad,
        qkv,
        ids.reshape(8, 128),
        ids_other,
        logsum,
        [
            grad_o.reshape(shape + (1024,)),
            grad_u.reshape(shape + (2048,)),
            grad_d.reshape(shape + (2048,)),
        ],
    )
    part = dot_cols(proj_grad, gq)
    normed_one_grad = part[:256] + swap(part[256:].astype(LOW), 9).astype(FULL)
    input_grad = middle_grad + normalize_back(normed_one_grad, scaled_one, inverse_one, gain_first)

    grad_q = dot_rows(rows_one, proj_grad).astype(LOW)

    head = lax.broadcasted_iota(jnp.int32, (8, 128), 1)
    peaks = jnp.where(
        head == 4 * z + core,
        peak[0, 0],
        jnp.where(head == 4 * z + 2 + core, peak[1, 0], LOWEST),
    )

    def total(values):
        return jnp.sum(values.astype(FULL), axis=0)

    vector = jnp.concatenate(
        [
            total(proj_grad),
            total(hidden_grad),
            total(branch_low),
            total(upstream),
            total(normed_one_grad * scaled_one),
            total(normed_one_grad),
            total(normed_two_grad * scaled_two),
            total(normed_two_grad),
            jnp.zeros((128,), FULL),
        ]
    ).reshape(88, 128)
    vector = jnp.concatenate([vector, peaks])
    grads, totals = tail_scatter(grad_q.reshape(shape + (2048,)), unit_behind, vector)

    def side(first, size):
        return jnp.concatenate([grads[0, :, first : first + size], grads[1, :, first : first + size]], axis=1)

    def hidden_side(main, tail):
        return jnp.concatenate(
            [
                grads[0, :, main : main + MAIN],
                grads[0, :, tail : tail + TAIL],
                grads[1, :, main : main + MAIN],
                grads[1, :, tail : tail + TAIL],
            ],
            axis=1,
        )

    query_w, key_w, value_w = side(0, 72), side(72, 72), side(144, 72)
    out_w = side(256, 72).T
    up_w = hidden_side(384, 256 + 72)
    down_w = hidden_side(640, 256 + 72 + TAIL).T
    flat = totals[:, :88].reshape(2, 88 * 128)
    heads = flat[:, :2048].reshape(2, 8, 256)
    query_b_grad = heads[:, :, :72].transpose(1, 0, 2).reshape(width)
    value_b_grad = heads[:, :, 144:216].transpose(1, 0, 2).reshape(width)
    up_b_grad = (
        jnp.concatenate(
            [
                flat[:, 2048:4096].reshape(2, 8, MAIN),
                flat[:, 4096 : 4096 + 8 * TAIL].reshape(2, 8, TAIL),
            ],
            axis=2,
        )
        .transpose(1, 0, 2)
        .reshape(-1)
    )
    summed = (flat[0] + flat[1])[2048 + HIDDEN : 2048 + HIDDEN + 6 * width].reshape(6, width)
    high = jnp.maximum(totals[0, 88, :16], totals[1, 88, :16])
    factor = jnp.sqrt(CLIP_LIMIT / jnp.maximum(high, CLIP_LIMIT))
    column_factor = jnp.repeat(lax.dynamic_slice_in_dim(factor, 2 * t, 2), HEAD_DIM)
    clipped_query = query_weight.astype(FULL) * column_factor[None, :]
    clipped_key = key_weight.astype(FULL) * column_factor[None, :]
    return (
        result,
        input_grad,
        query_w,
        key_w,
        value_w,
        out_w,
        up_w,
        down_w,
        query_b_grad,
        value_b_grad,
        up_b_grad,
        summed[0],
        summed[1],
        summed[2],
        summed[3],
        summed[4],
        summed[5],
        clipped_query,
        clipped_key,
    )


def solution(mesh):
    in_specs = (
        P(("dp", "tensor"), None),
        P("dp"),
        P(("dp", "tensor"), None),
        P(),
        P(),
        P("dp", "tensor"),
        P(),
        P("dp", "tensor"),
        P("dp", "tensor"),
        P(),
        P("tensor", "dp"),
        P(),
        P(),
        P(),
        P("dp", "tensor"),
        P(),
        P("tensor", "dp"),
        P(),
    )
    out_specs = (
        P(("dp", "tensor"), None),
        P(("dp", "tensor"), None),
        P("dp", "tensor"),
        P("dp", "tensor"),
        P("dp", "tensor"),
        P("tensor", "dp"),
        P("dp", "tensor"),
        P("tensor", "dp"),
        P(),
        P(),
        P(),
        P(),
        P(),
        P(),
        P(),
        P(),
        P(),
        P("dp", "tensor"),
        P("dp", "tensor"),
    )
    return jax.shard_map(
        per_device, mesh=mesh, in_specs=in_specs, out_specs=out_specs, check_vma=False
    )
```

```python
import functools

import jax
import jax.numpy as jnp
import numpy as np
from jax import lax
from jax.experimental import pallas as pl
from jax.experimental.pallas import tpu as pltpu
from jax.sharding import PartitionSpec as P

HEAD_DIM = 72
EPSILON = 1e-06
CLIP_LIMIT = 2.0
LOWEST = -1e30
SCALE = HEAD_DIM**-0.5

MESH = pl.DeviceIdType.MESH
LOW = jnp.bfloat16
FULL = jnp.float32

WIDTHS = (256, 128, 256, 256)
STARTS = (0, 256, 384, 640)
UNIT = 896
MAIN = 256
TAIL = 13
HIDDEN = 8 * MAIN + 128
PARTS = ((0, 48, "zyx"), (48, 48, "xzy"), (96, 48, "yxz"))
PARTS_BEHIND = ((0, 64, "zyx"), (64, 64, "zxy"), (128, 16, "yxz"))
STEPS = (1, 3, 2)
ALL = "xyz"


def place():
    d, t = lax.axis_index("dp"), lax.axis_index("tensor")
    return {"x": (d // 2) % 4, "y": (t // 4) * 2 + d // 8, "z": t % 4, "core": d % 2}


def device(at):
    return ((at["y"] % 2) * 8 + at["x"] * 2 + at["core"], (at["y"] // 2) * 4 + at["z"])


def moved(at, axis, step):
    other = dict(at)
    other[axis] = 1 - at["core"] if axis == "core" else (at[axis] + step) % 4
    return other


def greet(partners):
    barrier = pltpu.get_barrier_semaphore()
    for partner in partners:
        pl.semaphore_signal(barrier, inc=1, device_id=device(partner), device_id_type=MESH)
    pl.semaphore_wait(barrier, len(partners))


class Copies:
    def __init__(self, send, receive):
        self.send, self.receive, self.used = send, receive, 0

    def start(self, source, target, partner):
        copy = pltpu.make_async_remote_copy(
            src_ref=source,
            dst_ref=target,
            send_sem=self.send.at[self.used],
            recv_sem=self.receive.at[self.used],
            device_id=device(partner),
            device_id_type=MESH,
        )
        self.used += 1
        copy.start()
        return copy


def lanes(first, size):
    return pl.ds(first if isinstance(first, int) else pl.multiple_of(first, 128), size)


def spots(held, have, at, width, rows, half=None):
    zs, ys = (4 if "z" in held else 1), at["y"] if "y" in held else 0
    x_at = pl.ds(0, 4) if "x" in have else pl.ds(at["x"] if "x" in held else 0, 1)
    y_at = pl.ds(0, 2) if "y" in have else pl.ds(ys % 2, 1)
    z = at["z"] if "z" in held else 0
    if "y" in have and "z" in have:
        ranges = [(0, 8 * width)]
    elif "y" in have:
        ranges = [((h * zs + z) * width, width) for h in (0, 1)]
    elif "z" in have:
        ranges = [((ys // 2) * zs * width, 4 * width)]
    else:
        ranges = [(((ys // 2) * zs + z) * width, width)]
    if half is not None:
        if len(ranges) == 2:
            ranges = [ranges[half]]
        elif "x" in have:
            x_at = pl.ds(2 * half, 2)
        elif "y" in have:
            y_at = pl.ds(half, 1)
        else:
            ((first, size),) = ranges
            ranges = [(first + half * (size // 2), size // 2)]
    return [(y_at, x_at, pl.ds(*rows), lanes(*r)) for r in ranges]


def rect_shape(have, width, rows):
    ys, xs, zs = 2 if "y" in have else 1, 4 if "x" in have else 1, 4 if "z" in have else 1
    return (ys, xs, rows, ys * zs * width)


class Gather:
    def __init__(self, copies, at, grids, widths, part):
        self.copies, self.at, self.grids, self.widths = copies, at, grids, widths
        self.rows, self.order = part[:2], part[2]
        self.arriving, self.sent = [], []

    def views(self, grid, width, have, at, half=None):
        return [grid.at[spot] for spot in spots(ALL, have, at, width, self.rows, half)]

    def send(self, have, owner, partner, half=None):
        started = []
        for grid, width in zip(self.grids, self.widths):
            for view in self.views(grid, width, have, owner, half):
                started.append(self.copies.start(view, view, partner))
        self.sent += started
        return started

    def settle(self):
        for copy in self.arriving:
            copy.wait_recv()
        self.arriving = []

    def first(self):
        for step in STEPS:
            self.arriving += self.send("", self.at, moved(self.at, self.order[0], step))

    def ring(self, phase):
        self.settle()
        axis, have = self.order[phase], self.order[:phase]
        self.after = self.send(have, self.at, moved(self.at, axis, 1))
        self.before = self.send(have, self.at, moved(self.at, axis, 3))

    def forward(self, phase):
        axis, have = self.order[phase], self.order[:phase]
        up, down = moved(self.at, axis, 1), moved(self.at, axis, 3)
        for copy in self.after:
            copy.wait_recv()
        self.arriving += self.send(have, down, up, 0)
        for copy in self.before:
            copy.wait_recv()
        self.arriving += self.send(have, up, down, 1)


def add_into(target, terms, shape):
    @pl.loop(0, shape[0] * shape[1] * (shape[2] // 16))
    def _(n):
        block = n // (shape[2] // 16)
        spot = (
            block // shape[1],
            block % shape[1],
            pl.ds(pl.multiple_of((n % (shape[2] // 16)) * 16, 16), 16),
            slice(None),
        )
        total = terms[0][spot].astype(FULL)
        for term in terms[1:]:
            total = total + term[spot].astype(FULL)
        target[spot] = total.astype(target.dtype)


def half_shape(have, shape):
    ys, xs, rows, cols = shape
    if "y" in have and "z" not in have:
        return (ys, xs, rows, cols // 2)
    if "x" in have:
        return (ys, 2, rows, cols)
    if "y" in have:
        return (1, xs, rows, cols)
    return (ys, xs, rows, cols // 2)


class Scatter:
    @staticmethod
    def shapes(widths, part, loaded):
        _, rows, order = part
        shapes = []
        for have, count in ((order[:2], 5 if loaded else 4), (order[:1], 4)):
            for _ in range(count):
                shapes += [pltpu.VMEM(rect_shape(have, w, rows), LOW) for w in widths]
        shapes += [pltpu.VMEM((3, 1, 1, rows, w), LOW) for w in widths]
        return shapes

    def __init__(self, copies, at, grids, widths, part, buffers, local=None):
        self.copies, self.at, self.grids, self.widths = copies, at, grids, widths
        self.rows, self.order = part[:2], part[2]
        self.local = local
        self.sent = []

        def take():
            taken, buffers[:] = buffers[: len(widths)], buffers[len(widths) :]
            return taken

        self.near, self.low, self.high, self.own = [], [], [], []
        for phase in (0, 1):
            for group in (self.near, self.low, self.high, self.own):
                group.append(take())
            if phase == 0 and local:
                self.mix = [take()]
        self.direct = take()

    def source(self, phase, a, at, half=None):
        have = self.order[: 2 - phase]
        if phase == 0:
            found = spots(ALL, have, at, self.widths[a], self.rows, half)
            return [self.grids[a].at[spot] for spot in found]
        held = self.order[: 3 - phase]
        found = spots(held, have, at, self.widths[a], (0, self.rows[1]), half)
        return [self.own[phase - 1][a].at[spot] for spot in found]

    def target(self, phase, buffer, a, half=None):
        have = self.order[: 2 - phase]
        found = spots(have, have, self.at, self.widths[a], (0, self.rows[1]), half)
        return [buffer[phase][a].at[spot] for spot in found]

    def push(self, sources, targets, partner):
        started = [self.copies.start(s, t, partner) for s, t in zip(sources, targets)]
        self.sent += started
        return started

    def begin(self, phase):
        axis = self.order[2 - phase]
        up, down, far = (moved(self.at, axis, step) for step in STEPS)
        self.arriving, self.loading = [], []
        for a in range(len(self.grids)):
            for half, partner in ((0, up), (1, down)):
                self.arriving += self.push(
                    self.source(phase, a, far, half),
                    self.target(phase, self.near, a, half),
                    partner,
                )
        if phase == 0 and self.local:
            for a in range(len(self.grids)):
                pairs = list(
                    zip(
                        self.source(0, a, up, 0) + self.source(0, a, down, 1),
                        self.target(0, self.mix, a, 0) + self.target(0, self.mix, a, 1),
                    )
                )
                pairs += list(zip(self.source(0, a, self.at), self.target(0, self.own, a)))
                for view, target in pairs:
                    copy = pltpu.make_async_copy(view, target, self.local[0].at[self.local[1]])
                    self.local[1] += 1
                    copy.start()
                    self.loading.append(copy)

    def relay(self, phase):
        axis = self.order[2 - phase]
        have = self.order[: 2 - phase]
        up, down, _ = (moved(self.at, axis, step) for step in STEPS)
        for copy in self.loading:
            copy.wait()
        for copy in self.arriving:
            copy.wait_recv()
        self.arriving = []
        for a in range(len(self.grids)):
            shape = half_shape(have, rect_shape(have, self.widths[a], self.rows[1]))
            for half, partner in ((0, up), (1, down)):
                (near,) = self.target(phase, self.near, a, half)
                if phase == 0 and self.local:
                    (view,) = self.target(phase, self.mix, a, half)
                else:
                    (view,) = self.source(phase, a, partner, half)
                add_into(near, [view, near], shape)
                buffer = self.low if half == 0 else self.high
                self.arriving += self.push(
                    [near] + self.source(phase, a, partner, 1 - half),
                    self.target(phase, buffer, a, half) + self.target(phase, buffer, a, 1 - half),
                    partner,
                )

    def finish(self, phase):
        have = self.order[: 2 - phase]
        for copy in self.arriving:
            copy.wait_recv()
        for a in range(len(self.grids)):
            for low, high, own, source in zip(
                self.target(phase, self.low, a),
                self.target(phase, self.high, a),
                self.target(phase, self.own, a),
                self.source(phase, a, self.at),
            ):
                shape = rect_shape(have, self.widths[a], self.rows[1])
                if "y" in have and "z" not in have:
                    shape = half_shape(have, shape)
                add_into(own, [own if phase == 0 and self.local else source, low, high], shape)

    def last(self):
        self.arriving = []
        for k, step in enumerate(STEPS):
            partner = moved(self.at, self.order[0], step)
            for a in range(len(self.grids)):
                self.arriving += self.push(
                    self.source(2, a, partner), [self.direct[a].at[k]], partner
                )

    def result(self, out, starts):
        for copy in self.arriving:
            copy.wait_recv()
        for a, start in enumerate(starts):
            (mine,) = self.source(2, a, self.at)
            total = mine[0, 0].astype(FULL)
            for k in range(3):
                total = total + self.direct[a][k, 0, 0].astype(FULL)
            out[pl.ds(*self.rows), start : start + self.widths[a]] = total


def hbm():
    return pl.BlockSpec(memory_space=pltpu.HBM)


def anywhere():
    return pl.BlockSpec(memory_space=pl.ANY)


def vmem():
    return pl.BlockSpec(memory_space=pltpu.VMEM)


def picker(which):
    row = lax.broadcasted_iota(jnp.int32, (256, 128), 0)
    lane = lax.broadcasted_iota(jnp.int32, (256, 128), 1)
    return jnp.where((row == lane + HEAD_DIM * which) & (lane < HEAD_DIM), 1.0, 0.0).astype(LOW)


def placer(which):
    row = lax.broadcasted_iota(jnp.int32, (128, 256), 0)
    lane = lax.broadcasted_iota(jnp.int32, (128, 256), 1)
    return jnp.where((lane == row + HEAD_DIM * which) & (row < HEAD_DIM), 1.0, 0.0).astype(LOW)


def dot(left, right):
    return jnp.dot(left, right, preferred_element_type=FULL)


def dot_rows(left, right):
    return lax.dot_general(left, right, (((0,), (0,)), ((), ())), preferred_element_type=FULL)


def dot_cols(left, right):
    return lax.dot_general(left, right, (((1,), (1,)), ((), ())), preferred_element_type=FULL)


def set_ids(ids, r, ids_row, ids_col):
    eye = lax.broadcasted_iota(jnp.int32, (128, 128), 0) == lax.broadcasted_iota(
        jnp.int32, (128, 128), 1
    )
    for k in range(8):
        piece = ids[k : k + 1, :]
        ids_row[r, :, k * 128 : (k + 1) * 128] = piece
        ids_col[r, k * 128 : (k + 1) * 128, :] = jnp.sum(
            jnp.where(eye, piece, 0.0), axis=1, keepdims=True
        )


def forward_kernel(
    pack, n1, cot, ids, bias, go, gu, gd, gq_out, n1t, cot_rows, ids_other, mixed, q_s, k_s, v_s, logsum, peak,
    both, unit, gq, proj, rows_one, qkv, ids_row, ids_col, out_s, top_s, send, receive, local,
):
    at = place()
    core, z = at["core"], at["z"]
    sibling = moved(at, "core", 1)
    partners = [moved(at, "z", step) for step in STEPS]
    greet([sibling] + [moved(at, axis, step) for axis in ALL for step in STEPS])
    copies = Copies(send, receive)
    mine = pl.ds(pl.multiple_of(core * 72, 8), 72)
    first = copies.start(pack.at[1 - core], both.at[mine], sibling)
    ids_copy = copies.start(ids, ids_other, sibling)
    n1_copy = copies.start(n1, rows_one.at[pl.ds(256, 256)], sibling)
    cot_copy = copies.start(cot, cot_rows.at[pl.ds(256, 256)], sibling)
    n1_own = pltpu.make_async_copy(n1, rows_one.at[pl.ds(0, 256)], local.at[0])
    cot_own = pltpu.make_async_copy(cot, cot_rows.at[pl.ds(0, 256)], local.at[1])
    n1_own.start()
    cot_own.start()
    both[mine, :] = pack[core]
    first.wait_recv()
    unit[...] = both[...].astype(LOW)
    block = (at["y"] // 2) * 4 + z
    gq[at["y"] % 2, at["x"], :, lanes(block * 256, 256)] = unit[:, 0:256]
    held = []
    for k, grid in enumerate((go, gu, gd)):
        (spot,) = spots(ALL, "", at, WIDTHS[k + 1], (0, 144))
        copy = pltpu.make_async_copy(
            unit.at[:, pl.ds(STARTS[k + 1], WIDTHS[k + 1])],
            grid.at[at["y"] % 2, at["x"], :, spot[3]],
            local.at[2 + k],
        )
        copy.start()
        held.append(copy)
    ahead = [Gather(copies, at, [gq], WIDTHS[:1], part) for part in PARTS]
    behind = [Gather(copies, at, [go, gu, gd], WIDTHS[1:], part) for part in PARTS_BEHIND]
    for g in ahead:
        g.first()
    for phase in (1, 2):
        for g in ahead:
            g.ring(phase)
        for g in ahead:
            g.forward(phase)
    for copy in held:
        copy.wait()
    for g in behind:
        g.first()
    n1_own.wait()
    n1_copy.wait_recv()
    ids_copy.wait_recv()
    set_ids(ids, 0, ids_row, ids_col)
    set_ids(ids_other, 1, ids_row, ids_col)
    for g in ahead:
        g.settle()
    started = []
    for step in STEPS + (0,):
        to = (z + step) % 4
        spot = lanes(to * 512, 512)
        weights = gq[:, :, :, spot].reshape(1152, 512)
        product = (dot(rows_one[...], weights) + bias[:, spot]).astype(LOW)
        if step:
            proj[to] = product
            started.append(copies.start(proj.at[to], qkv.at[z], moved(at, "z", step)))
        else:
            qkv[z] = product
        if step == 1:
            for g in behind:
                g.ring(1)
        if step == 2:
            for g in behind:
                g.forward(1)
    for g in behind:
        g.ring(2)
    n1t[...] = rows_one[...].T
    gq_copy = pltpu.make_async_copy(gq, gq_out, local.at[5])
    gq_copy.start()
    for copy in started:
        copy.wait_recv()
    for r in range(2):
        for j in range(2):
            for b in range(4):
                block = qkv[b, r * 256 : (r + 1) * 256, j * 256 : (j + 1) * 256]
                spot = slice(b * 256, (b + 1) * 256)
                q_s[2 * r + j, spot, :] = dot(block, picker(0)).astype(LOW)
                k_s[2 * r + j, spot, :] = dot(block, picker(1)).astype(LOW)
                v_s[2 * r + j, spot, :] = dot(block, picker(2)).astype(LOW)
    top_s[...] = jnp.full(top_s.shape, LOWEST, FULL)
    back = []
    for step in STEPS + (0,):
        b = (z + step) % 4
        rows = pl.ds(pl.multiple_of(b * 256, 256), 256)

        @pl.loop(0, 4)
        def _(n, b=b, rows=rows):
            r, j = n // 2, n % 2
            scores = dot_cols(q_s[n, rows, :], k_s[n]) * SCALE
            query_ids = ids_col[r, rows, :]
            scores = jnp.where(query_ids == ids_row[r], scores, LOWEST)
            top = jnp.max(scores, axis=1, keepdims=True)
            expo = jnp.exp(scores - top)
            total = jnp.sum(expo, axis=1, keepdims=True)
            weights = (expo * (1.0 / total)).astype(LOW)
            out_s[n, b] = dot(weights, v_s[n]).astype(LOW)
            logsum[n, rows, :] = top + jnp.log(total)
            top_s[n] = jnp.maximum(top_s[n], jnp.where(query_ids >= 0.0, top, LOWEST))

        for n in range(4):
            r, j = n // 2, n % 2
            source = out_s.at[n, b]
            spot = (pl.ds(r * 256, 256), lanes(z * 256 + j * 128, 128))
            if step:
                back.append(copies.start(source, mixed.at[spot], moved(at, "z", step)))
            else:
                copy = pltpu.make_async_copy(source, mixed.at[spot], local.at[6 + n])
                copy.start()
                back.append(copy)
        if step == 2:
            for g in behind:
                g.forward(2)
    row = lax.broadcasted_iota(jnp.int32, (8, 128), 0)
    high = [jnp.maximum(jnp.max(top_s[j]), jnp.max(top_s[2 + j])) for j in range(2)]
    peak[...] = jnp.where(row == 0, high[0], high[1])
    for copy in back[:12]:
        copy.wait_recv()
    for copy in back[12:]:
        copy.wait()
    cot_own.wait()
    cot_copy.wait_recv()
    gq_copy.wait()
    for g in behind:
        g.settle()
    sent = [first, ids_copy, n1_copy, cot_copy] + started + back[:12]
    for copy in sent + [copy for g in ahead + behind for copy in g.sent]:
        copy.wait_send()


def forward(pack, n1, cot, ids, bias):
    count = 4 + 3 + 12 + 4 * 45
    return pl.pallas_call(
        forward_kernel,
        out_shape=[
            jax.ShapeDtypeStruct((2, 4, 144, 1024), LOW),
            jax.ShapeDtypeStruct((2, 4, 144, 2048), LOW),
            jax.ShapeDtypeStruct((2, 4, 144, 2048), LOW),
            jax.ShapeDtypeStruct((2, 4, 144, 2048), LOW),
            jax.ShapeDtypeStruct((1152, 512), LOW),
            jax.ShapeDtypeStruct((512, 1152), LOW),
            jax.ShapeDtypeStruct((8, 128), FULL),
            jax.ShapeDtypeStruct((512, 1024), LOW),
            jax.ShapeDtypeStruct((4, 1024, 128), LOW),
            jax.ShapeDtypeStruct((4, 1024, 128), LOW),
            jax.ShapeDtypeStruct((4, 1024, 128), LOW),
            jax.ShapeDtypeStruct((4, 1024, 1), FULL),
            jax.ShapeDtypeStruct((8, 128), FULL),
        ],
        in_specs=[vmem(), anywhere(), anywhere(), vmem(), vmem()],
        out_specs=[hbm()] * 4
        + [vmem(), hbm(), vmem(), anywhere()]
        + [vmem()] * 5,
        scratch_shapes=[
            pltpu.VMEM((144, UNIT), FULL),
            pltpu.VMEM((144, UNIT), LOW),
            pltpu.VMEM((2, 4, 144, 2048), LOW),
            pltpu.VMEM((4, 512, 512), LOW),
            pltpu.VMEM((512, 1152), LOW),
            pltpu.VMEM((4, 512, 512), LOW),
            pltpu.VMEM((2, 1, 1024), FULL),
            pltpu.VMEM((2, 1024, 1), FULL),
            pltpu.VMEM((4, 4, 256, 128), LOW),
            pltpu.VMEM((4, 256, 1), FULL),
            pltpu.SemaphoreType.DMA((count,)),
            pltpu.SemaphoreType.DMA((count,)),
            pltpu.SemaphoreType.DMA((10,)),
        ],
        compiler_params=pltpu.CompilerParams(
            collective_id=0, has_side_effects=True, vmem_limit_bytes=48 << 20
        ),
        name="forward_attention",
    )(pack, n1, cot, ids, bias)


def selector(offset):
    row = lax.broadcasted_iota(jnp.int32, (1024, 128), 0)
    lane = lax.broadcasted_iota(jnp.int32, (1024, 128), 1)
    inner = (row & 127) - offset
    hit = (inner >= 0) & (inner < TAIL) & (lane == (row >> 7) * TAIL + inner)
    return jnp.where(hit, 1.0, 0.0).astype(LOW)


def smooth(inner):
    root = 0.7978845608028654
    square = inner * inner
    wave = jnp.tanh(root * inner * (1.0 + 0.044715 * square))
    up = 0.5 * (1.0 + wave)
    slope = up + 0.5 * inner * (1.0 - wave * wave) * root * (1.0 + 3 * 0.044715 * square)
    return inner * up, slope


def mean(values):
    return jnp.sum(values, axis=1, keepdims=True) * (1.0 / values.shape[1])


def column_sum(values):
    return jnp.sum(values.astype(FULL), axis=0, keepdims=True)


def middle_kernel(
    mixed, go, gu, gd, tokens, cot_rows, consts, up_bias,
    result, middle_grad, mixed_grad, dgo, dgu, dgd, sums_hidden, sums,
    go_v, gu_v, gd_v, ut, dt, n2, n2t, ct, acc2, acc3, xhat, mid, bg, dgo_acc, dgo_v, dgu_v, dgd_v,
    out1, out2, out3, in1, in2, in3, send, receive, local,
):
    sibling = moved(place(), "core", 1)
    loads = [
        pltpu.make_async_copy(a, b, local.at[k])
        for k, (a, b) in enumerate(((go, go_v), (gu, gu_v), (gd, gd_v)))
    ]
    for copy in loads:
        copy.start()
    greet([sibling])
    copies = Copies(send, receive)
    out_bias, gain, shift, down_bias = (consts[k : k + 1, :] for k in range(4))
    first, second = slice(0, 256), slice(256, 512)
    thirds = [slice(k * 384, (k + 1) * 384) for k in range(3)]
    quarters = [slice(k * 256, (k + 1) * 256) for k in range(4)]
    loads[0].wait()
    for cols in thirds:
        out1[:, cols] = dot_cols(mixed[second, :], go_v[cols, :]).astype(LOW)
    branch = copies.start(out1, in1, sibling)
    for cols in thirds:
        mid[:, cols] = (
            dot_cols(mixed[first, :], go_v[cols, :])
            + tokens[:, cols].astype(FULL)
            + out_bias[:, cols]
        )
    ut[...] = dot(go_v[...], selector(72)).astype(LOW)
    dt[...] = dot(go_v[...], selector(72 + TAIL)).astype(LOW)
    branch.wait_recv()
    middle = mid[...] + in1[...].astype(FULL)
    mid[...] = middle
    centre = middle - mean(middle)
    inverse = lax.rsqrt(mean(centre * centre) + EPSILON)
    scaled = centre * inverse
    xhat[...] = scaled
    n2[first, :] = (scaled * gain + shift).astype(LOW)
    normed = copies.start(n2.at[pl.ds(0, 256)], n2.at[pl.ds(256, 256)], sibling)
    ct[...] = cot_rows[...].T
    acc2[...] = jnp.zeros(acc2.shape, FULL)
    acc3[...] = jnp.zeros(acc3.shape, FULL)
    normed.wait_recv()
    n2t[...] = n2[...].T
    loads[1].wait()
    loads[2].wait()

    def hidden_block(u, d, bias):
        active, slope = smooth(dot(n2[...], u) + bias)
        upper = (dot(cot_rows[...], d) * slope).astype(LOW)
        active = active.astype(LOW)
        acc2[...] += dot_cols(active, d)
        acc3[...] += dot_cols(upper, u)
        return active, upper

    def grad_copies(f):
        cols = lanes(f * 256, 256)
        return [
            pltpu.make_async_copy(dgu_v.at[:, cols], dgu.at[:, cols], local.at[3 + f]),
            pltpu.make_async_copy(dgd_v.at[:, cols], dgd.at[:, cols], local.at[11 + f]),
        ]

    @pl.loop(0, 8)
    def _(f):
        cols = lanes(f * 256, 256)
        active, upper = hidden_block(gu_v[:, cols], gd_v[:, cols], up_bias[:, cols])
        sums_hidden[:, cols] = column_sum(upper)
        dgd_v[:, cols] = dot(ct[...], active).astype(LOW)
        dgu_v[:, cols] = dot(n2t[...], upper).astype(LOW)
        for copy in grad_copies(f):
            copy.start()

    active, upper = hidden_block(ut[...], dt[...], up_bias[:, 2048:HIDDEN])
    sums_hidden[:, 2048:HIDDEN] = column_sum(upper)
    out3[...] = acc3[second, :].astype(LOW)
    back = copies.start(out3, in3, sibling)
    out2[...] = acc2[second, :].astype(LOW)
    forth = copies.start(out2, in2, sibling)
    up_tail = dot_cols(upper, selector(72)).astype(LOW)
    down_tail = dot_cols(active, selector(72 + TAIL)).astype(LOW)
    for cols in quarters:
        dgo_acc[:, cols] = dot(n2t[...], up_tail[:, cols]) + dot(ct[...], down_tail[:, cols])
    back.wait_recv()
    upstream = cot_rows[first, :].astype(FULL)
    normed_grad = acc3[first, :] + in3[...].astype(FULL)
    scaled = xhat[...]
    along = normed_grad * gain
    grad = upstream + inverse * (along - mean(along) - scaled * mean(along * scaled))
    middle_grad[...] = grad
    low = grad.astype(LOW)
    bg[first, :] = low
    branch_grad = copies.start(bg.at[pl.ds(0, 256)], bg.at[pl.ds(256, 256)], sibling)
    sums[0:1, :] = column_sum(low)
    sums[1:2, :] = column_sum(upstream)
    sums[2:3, :] = column_sum(normed_grad * scaled)
    sums[3:4, :] = column_sum(normed_grad)
    sums[4:8, :] = jnp.zeros((4, 1152), FULL)
    forth.wait_recv()
    result[...] = mid[...] + acc2[first, :] + in2[...].astype(FULL) + down_bias
    branch_grad.wait_recv()
    for cols in quarters:
        mixed_grad[:, cols] = dot(bg[...], go_v[:, cols]).astype(LOW)
    for cols in quarters:
        dgo_v[:, cols] = (dgo_acc[:, cols] + dot_rows(bg[...], mixed[:, cols])).astype(LOW)
    last = pltpu.make_async_copy(dgo_v, dgo, local.at[19])
    last.start()
    for f in range(8):
        for copy in grad_copies(f):
            copy.wait()
    last.wait()
    for copy in (branch, normed, back, forth, branch_grad):
        copy.wait_send()


def middle_block(mixed, go, gu, gd, tokens, cot_rows, consts, up_bias):
    rows, half = (512, 1152), (256, 1152)
    return pl.pallas_call(
        middle_kernel,
        out_shape=[
            jax.ShapeDtypeStruct(half, FULL),
            jax.ShapeDtypeStruct(half, FULL),
            jax.ShapeDtypeStruct((512, 1024), LOW),
            jax.ShapeDtypeStruct((1152, 1024), LOW),
            jax.ShapeDtypeStruct((1152, 2048), LOW),
            jax.ShapeDtypeStruct((1152, 2048), LOW),
            jax.ShapeDtypeStruct((1, HIDDEN), FULL),
            jax.ShapeDtypeStruct((8, 1152), FULL),
        ],
        in_specs=[vmem()] + [hbm()] * 3 + [vmem()] * 4,
        out_specs=[vmem()] * 3 + [hbm()] * 3 + [vmem()] * 2,
        scratch_shapes=[
            pltpu.VMEM((1152, 1024), LOW),
            pltpu.VMEM((1152, 2048), LOW),
            pltpu.VMEM((1152, 2048), LOW),
            pltpu.VMEM((1152, 128), LOW),
            pltpu.VMEM((1152, 128), LOW),
            pltpu.VMEM(rows, LOW),
            pltpu.VMEM((1152, 512), LOW),
            pltpu.VMEM((1152, 512), LOW),
            pltpu.VMEM(rows, FULL),
            pltpu.VMEM(rows, FULL),
            pltpu.VMEM(half, FULL),
            pltpu.VMEM(half, FULL),
            pltpu.VMEM(rows, LOW),
            pltpu.VMEM((1152, 1024), FULL),
            pltpu.VMEM((1152, 1024), LOW),
            pltpu.VMEM((1152, 2048), LOW),
            pltpu.VMEM((1152, 2048), LOW),
        ]
        + [pltpu.VMEM(half, LOW)] * 6
        + [
            pltpu.SemaphoreType.DMA((5,)),
            pltpu.SemaphoreType.DMA((5,)),
            pltpu.SemaphoreType.DMA((20,)),
        ],
        compiler_params=pltpu.CompilerParams(
            collective_id=2, has_side_effects=True, vmem_limit_bytes=58 << 20
        ),
        name="middle_block",
    )(mixed, go, gu, gd, tokens, cot_rows, consts, up_bias)


def backward_kernel(
    upstream, q_s, k_s, v_s, ids, ids_other, logsum, go, gu, gd, gq, n1t, tokens, middle_grad, gain,
    sums_hidden, sums, peak, token_grad, out, totals, *rest
):
    (
        grad, g_s, dq_s, dk_s, dv_s, out_s, ids_row, ids_col, back, gq_v, dgq, part_mine,
        part_out, part_in, unit, other, line, near_lines, send, receive, local,
    ) = rest[:21]
    buffers = list(rest[21:])
    at = place()
    z, core = at["z"], at["core"]
    sibling = moved(at, "core", 1)
    partners = [moved(at, "z", step) for step in STEPS]
    gq_copy = pltpu.make_async_copy(gq, gq_v, local.at[3])
    gq_copy.start()
    greet([sibling] + [moved(at, axis, step) for axis in ALL for step in STEPS])
    copies = Copies(send, receive)
    sent = []
    started = [
        copies.start(upstream.at[:, lanes(partner["z"] * 256, 256)], grad.at[z], partner)
        for partner in partners
    ]
    sent += started
    own = pltpu.make_async_copy(upstream.at[:, lanes(z * 256, 256)], grad.at[z], local.at[0])
    own.start()
    counter = [local, 4]
    behind = [
        Scatter(copies, at, [go, gu, gd], WIDTHS[1:], part, buffers, counter)
        for part in PARTS_BEHIND
    ]
    last = [Scatter(copies, at, [dgq], WIDTHS[:1], part, buffers) for part in PARTS]
    for s in behind:
        s.begin(0)
    set_ids(ids, 0, ids_row, ids_col)
    set_ids(ids_other, 1, ids_row, ids_col)
    own.wait()
    for copy in started:
        copy.wait_recv()
    lane = lax.broadcasted_iota(jnp.int32, (256, 128), 1)
    for r in range(2):
        for j in range(2):
            for b in range(4):
                block = grad[b, r * 256 : (r + 1) * 256, j * 128 : (j + 1) * 128]
                g_s[2 * r + j, b * 256 : (b + 1) * 256, :] = jnp.where(
                    lane < HEAD_DIM, block.astype(FULL), 0.0
                ).astype(LOW)
    returned = [[], []]
    for r in range(2):
        for j in range(2):
            n = 2 * r + j
            dk_s[...] = jnp.zeros(dk_s.shape, FULL)
            dv_s[...] = jnp.zeros(dv_s.shape, FULL)

            @pl.loop(0, 4)
            def _(b, n=n, r=r):
                rows = pl.ds(pl.multiple_of(b * 256, 256), 256)
                query, upper = q_s[n, rows, :], g_s[n, rows, :]
                scores = dot_cols(query, k_s[n]) * SCALE
                allowed = ids_col[r, rows, :] == ids_row[r]
                probs = jnp.where(allowed, jnp.exp(scores - logsum[n, rows, :]), 0.0)
                dv_s[...] += dot_rows(probs.astype(LOW), upper)
                prob_grad = dot_cols(upper, v_s[n])
                centre = jnp.sum(probs * prob_grad, axis=1, keepdims=True)
                score_grad = (probs * (prob_grad - centre)).astype(LOW)
                dq_s[rows, :] = (dot(score_grad, k_s[n]) * SCALE).astype(LOW)
                dk_s[...] += dot_rows(score_grad, query)

            for b in range(4):
                spot = slice(b * 256, (b + 1) * 256)
                out_s[b, r * 256 : (r + 1) * 256, j * 256 : (j + 1) * 256] = (
                    dot(dq_s[spot, :], placer(0))
                    + dot((dk_s[spot, :] * SCALE).astype(LOW), placer(1))
                    + dot(dv_s[spot, :].astype(LOW), placer(2))
                ).astype(LOW)
        rows = pl.ds(r * 256, 256)
        for partner in partners:
            source = out_s.at[partner["z"], rows]
            copy = copies.start(source, back.at[rows, lanes(z * 512, 512)], partner)
            returned[r].append(copy)
            sent.append(copy)
        back[rows, lanes(z * 512, 512)] = out_s[z, r * 256 : (r + 1) * 256, :]
        if r == 0:
            for s in behind:
                s.relay(0)
    gq_copy.wait()
    thirds = [slice(k * 384, (k + 1) * 384) for k in range(3)]
    for copy in returned[0]:
        copy.wait_recv()
    for cols in thirds:
        part_mine[:, cols] = dot_cols(back[0:256, :], gq_v[cols, :])
    for s in behind:
        s.finish(0)
        s.begin(1)
    for s in behind:
        s.relay(1)
    for copy in returned[1]:
        copy.wait_recv()
    for cols in thirds:
        part_out[:, cols] = dot_cols(back[256:512, :], gq_v[cols, :]).astype(LOW)
    part = copies.start(part_out, part_in, sibling)
    sent.append(part)

    @pl.loop(0, 8)
    def _(f):
        cols = lanes(f * 256, 256)
        dgq[:, :, :, cols] = dot(n1t[...], back[:, cols]).astype(LOW).reshape(2, 4, 144, 256)

    for s in last:
        s.begin(0)
    for s in behind:
        s.finish(1)
        s.last()
    part.wait_recv()
    normed_grad = part_mine[...] + part_in[...].astype(FULL)
    values = tokens[...].astype(FULL)
    centre = values - mean(values)
    inverse = lax.rsqrt(mean(centre * centre) + EPSILON)
    scaled = centre * inverse
    along = normed_grad * gain[...]
    token_grad[...] = middle_grad[...] + inverse * (
        along - mean(along) - scaled * mean(along * scaled)
    )
    pieces = [
        column_sum(back[...]),
        sums_hidden[...],
        sums[0:1, :],
        sums[1:2, :],
        column_sum(normed_grad * scaled),
        column_sum(normed_grad),
        sums[2:3, :],
        sums[3:4, :],
        jnp.zeros((1, 128), FULL),
    ]
    row = 0
    for piece in pieces:
        for k in range(piece.shape[1] // 128):
            line[0, row : row + 1, :] = piece[:, k * 128 : (k + 1) * 128]
            row += 1
    head = lax.broadcasted_iota(jnp.int32, (8, 128), 1) - (4 * z + core)
    line[0, 88:96, :] = jnp.where(
        head == 0, peak[0:1, 0:1], jnp.where(head == 2, peak[1:2, 0:1], LOWEST)
    )

    def send_line(phase):
        begun = [
            copies.start(line.at[phase], near_lines.at[phase, k], moved(at, ALL[phase], step))
            for k, step in enumerate(STEPS)
        ]
        sent.extend(begun)
        return begun

    def add_line(phase, begun):
        for copy in begun:
            copy.wait_recv()
        parts = [line[phase]] + [near_lines[phase, k] for k in range(3)]
        line[phase + 1, 0:88, :] = (parts[0][:88] + parts[1][:88]) + (parts[2][:88] + parts[3][:88])
        line[phase + 1, 88:96, :] = jnp.maximum(
            jnp.maximum(parts[0][88:], parts[1][88:]), jnp.maximum(parts[2][88:], parts[3][88:])
        )

    arriving = send_line(0)
    for s in last:
        s.relay(0)
    for s in behind:
        s.result(unit, [start for start in STARTS[1:]])
    mine = pl.ds(pl.multiple_of(core * 72, 8), 72)
    theirs = pl.ds(pl.multiple_of((1 - core) * 72, 8), 72)
    early = copies.start(unit.at[theirs, pl.ds(256, UNIT - 256)], other.at[:, pl.ds(256, UNIT - 256)], sibling)
    add_line(0, arriving)
    arriving = send_line(1)
    for s in last:
        s.finish(0)
        s.begin(1)
    add_line(1, arriving)
    arriving = send_line(2)
    for s in last:
        s.relay(1)
    for s in last:
        s.finish(1)
        s.last()
    add_line(2, arriving)
    line_copy = copies.start(line.at[3], totals.at[core], sibling)
    totals[core] = line[3]
    for s in last:
        s.result(unit, [0])
    late = copies.start(unit.at[theirs, pl.ds(0, 256)], other.at[:, pl.ds(0, 256)], sibling)
    out[core] = unit[mine, :]
    early.wait_recv()
    late.wait_recv()
    out[1 - core] = other[...]
    line_copy.wait_recv()
    sent += [early, late, line_copy]
    for copy in sent + [copy for s in behind + last for copy in s.sent]:
        copy.wait_send()


def backward(upstream, heads, ids, ids_other, logsum, grids, gq, n1t, tokens, middle_grad, gain, sums_hidden, sums, peak):
    count = 3 + 6 + 4 * 45 + 9 + 4
    shapes = []
    for part in PARTS_BEHIND:
        shapes += Scatter.shapes(WIDTHS[1:], part, True)
    for part in PARTS:
        shapes += Scatter.shapes(WIDTHS[:1], part, False)
    half = (256, 1152)
    return pl.pallas_call(
        backward_kernel,
        out_shape=[
            jax.ShapeDtypeStruct(half, FULL),
            jax.ShapeDtypeStruct((2, 72, UNIT), FULL),
            jax.ShapeDtypeStruct((2, 96, 128), FULL),
        ],
        in_specs=[anywhere()] + [vmem()] * 6 + [anywhere()] * 4 + [vmem()] * 7,
        out_specs=[vmem()] * 3,
        scratch_shapes=[
            pltpu.VMEM((4, 512, 256), LOW),
            pltpu.VMEM((4, 1024, 128), LOW),
            pltpu.VMEM((1024, 128), LOW),
            pltpu.VMEM((1024, 128), FULL),
            pltpu.VMEM((1024, 128), FULL),
            pltpu.VMEM((4, 512, 512), LOW),
            pltpu.VMEM((2, 1, 1024), FULL),
            pltpu.VMEM((2, 1024, 1), FULL),
            pltpu.VMEM((512, 2048), LOW),
            pltpu.VMEM((1152, 2048), LOW),
            pltpu.VMEM((2, 4, 144, 2048), LOW),
            pltpu.VMEM(half, FULL),
            pltpu.VMEM(half, LOW),
            pltpu.VMEM(half, LOW),
            pltpu.VMEM((144, UNIT), FULL),
            pltpu.VMEM((72, UNIT), FULL),
            pltpu.VMEM((4, 96, 128), FULL),
            pltpu.VMEM((3, 3, 96, 128), FULL),
            pltpu.SemaphoreType.DMA((count,)),
            pltpu.SemaphoreType.DMA((count,)),
            pltpu.SemaphoreType.DMA((48,)),
        ]
        + shapes,
        compiler_params=pltpu.CompilerParams(
            collective_id=1, has_side_effects=True, vmem_limit_bytes=60 << 20
        ),
        name="backward_attention",
    )(
        upstream, *heads, ids, ids_other, logsum, *grids, gq, n1t, tokens, middle_grad, gain, sums_hidden,
        sums, peak,
    )


def normalize(values, gain, shift):
    centre = values - jnp.mean(values, axis=-1, keepdims=True)
    inverse = lax.rsqrt(jnp.mean(centre * centre, axis=-1, keepdims=True) + EPSILON)
    return centre * inverse * gain + shift


def per_device(
    tokens,
    picture,
    cotangent,
    gain_one,
    shift_one,
    query_weight,
    query_bias,
    key_weight,
    value_weight,
    value_bias,
    out_weight,
    out_bias,
    gain_two,
    shift_two,
    up_weight,
    up_bias,
    down_weight,
    down_bias,
):
    width = tokens.shape[1]
    t = lax.axis_index("tensor")
    core = lax.axis_index("dp") % 2
    gain_first = gain_one.astype(FULL)

    out_t = out_weight.astype(FULL).T
    down_t = down_weight.astype(FULL).T
    up = up_weight.astype(FULL)
    halves = []
    for h in range(2):
        cols = slice(h * 72, (h + 1) * 72)
        first = h * (MAIN + TAIL)
        main, tail = slice(first, first + MAIN), slice(first + MAIN, first + MAIN + TAIL)
        halves.append(
            jnp.concatenate(
                [
                    query_weight[:, cols].astype(FULL),
                    key_weight[:, cols].astype(FULL),
                    value_weight[:, cols].astype(FULL),
                    jnp.zeros((72, 40), FULL),
                    out_t[:, cols],
                    up[:, tail],
                    down_t[:, tail],
                    jnp.zeros((72, 30), FULL),
                    up[:, main],
                    down_t[:, main],
                ],
                axis=1,
            )
        )
    pack = jnp.stack(halves)

    inputs = tokens.astype(FULL)
    normed = normalize(inputs, gain_first, shift_one.astype(FULL))
    normed_mine = normed.astype(LOW)
    half = lax.dynamic_slice_in_dim(picture, (t // 4) * 1024, 1024)
    ids = jnp.where(half >= 0, half, -1 - jnp.arange(1024, dtype=jnp.int32)).astype(FULL)
    def halves_of(vector, size):
        return lax.dynamic_index_in_dim(
            vector.astype(FULL).reshape(8, 2, size), core, axis=1, keepdims=False
        )

    query_b, value_b = halves_of(query_bias, 72), halves_of(value_bias, 72)
    proj_bias = jnp.concatenate(
        [query_b, jnp.zeros((8, 72), FULL), value_b, jnp.zeros((8, 40), FULL)], axis=1
    ).reshape(1, 2048)
    up_b = halves_of(up_bias, MAIN + TAIL)
    hidden_bias = jnp.concatenate(
        [up_b[:, :MAIN].reshape(2048), up_b[:, MAIN:].reshape(8 * TAIL), jnp.zeros((24,), FULL)]
    ).reshape(1, HIDDEN)

    go, gu, gd, gq, rows_one_t, cot_rows, ids_other, mixed, *heads, logsum, peak = forward(
        pack, normed_mine, cotangent, ids.reshape(8, 128), proj_bias
    )
    gq = gq.reshape(width, 2048)
    consts = jnp.concatenate(
        [
            jnp.stack([out_bias, gain_two, shift_two, down_bias]).astype(FULL),
            jnp.zeros((4, width), FULL),
        ]
    )
    result, middle_grad, mixed_grad, grad_o, grad_u, grad_d, sums_hidden, sums = middle_block(
        mixed,
        go.reshape(width, 1024),
        gu.reshape(width, 2048),
        gd.reshape(width, 2048),
        tokens,
        cot_rows,
        consts,
        hidden_bias,
    )
    shape = (2, 4, 144)
    input_grad, grads, totals = backward(
        mixed_grad,
        heads,
        ids.reshape(8, 128),
        ids_other,
        logsum,
        [
            grad_o.reshape(shape + (1024,)),
            grad_u.reshape(shape + (2048,)),
            grad_d.reshape(shape + (2048,)),
        ],
        gq,
        rows_one_t,
        tokens,
        middle_grad,
        gain_first.reshape(1, width),
        sums_hidden,
        sums,
        peak,
    )

    def side(first, size):
        return jnp.concatenate([grads[0, :, first : first + size], grads[1, :, first : first + size]], axis=1)

    def hidden_side(main, tail):
        return jnp.concatenate(
            [
                grads[0, :, main : main + MAIN],
                grads[0, :, tail : tail + TAIL],
                grads[1, :, main : main + MAIN],
                grads[1, :, tail : tail + TAIL],
            ],
            axis=1,
        )

    query_w, key_w, value_w = side(0, 72), side(72, 72), side(144, 72)
    out_w = side(256, 72).T
    up_w = hidden_side(384, 256 + 72)
    down_w = hidden_side(640, 256 + 72 + TAIL).T
    flat = totals[:, :88].reshape(2, 88 * 128)
    heads = flat[:, :2048].reshape(2, 8, 256)
    query_b_grad = heads[:, :, :72].transpose(1, 0, 2).reshape(width)
    value_b_grad = heads[:, :, 144:216].transpose(1, 0, 2).reshape(width)
    up_b_grad = (
        jnp.concatenate(
            [
                flat[:, 2048:4096].reshape(2, 8, MAIN),
                flat[:, 4096 : 4096 + 8 * TAIL].reshape(2, 8, TAIL),
            ],
            axis=2,
        )
        .transpose(1, 0, 2)
        .reshape(-1)
    )
    summed = (flat[0] + flat[1])[2048 + HIDDEN : 2048 + HIDDEN + 6 * width].reshape(6, width)
    high = jnp.maximum(totals[0, 88, :16], totals[1, 88, :16])
    factor = jnp.sqrt(CLIP_LIMIT / jnp.maximum(high, CLIP_LIMIT))
    column_factor = jnp.repeat(lax.dynamic_slice_in_dim(factor, 2 * t, 2), HEAD_DIM)
    clipped_query = query_weight.astype(FULL) * column_factor[None, :]
    clipped_key = key_weight.astype(FULL) * column_factor[None, :]
    return (
        result,
        input_grad,
        query_w,
        key_w,
        value_w,
        out_w,
        up_w,
        down_w,
        query_b_grad,
        value_b_grad,
        up_b_grad,
        summed[0],
        summed[1],
        summed[2],
        summed[3],
        summed[4],
        summed[5],
        clipped_query,
        clipped_key,
    )


def solution(mesh):
    in_specs = (
        P(("dp", "tensor"), None),
        P("dp"),
        P(("dp", "tensor"), None),
        P(),
        P(),
        P("dp", "tensor"),
        P(),
        P("dp", "tensor"),
        P("dp", "tensor"),
        P(),
        P("tensor", "dp"),
        P(),
        P(),
        P(),
        P("dp", "tensor"),
        P(),
        P("tensor", "dp"),
        P(),
    )
    out_specs = (
        P(("dp", "tensor"), None),
        P(("dp", "tensor"), None),
        P("dp", "tensor"),
        P("dp", "tensor"),
        P("dp", "tensor"),
        P("tensor", "dp"),
        P("dp", "tensor"),
        P("tensor", "dp"),
        P(),
        P(),
        P(),
        P(),
        P(),
        P(),
        P(),
        P(),
        P(),
        P("dp", "tensor"),
        P("dp", "tensor"),
    )
    return jax.shard_map(
        per_device, mesh=mesh, in_specs=in_specs, out_specs=out_specs, check_vma=False
    )
```

```python
import functools

import jax
import jax.numpy as jnp
import numpy as np
from jax import lax
from jax.experimental import pallas as pl
from jax.experimental.pallas import tpu as pltpu
from jax.sharding import PartitionSpec as P

HEAD_DIM = 72
EPSILON = 1e-06
CLIP_LIMIT = 2.0
LOWEST = -1e30
SCALE = HEAD_DIM**-0.5

MESH = pl.DeviceIdType.MESH
LOW = jnp.bfloat16
FULL = jnp.float32

STARTS = (0, 256, 384, 640)
WIDTHS = (256, 128, 256, 256)
STREAMS = ((0, 1), (2,))
UNIT = 896
MAIN = 256
TAIL = 13
HIDDEN = 8 * MAIN + 128
PARTS = ((0, 80, "xy"), (80, 64, "yx"))
PARTS_BEHIND = ((0, 48, "zyx"), (48, 64, "zxy"), (112, 32, "yxz"))
PARTS_BACK = ((0, 64, "zyx"), (64, 64, "zxy"), (128, 16, "yxz"))
STEPS = (1, 3, 2)
ALL = "xyz"


def place():
    d, t = lax.axis_index("dp"), lax.axis_index("tensor")
    return {"x": (d // 2) % 4, "y": (t // 4) * 2 + d // 8, "z": t % 4, "core": d % 2}


def device(at):
    return ((at["y"] % 2) * 8 + at["x"] * 2 + at["core"], (at["y"] // 2) * 4 + at["z"])


def moved(at, axis, step):
    other = dict(at)
    other[axis] = 1 - at["core"] if axis == "core" else (at[axis] + step) % 4
    return other


def greet(partners):
    barrier = pltpu.get_barrier_semaphore()
    for partner in partners:
        pl.semaphore_signal(barrier, inc=1, device_id=device(partner), device_id_type=MESH)
    pl.semaphore_wait(barrier, len(partners))


class Copies:
    def __init__(self, send, receive):
        self.send, self.receive, self.used = send, receive, 0

    def start(self, source, target, partner):
        copy = pltpu.make_async_remote_copy(
            src_ref=source,
            dst_ref=target,
            send_sem=self.send.at[self.used],
            recv_sem=self.receive.at[self.used],
            device_id=device(partner),
            device_id_type=MESH,
        )
        self.used += 1
        copy.start()
        return copy


def lanes(first, size):
    return pl.ds(first if isinstance(first, int) else pl.multiple_of(first, 128), size)


def spots(held, have, at, width, rows, half=None):
    zs, ys = (4 if "z" in held else 1), at["y"] if "y" in held else 0
    x_at = pl.ds(0, 4) if "x" in have else pl.ds(at["x"] if "x" in held else 0, 1)
    y_at = pl.ds(0, 2) if "y" in have else pl.ds(ys % 2, 1)
    z = at["z"] if "z" in held else 0
    if "y" in have and "z" in have:
        ranges = [(0, 8 * width)]
    elif "y" in have:
        ranges = [((h * zs + z) * width, width) for h in (0, 1)]
    elif "z" in have:
        ranges = [((ys // 2) * zs * width, 4 * width)]
    else:
        ranges = [(((ys // 2) * zs + z) * width, width)]
    if half is not None:
        if len(ranges) == 2:
            ranges = [ranges[half]]
        elif "x" in have:
            x_at = pl.ds(2 * half, 2)
        elif "y" in have:
            y_at = pl.ds(half, 1)
        else:
            ((first, size),) = ranges
            ranges = [(first + half * (size // 2), size // 2)]
    return [(y_at, x_at, pl.ds(*rows), lanes(*r)) for r in ranges]


def rect_shape(have, width, rows):
    ys, xs, zs = 2 if "y" in have else 1, 4 if "x" in have else 1, 4 if "z" in have else 1
    return (ys, xs, rows, ys * zs * width)


class Gather:
    def __init__(self, copies, at, grids, widths, part, held=ALL):
        self.copies, self.at, self.grids, self.widths = copies, at, grids, widths
        self.rows, self.order, self.held = part[:2], part[2], held
        self.arriving, self.sent = [], []

    def views(self, grid, width, have, at, half=None):
        return [grid.at[spot] for spot in spots(self.held, have, at, width, self.rows, half)]

    def send(self, have, owner, partner, half=None):
        started = []
        for grid, width in zip(self.grids, self.widths):
            for view in self.views(grid, width, have, owner, half):
                started.append(self.copies.start(view, view, partner))
        self.sent += started
        return started

    def settle(self):
        for copy in self.arriving:
            copy.wait_recv()
        self.arriving = []

    def first(self):
        for step in STEPS:
            self.arriving += self.send("", self.at, moved(self.at, self.order[0], step))

    def ring(self, phase):
        self.settle()
        axis, have = self.order[phase], self.order[:phase]
        self.after = self.send(have, self.at, moved(self.at, axis, 1))
        self.before = self.send(have, self.at, moved(self.at, axis, 3))

    def forward(self, phase):
        axis, have = self.order[phase], self.order[:phase]
        up, down = moved(self.at, axis, 1), moved(self.at, axis, 3)
        for copy in self.after:
            copy.wait_recv()
        self.arriving += self.send(have, down, up, 0)
        for copy in self.before:
            copy.wait_recv()
        self.arriving += self.send(have, up, down, 1)


def add_into(target, terms, shape):
    @pl.loop(0, shape[0] * shape[1] * (shape[2] // 16))
    def _(n):
        block = n // (shape[2] // 16)
        spot = (
            block // shape[1],
            block % shape[1],
            pl.ds(pl.multiple_of((n % (shape[2] // 16)) * 16, 16), 16),
            slice(None),
        )
        total = terms[0][spot].astype(FULL)
        for term in terms[1:]:
            total = total + term[spot].astype(FULL)
        target[spot] = total.astype(target.dtype)


def half_shape(have, shape):
    ys, xs, rows, cols = shape
    if "y" in have and "z" not in have:
        return (ys, xs, rows, cols // 2)
    if "x" in have:
        return (ys, 2, rows, cols)
    if "y" in have:
        return (1, xs, rows, cols)
    return (ys, xs, rows, cols // 2)


class Scatter:
    @staticmethod
    def shapes(widths, part, loaded):
        _, rows, order = part
        shapes = []
        for phase in range(len(order) - 1):
            have = order[: len(order) - 1 - phase]
            for _ in range(5 if loaded and phase == 0 else 4):
                shapes += [pltpu.VMEM(rect_shape(have, w, rows), LOW) for w in widths]
        shapes += [pltpu.VMEM((3, 1, 1, rows, w), LOW) for w in widths]
        return shapes

    def __init__(self, copies, at, grids, widths, part, buffers, held=ALL, local=None):
        self.copies, self.at, self.grids, self.widths = copies, at, grids, widths
        self.rows, self.order = part[:2], part[2]
        self.rings = len(self.order) - 1
        self.held = [held] + [self.order[: self.rings - phase] for phase in range(self.rings)]
        self.local = local
        self.sent = []

        def take():
            taken, buffers[:] = buffers[: len(widths)], buffers[len(widths) :]
            return taken

        self.near, self.low, self.high, self.own = [], [], [], []
        for phase in range(self.rings):
            for group in (self.near, self.low, self.high, self.own):
                group.append(take())
            if phase == 0 and local:
                self.mix = [take()]
        self.direct = take()

    def have(self, phase):
        return self.order[: self.rings - phase]

    def source(self, phase, a, at, half=None):
        grid = self.grids[a] if phase == 0 else self.own[phase - 1][a]
        rows = self.rows if phase == 0 else (0, self.rows[1])
        found = spots(self.held[phase], self.have(phase), at, self.widths[a], rows, half)
        return [grid.at[spot] for spot in found]

    def target(self, phase, buffer, a, half=None):
        have = self.have(phase)
        found = spots(have, have, self.at, self.widths[a], (0, self.rows[1]), half)
        return [buffer[phase][a].at[spot] for spot in found]

    def push(self, sources, targets, partner):
        started = [self.copies.start(s, t, partner) for s, t in zip(sources, targets)]
        self.sent += started
        return started

    def begin(self, phase):
        axis = self.order[self.rings - phase]
        up, down, far = (moved(self.at, axis, step) for step in STEPS)
        self.arriving, self.loading = [], []
        for a in range(len(self.grids)):
            for half, partner in ((0, up), (1, down)):
                self.arriving += self.push(
                    self.source(phase, a, far, half),
                    self.target(phase, self.near, a, half),
                    partner,
                )
        if phase == 0 and self.local:
            for a in range(len(self.grids)):
                pairs = list(
                    zip(
                        self.source(0, a, up, 0) + self.source(0, a, down, 1),
                        self.target(0, self.mix, a, 0) + self.target(0, self.mix, a, 1),
                    )
                )
                pairs += list(zip(self.source(0, a, self.at), self.target(0, self.own, a)))
                for view, target in pairs:
                    copy = pltpu.make_async_copy(view, target, self.local[0].at[self.local[1]])
                    self.local[1] += 1
                    copy.start()
                    self.loading.append(copy)

    def relay(self, phase):
        axis, have = self.order[self.rings - phase], self.have(phase)
        up, down, _ = (moved(self.at, axis, step) for step in STEPS)
        for copy in self.loading:
            copy.wait()
        for copy in self.arriving:
            copy.wait_recv()
        self.arriving = []
        for a in range(len(self.grids)):
            shape = half_shape(have, rect_shape(have, self.widths[a], self.rows[1]))
            for half, partner in ((0, up), (1, down)):
                (near,) = self.target(phase, self.near, a, half)
                if phase == 0 and self.local:
                    (view,) = self.target(phase, self.mix, a, half)
                else:
                    (view,) = self.source(phase, a, partner, half)
                add_into(near, [view, near], shape)
                buffer = self.low if half == 0 else self.high
                self.arriving += self.push(
                    [near] + self.source(phase, a, partner, 1 - half),
                    self.target(phase, buffer, a, half) + self.target(phase, buffer, a, 1 - half),
                    partner,
                )

    def finish(self, phase):
        have = self.have(phase)
        for copy in self.arriving:
            copy.wait_recv()
        for a in range(len(self.grids)):
            for low, high, own, source in zip(
                self.target(phase, self.low, a),
                self.target(phase, self.high, a),
                self.target(phase, self.own, a),
                self.source(phase, a, self.at),
            ):
                shape = rect_shape(have, self.widths[a], self.rows[1])
                if "y" in have and "z" not in have:
                    shape = half_shape(have, shape)
                add_into(own, [own if phase == 0 and self.local else source, low, high], shape)

    def last(self):
        self.arriving = []
        for k, step in enumerate(STEPS):
            partner = moved(self.at, self.order[0], step)
            for a in range(len(self.grids)):
                self.arriving += self.push(
                    self.source(self.rings, a, partner), [self.direct[a].at[k]], partner
                )

    def result(self, out, starts):
        for copy in self.arriving:
            copy.wait_recv()
        for a, start in enumerate(starts):
            (mine,) = self.source(self.rings, a, self.at)
            total = mine[0, 0].astype(FULL)
            for k in range(3):
                total = total + self.direct[a][k, 0, 0].astype(FULL)
            out[pl.ds(*self.rows), start : start + self.widths[a]] = total


def hbm():
    return pl.BlockSpec(memory_space=pltpu.HBM)


def anywhere():
    return pl.BlockSpec(memory_space=pl.ANY)


def vmem():
    return pl.BlockSpec(memory_space=pltpu.VMEM)


def picker():
    row = lax.broadcasted_iota(jnp.int32, (256, 384), 0)
    lane = lax.broadcasted_iota(jnp.int32, (256, 384), 1)
    hit = ((lane & 127) < HEAD_DIM) & (row == (lane >> 7) * HEAD_DIM + (lane & 127))
    return jnp.where(hit, 1.0, 0.0).astype(LOW)


def dot(left, right):
    return jnp.dot(left, right, preferred_element_type=FULL)


def dot_rows(left, right):
    return lax.dot_general(left, right, (((0,), (0,)), ((), ())), preferred_element_type=FULL)


def dot_cols(left, right):
    return lax.dot_general(left, right, (((1,), (1,)), ((), ())), preferred_element_type=FULL)


def set_ids(ids, r, ids_row, ids_col):
    eye = lax.broadcasted_iota(jnp.int32, (128, 128), 0) == lax.broadcasted_iota(
        jnp.int32, (128, 128), 1
    )
    for k in range(8):
        piece = ids[k : k + 1, :]
        ids_row[r, :, k * 128 : (k + 1) * 128] = piece
        ids_col[r, k * 128 : (k + 1) * 128, :] = jnp.sum(
            jnp.where(eye, piece, 0.0), axis=1, keepdims=True
        )


def selector(offset):
    row = lax.broadcasted_iota(jnp.int32, (1024, 128), 0)
    lane = lax.broadcasted_iota(jnp.int32, (1024, 128), 1)
    inner = (row & 127) - offset
    hit = (inner >= 0) & (inner < TAIL) & (lane == (row >> 7) * TAIL + inner)
    return jnp.where(hit, 1.0, 0.0).astype(LOW)


def smooth(inner):
    root = 0.7978845608028654
    square = inner * inner
    wave = jnp.tanh(root * inner * (1.0 + 0.044715 * square))
    up = 0.5 * (1.0 + wave)
    slope = up + 0.5 * inner * (1.0 - wave * wave) * root * (1.0 + 3 * 0.044715 * square)
    return inner * up, slope


def mean(values):
    return jnp.sum(values, axis=1, keepdims=True) * (1.0 / values.shape[1])


def column_sum(values):
    return jnp.sum(values.astype(FULL), axis=0, keepdims=True)


def forward_kernel(
    pack, n1, cot, ids, bias, tokens, consts, up_bias,
    result, middle_grad, mixed_grad, dout, dffn_a, dffn_b, n1t_out, weights, ids_other, q_s, k_s, v_s,
    logsum, peak, sums_hidden, sums,
    both, unit, slab, go, ffn_a, ffn_b, n1_all, n1t, ids_row, ids_col, vt_s, out_s, top_s, cot_rows, mixed,
    ut, dt, n2, n2t, ct, acc2, acc3, xhat, bg, out1, out2, out3, in1, in2, in3, send, receive, local,
):
    at = place()
    core, z = at["core"], at["z"]
    sibling = moved(at, "core", 1)
    up, down, far = (moved(at, "z", step) for step in STEPS)
    grids = (go, ffn_a, ffn_b)
    loads = [
        pltpu.make_async_copy(n1, n1_all.at[z, pl.ds(0, 256)], local.at[0]),
        pltpu.make_async_copy(cot, cot_rows.at[pl.ds(0, 256)], local.at[1]),
    ]
    for copy in loads:
        copy.start()
    greet([sibling] + [moved(at, axis, step) for axis in ALL for step in STEPS])
    copies = Copies(send, receive)
    sent = []

    def start(source, target, partner):
        copy = copies.start(source, target, partner)
        sent.append(copy)
        return copy

    mine = pl.ds(pl.multiple_of(core * 72, 8), 72)
    first_copy = start(pack.at[1 - core], both.at[mine], sibling)
    ids_copy = start(ids, ids_other, sibling)

    def block(owner, r, first=0, size=256):
        return n1_all.at[owner["z"], pl.ds(r * 256 + first, size)]

    def ring_step(first):
        return [
            start(n1.at[pl.ds(first, 128)], block(at, 0, first, 128), partner) for partner in (up, down)
        ]

    ring = [ring_step(0)]
    other = {0: start(n1, block(at, 1), sibling)}
    cot_copy = start(cot, cot_rows.at[pl.ds(256, 256)], sibling)
    both[mine, :] = pack[core]
    first_copy.wait_recv()
    unit[...] = both[...].astype(LOW)
    tensor = (at["y"] // 2) * 4 + z
    slab[at["y"] % 2, at["x"], :, lanes((at["y"] // 2) * 256, 256)] = unit[:, 0:256]
    for grid, first, width in zip(grids, STARTS[1:], WIDTHS[1:]):
        grid[at["y"] % 2, at["x"], :, lanes(tensor * width, width)] = unit[:, first : first + width]
    ahead = [Gather(copies, at, [slab], [256], part, "xy") for part in PARTS]
    behind = [
        [
            Gather(copies, at, [grids[n] for n in names], [WIDTHS[n + 1] for n in names], part)
            for part in PARTS_BEHIND
        ]
        for names in STREAMS
    ]

    def step(group, name, *phase):
        for g in group:
            getattr(g, name)(*phase)

    for group in behind:
        step(group, "first")
    ring.append(ring_step(128))
    step(ahead, "first")
    ids_copy.wait_recv()
    set_ids(ids, 0, ids_row, ids_col)
    set_ids(ids_other, 1, ids_row, ids_col)
    step(ahead, "ring", 1)
    ring[0][0].wait_recv()
    halves = [start(block(down, 0, 0, 128), block(down, 0, 0, 128), up)]
    step(ahead, "forward", 1)
    step(behind[0], "ring", 1)
    step(behind[1], "ring", 1)
    step(ahead, "settle")
    for j in range(2):
        packed = slab[:, :, :, j * 256 : (j + 1) * 256].reshape(1152, 256)
        weights[:, j * 384 : (j + 1) * 384] = dot(packed, picker()).astype(LOW)

    def project(owner, r):
        rows = pl.ds(pl.multiple_of(owner["z"] * 256, 256), 256)
        product = (dot(n1_all[owner["z"], r * 256 : (r + 1) * 256, :], weights[...]) + bias[...]).astype(LOW)
        for j in range(2):
            for k, target in enumerate((q_s, k_s, v_s)):
                first_lane = j * 384 + k * 128
                target[2 * r + j, rows, :] = product[:, first_lane : first_lane + 128]

    loads[0].wait()
    project(at, 0)
    ring[1][1].wait_recv()
    halves.append(start(block(up, 0, 128, 128), block(up, 0, 128, 128), down))
    ring[0][1].wait_recv()
    other[2] = start(block(up, 0), block(up, 1), sibling)
    ring[1][0].wait_recv()
    other[1] = start(block(down, 0), block(down, 1), sibling)
    step(behind[0], "forward", 1)
    other[0].wait_recv()
    project(at, 1)
    step(behind[1], "forward", 1)
    step(behind[0], "ring", 2)
    project(down, 0)
    project(up, 0)
    step(behind[1], "ring", 2)
    other[1].wait_recv()
    project(down, 1)
    other[2].wait_recv()
    project(up, 1)
    for copy in halves:
        copy.wait_recv()
    other[3] = start(block(far, 0), block(far, 1), sibling)
    project(far, 0)
    other[3].wait_recv()
    project(far, 1)
    for n in range(4):
        vt_s[n] = v_s[n].T
    top_s[...] = jnp.full(top_s.shape, LOWEST, FULL)
    stores, back = [], []
    for k, hop in enumerate(STEPS + (0,)):
        b = (z + hop) % 4
        rows = pl.ds(pl.multiple_of(b * 256, 256), 256)

        @pl.loop(0, 4)
        def _(n, b=b, rows=rows):
            r = n // 2
            scores = dot_cols(k_s[n], q_s[n, rows, :]) * SCALE
            query_ids = ids_row[r, :, rows]
            scores = jnp.where(ids_col[r] == query_ids, scores, LOWEST)
            top = jnp.max(scores, axis=0, keepdims=True)
            expo = jnp.exp(scores - top)
            total = jnp.sum(expo, axis=0, keepdims=True)
            weights_low = (expo * (1.0 / total)).astype(LOW)
            out_s[n, b] = dot(vt_s[n], weights_low).T.astype(LOW)
            logsum[n, :, rows] = top + jnp.log(total)
            top_s[n] = jnp.maximum(top_s[n], jnp.where(query_ids >= 0.0, top, LOWEST))

        for n in range(4):
            r, j = n // 2, n % 2
            source = out_s.at[n, b]
            spot = (pl.ds(r * 256, 256), lanes((4 * j + z) * 128, 128))
            if hop:
                back.append(start(source, mixed.at[spot], moved(at, "z", hop)))
            else:
                copy = pltpu.make_async_copy(source, mixed.at[spot], local.at[2 + n])
                copy.start()
                stores.append(copy)
    row = lax.broadcasted_iota(jnp.int32, (8, 128), 0)
    high = [jnp.maximum(jnp.max(top_s[j]), jnp.max(top_s[2 + j])) for j in range(2)]
    peak[...] = jnp.where(row == 0, high[0], high[1])
    step(behind[0], "forward", 2)
    loads[1].wait()
    cot_copy.wait_recv()
    ct[...] = cot_rows[...].T
    n1t[...] = n1_all[...].reshape(2048, 1152).T
    n1t_copy = pltpu.make_async_copy(n1t, n1t_out, local.at[6])
    n1t_copy.start()
    step(behind[1], "forward", 2)
    step(behind[0], "settle")
    ut[...] = dot(go[...].reshape(1152, 1024), selector(72)).astype(LOW)
    dt[...] = dot(go[...].reshape(1152, 1024), selector(72 + TAIL)).astype(LOW)
    acc2[...] = jnp.zeros(acc2.shape, FULL)
    acc3[...] = jnp.zeros(acc3.shape, FULL)
    for copy in back:
        copy.wait_recv()
    for copy in stores:
        copy.wait()

    out_bias, gain, shift, down_bias = (consts[k : k + 1, :] for k in range(4))
    upper_half, lower_half = slice(0, 256), slice(256, 512)
    quarters = [slice(k * 256, (k + 1) * 256) for k in range(4)]

    def branch_part(rows):
        return dot_cols(mixed[rows, :], go[...].reshape(1152, 1024))

    out1[...] = branch_part(lower_half).astype(LOW)
    branch = start(out1, in1, sibling)
    middle = branch_part(upper_half) + tokens[...].astype(FULL) + out_bias
    branch.wait_recv()
    middle = middle + in1[...].astype(FULL)
    result[...] = middle + down_bias
    centre = middle - mean(middle)
    inverse = lax.rsqrt(mean(centre * centre) + EPSILON)
    scaled = centre * inverse
    xhat[...] = scaled
    n2[upper_half, :] = (scaled * gain + shift).astype(LOW)
    normed = start(n2.at[pl.ds(0, 256)], n2.at[pl.ds(256, 256)], sibling)
    normed.wait_recv()
    n2t[...] = n2[...].T

    def hidden_block(u, d, block_bias):
        active, slope = smooth(dot(n2[...], u) + block_bias)
        upper = (dot(cot_rows[...], d) * slope).astype(LOW)
        active = active.astype(LOW)
        acc2[...] += dot_cols(active, d)
        acc3[...] += dot_cols(upper, u)
        return active, upper

    def grad_copy(ref, out, f, first):
        cols = lanes(f * 512, 512)
        return pltpu.make_async_copy(ref.at[:, :, :, cols], out.at[:, :, :, cols], local.at[first + f])

    streams = ((ffn_a, dffn_a, 7), (ffn_b, dffn_b, 11))
    for k, (ref, out, first) in enumerate(streams):
        step(behind[k], "settle")
        for g in behind[k]:
            for copy in g.sent:
                copy.wait_send()

        @pl.loop(0, 4)
        def _(f, k=k, ref=ref, out=out, first=first):
            def piece(n):
                return lanes(f * 512 + n * 128, 128)

            def columns(n):
                return jnp.concatenate(
                    [ref[:, :, :, piece(m)].reshape(1152, 128) for m in (n, n + 2)], axis=1
                )

            hidden_cols = lanes(k * 1024 + f * 256, 256)
            active, upper = hidden_block(columns(0), columns(1), up_bias[:, hidden_cols])
            sums_hidden[:, hidden_cols] = column_sum(upper)
            for n, grad in enumerate((dot(n2t[...], upper).astype(LOW), dot(ct[...], active).astype(LOW))):
                ref[:, :, :, piece(n)] = grad[:, :128].reshape(2, 4, 144, 128)
                ref[:, :, :, piece(n + 2)] = grad[:, 128:].reshape(2, 4, 144, 128)
            grad_copy(ref, out, f, first).start()

    active, upper = hidden_block(ut[...], dt[...], up_bias[:, 2048:HIDDEN])
    sums_hidden[:, 2048:HIDDEN] = column_sum(upper)
    out3[...] = acc3[lower_half, :].astype(LOW)
    return_copy = start(out3, in3, sibling)
    out2[...] = acc2[lower_half, :].astype(LOW)
    forth = start(out2, in2, sibling)
    up_tail = dot_cols(upper, selector(72)).astype(LOW)
    down_tail = dot_cols(active, selector(72 + TAIL)).astype(LOW)
    upstream = cot_rows[upper_half, :].astype(FULL)
    return_copy.wait_recv()
    normed_grad = acc3[upper_half, :] + in3[...].astype(FULL)
    scaled = xhat[...]
    along = normed_grad * gain
    grad = upstream + inverse * (along - mean(along) - scaled * mean(along * scaled))
    middle_grad[...] = grad
    low = grad.astype(LOW)
    bg[upper_half, :] = low
    branch_grad = start(bg.at[pl.ds(0, 256)], bg.at[pl.ds(256, 256)], sibling)
    sums[0:1, :] = column_sum(low)
    sums[1:2, :] = column_sum(upstream)
    sums[2:3, :] = column_sum(normed_grad * scaled)
    sums[3:4, :] = column_sum(normed_grad)
    sums[4:8, :] = jnp.zeros((4, 1152), FULL)
    forth.wait_recv()
    result[...] += acc2[upper_half, :] + in2[...].astype(FULL)
    branch_grad.wait_recv()
    for cols in quarters:
        mixed_grad[:, cols] = dot(bg[...], go[:, :, :, cols].reshape(1152, 256)).astype(LOW)
    for cols in quarters:
        go[:, :, :, cols] = (
            (
                dot(n2t[...], up_tail[:, cols])
                + dot(ct[...], down_tail[:, cols])
                + dot_rows(bg[...], mixed[:, cols])
            )
            .astype(LOW)
            .reshape(2, 4, 144, 256)
        )
    last = pltpu.make_async_copy(go, dout, local.at[15])
    last.start()
    for ref, out, first in streams:
        for n in range(4):
            grad_copy(ref, out, n, first).wait()
    last.wait()
    n1t_copy.wait()
    for copy in sent + [copy for g in ahead for copy in g.sent]:
        copy.wait_send()


def forward(pack, n1, cot, ids, bias, tokens, consts, up_bias):
    count = 12 + 12 + 5 + 2 * 15 + 3 * 45
    grids = [(2, 4, 144, 8 * w) for w in WIDTHS[1:]]
    rows, half = (512, 1152), (256, 1152)
    return pl.pallas_call(
        forward_kernel,
        out_shape=[
            jax.ShapeDtypeStruct(half, FULL),
            jax.ShapeDtypeStruct(half, FULL),
            jax.ShapeDtypeStruct((512, 1024), LOW),
        ]
        + [jax.ShapeDtypeStruct(grid, LOW) for grid in grids]
        + [
            jax.ShapeDtypeStruct((1152, 2048), LOW),
            jax.ShapeDtypeStruct((1152, 768), LOW),
            jax.ShapeDtypeStruct((8, 128), FULL),
        ]
        + [jax.ShapeDtypeStruct((4, 1024, 128), LOW)] * 3
        + [
            jax.ShapeDtypeStruct((4, 1, 1024), FULL),
            jax.ShapeDtypeStruct((8, 128), FULL),
            jax.ShapeDtypeStruct((1, HIDDEN), FULL),
            jax.ShapeDtypeStruct((8, 1152), FULL),
        ],
        in_specs=[vmem(), anywhere(), anywhere()] + [vmem()] * 5,
        out_specs=[vmem()] * 3 + [hbm()] * 4 + [vmem()] * 9,
        scratch_shapes=[
            pltpu.VMEM((144, UNIT), FULL),
            pltpu.VMEM((144, UNIT), LOW),
            pltpu.VMEM((2, 4, 144, 512), LOW),
        ]
        + [pltpu.VMEM(grid, LOW) for grid in grids]
        + [
            pltpu.VMEM((4, 512, 1152), LOW),
            pltpu.VMEM((1152, 2048), LOW),
            pltpu.VMEM((2, 1, 1024), FULL),
            pltpu.VMEM((2, 1024, 1), FULL),
            pltpu.VMEM((4, 128, 1024), LOW),
            pltpu.VMEM((4, 4, 256, 128), LOW),
            pltpu.VMEM((4, 1, 256), FULL),
            pltpu.VMEM(rows, LOW),
            pltpu.VMEM((512, 1024), LOW),
            pltpu.VMEM((1152, 128), LOW),
            pltpu.VMEM((1152, 128), LOW),
            pltpu.VMEM(rows, LOW),
            pltpu.VMEM((1152, 512), LOW),
            pltpu.VMEM((1152, 512), LOW),
            pltpu.VMEM(rows, FULL),
            pltpu.VMEM(rows, FULL),
            pltpu.VMEM(half, FULL),
            pltpu.VMEM(rows, LOW),
        ]
        + [pltpu.VMEM(half, LOW)] * 6
        + [
            pltpu.SemaphoreType.DMA((count,)),
            pltpu.SemaphoreType.DMA((count,)),
            pltpu.SemaphoreType.DMA((16,)),
        ],
        compiler_params=pltpu.CompilerParams(
            collective_id=0, has_side_effects=True, vmem_limit_bytes=61 << 20
        ),
        name="forward_attention",
    )(pack, n1, cot, ids, bias, tokens, consts, up_bias)


def backward_kernel(
    upstream, q_s, k_s, v_s, ids, ids_other, logsum, dout, dffn_a, dffn_b, w_s, n1t, tokens,
    middle_grad, gain, sums_hidden, sums, peak, token_grad, out, totals, *rest
):
    (
        grad, g_s, n1t_s, kt_s, dk_s, dv_s, proj_grad, ids_row, ids_col, part_out, part_in,
        part_own, near, low, high, packed, dslab, unit, other, line, near_lines, send, receive, local,
    ) = rest[:24]
    buffers = list(rest[24:])
    at = place()
    z, core = at["z"], at["core"]
    sibling = moved(at, "core", 1)
    up, down, far = partners = [moved(at, "z", step) for step in STEPS]
    loads = [pltpu.make_async_copy(n1t, n1t_s, local.at[0])]
    for j in range(2):
        loads.append(
            pltpu.make_async_copy(
                upstream.at[:, lanes((4 * j + z) * 128, 128)],
                grad.at[z, :, pl.ds(j * 128, 128)],
                local.at[5 + j],
            )
        )
    for copy in loads:
        copy.start()
    greet([sibling] + [moved(at, axis, step) for axis in ALL for step in STEPS])
    copies = Copies(send, receive)
    sent = []

    def start(source, target, partner):
        copy = copies.start(source, target, partner)
        sent.append(copy)
        return copy

    started = [
        start(
            upstream.at[:, lanes((4 * j + partner["z"]) * 128, 128)],
            grad.at[z, :, pl.ds(j * 128, 128)],
            partner,
        )
        for partner in partners
        for j in range(2)
    ]
    counter = [local, 7]
    behind = [
        Scatter(copies, at, [dout, dffn_a, dffn_b], WIDTHS[1:], part, buffers, ALL, counter)
        for part in PARTS_BACK
    ]
    last = [Scatter(copies, at, [dslab], [256], part, buffers, "xy") for part in PARTS]
    for s in behind:
        s.begin(0)
    set_ids(ids, 0, ids_row, ids_col)
    set_ids(ids_other, 1, ids_row, ids_col)
    for n in range(4):
        kt_s[n] = k_s[n].T
    values = tokens[...].astype(FULL)
    centre = values - mean(values)
    inverse = lax.rsqrt(mean(centre * centre) + EPSILON)
    token_grad[...] = centre * inverse
    for copy in loads:
        copy.wait()
    for copy in started:
        copy.wait_recv()
    lane = lax.broadcasted_iota(jnp.int32, (256, 128), 1)
    for r in range(2):
        for j in range(2):
            for b in range(4):
                block = grad[b, r * 256 : (r + 1) * 256, j * 128 : (j + 1) * 128]
                g_s[2 * r + j, b * 256 : (b + 1) * 256, :] = jnp.where(
                    lane < HEAD_DIM, block.astype(FULL), 0.0
                ).astype(LOW)

    def heads_back(r):
        dk_s[...] = jnp.zeros(dk_s.shape, FULL)
        dv_s[...] = jnp.zeros(dv_s.shape, FULL)

        @pl.loop(0, 4)
        def _(b):
            rows = pl.ds(pl.multiple_of(b * 256, 256), 256)
            spot = pl.ds(pl.multiple_of(b * 512 + r * 256, 256), 256)
            allowed = ids_col[r] == ids_row[r, :, rows]
            for j in range(2):
                n = 2 * r + j
                query, upper = q_s[n, rows, :], g_s[n, rows, :]
                scores = dot_cols(k_s[n], query) * SCALE
                probs = jnp.where(allowed, jnp.exp(scores - logsum[n, :, rows]), 0.0)
                dv_s[j] += dot(probs.astype(LOW), upper)
                prob_grad = dot_cols(v_s[n], upper)
                centre = jnp.sum(probs * prob_grad, axis=0, keepdims=True)
                score_grad = (probs * (prob_grad - centre)).astype(LOW)
                proj_grad[spot, j * 384 : j * 384 + 128] = (
                    (dot(kt_s[n], score_grad) * SCALE).T.astype(LOW)
                )
                dk_s[j] += dot(score_grad, query)

        for j in range(2):
            for b in range(4):
                spot = slice(b * 512 + r * 256, b * 512 + (r + 1) * 256)
                rows = slice(b * 256, (b + 1) * 256)
                proj_grad[spot, j * 384 + 128 : j * 384 + 256] = (dk_s[j, rows, :] * SCALE).astype(LOW)
                proj_grad[spot, j * 384 + 256 : j * 384 + 384] = dv_s[j, rows, :].astype(LOW)

    def part(owner, r):
        spot = pl.ds(pl.multiple_of(owner["z"] * 512 + r * 256, 256), 256)
        return dot_cols(proj_grad[spot, :], w_s[...])

    heads_back(1)
    swapped = []
    for owner in (far, up, down, at):
        n = owner["z"]
        part_out[n] = part(owner, 1).astype(LOW)
        swapped.append(copies.start(part_out.at[n], part_in.at[n], sibling))
    for s in behind:
        s.relay(0)
    heads_back(0)

    def summed(owner, copy):
        copy.wait()
        return part(owner, 0) + part_in[owner["z"]].astype(FULL)

    half_a, half_b = pl.ds(0, 128), pl.ds(128, 128)
    part_out[far["z"]] = summed(far, swapped[0]).astype(LOW)
    arriving = [
        start(part_out.at[far["z"], half_a], near.at[half_a], up),
        start(part_out.at[far["z"], half_b], near.at[half_b], down),
    ]
    part_out[up["z"]] = summed(up, swapped[1]).astype(LOW)
    part_out[down["z"]] = summed(down, swapped[2]).astype(LOW)
    part_own[...] = summed(at, swapped[3])
    for copy in arriving:
        copy.wait_recv()
    near[0:128, :] = (near[0:128, :].astype(FULL) + part_out[up["z"], 0:128, :].astype(FULL)).astype(LOW)
    near[128:256, :] = (
        near[128:256, :].astype(FULL) + part_out[down["z"], 128:256, :].astype(FULL)
    ).astype(LOW)
    arriving = [
        start(near.at[half_a], low.at[half_a], up),
        start(part_out.at[up["z"], half_b], low.at[half_b], up),
        start(near.at[half_b], high.at[half_b], down),
        start(part_out.at[down["z"], half_a], high.at[half_a], down),
    ]
    for n in range(3):
        cols = slice(n * 256, (n + 1) * 256)
        packed[:, cols] = dot(n1t_s[...], proj_grad[:, cols]).astype(LOW)
    for j in range(2):
        dslab[:, :, :, j * 256 : (j + 1) * 256] = (
            dot_cols(packed[:, j * 384 : (j + 1) * 384], picker()).astype(LOW).reshape(2, 4, 144, 256)
        )
    for s in last:
        s.begin(0)
    projected = column_sum(proj_grad[...])
    for s in behind:
        s.finish(0)
        s.begin(1)
    for s in last:
        s.relay(0)
    for copy in arriving:
        copy.wait_recv()
    normed_grad = part_own[...] + low[...].astype(FULL) + high[...].astype(FULL)
    scaled = token_grad[...]
    along = normed_grad * gain[...]
    token_grad[...] = middle_grad[...] + inverse * (
        along - mean(along) - scaled * mean(along * scaled)
    )
    for t in range(8):
        for n in range(3):
            first = (t // 4) * 384 + n * 128
            line[0, 3 * t + n : 3 * t + n + 1, :] = jnp.where(
                z == t % 4, projected[:, first : first + 128], 0.0
            )
    row = 24
    for piece in (
        sums_hidden[...],
        sums[0:1, :],
        sums[1:2, :],
        column_sum(normed_grad * scaled),
        column_sum(normed_grad),
        sums[2:3, :],
        sums[3:4, :],
        jnp.zeros((1, 128), FULL),
    ):
        for n in range(piece.shape[1] // 128):
            line[0, row : row + 1, :] = piece[:, n * 128 : (n + 1) * 128]
            row += 1
    head = lax.broadcasted_iota(jnp.int32, (8, 128), 1) - (2 * z + core)
    line[0, 96:104, :] = jnp.where(
        head == 0, peak[0:1, 0:1], jnp.where(head == 8, peak[1:2, 0:1], LOWEST)
    )

    def send_line(phase):
        return [
            start(line.at[phase], near_lines.at[phase, n], moved(at, ALL[phase], step))
            for n, step in enumerate(STEPS)
        ]

    def add_line(phase, begun):
        for copy in begun:
            copy.wait_recv()
        parts = [line[phase]] + [near_lines[phase, n] for n in range(3)]
        line[phase + 1, 0:96, :] = (parts[0][:96] + parts[1][:96]) + (parts[2][:96] + parts[3][:96])
        line[phase + 1, 96:104, :] = jnp.maximum(
            jnp.maximum(parts[0][96:], parts[1][96:]), jnp.maximum(parts[2][96:], parts[3][96:])
        )

    arriving = send_line(0)
    for s in behind:
        s.relay(1)
    add_line(0, arriving)
    arriving = send_line(1)
    for s in behind:
        s.finish(1)
        s.last()
    for s in last:
        s.finish(0)
        s.last()
    add_line(1, arriving)
    arriving = send_line(2)
    for s in behind:
        s.result(unit, STARTS[1:])
    for s in last:
        s.result(unit, [0])
    mine = pl.ds(pl.multiple_of(core * 72, 8), 72)
    theirs = pl.ds(pl.multiple_of((1 - core) * 72, 8), 72)
    late = start(unit.at[theirs], other, sibling)
    add_line(2, arriving)
    line_copy = start(line.at[3], totals.at[core], sibling)
    totals[core] = line[3]
    out[core] = unit[mine, :]
    late.wait_recv()
    out[1 - core] = other[...]
    line_copy.wait_recv()
    for copy in sent + [copy for s in behind + last for copy in s.sent]:
        copy.wait_send()


def backward(upstream, heads, ids, ids_other, logsum, grids, weights, n1t, tokens, middle_grad, gain, sums_hidden, sums, peak):
    count = 6 + 4 + 6 + 9 + 2 + 3 * 45 + 2 * 15
    shapes = []
    for part in PARTS_BACK:
        shapes += Scatter.shapes(WIDTHS[1:], part, True)
    for part in PARTS:
        shapes += Scatter.shapes([256], part, False)
    half = (256, 1152)
    return pl.pallas_call(
        backward_kernel,
        out_shape=[
            jax.ShapeDtypeStruct(half, FULL),
            jax.ShapeDtypeStruct((2, 72, UNIT), FULL),
            jax.ShapeDtypeStruct((2, 104, 128), FULL),
        ],
        in_specs=[anywhere()] + [vmem()] * 6 + [anywhere()] * 3 + [vmem(), anywhere()] + [vmem()] * 6,
        out_specs=[vmem()] * 3,
        scratch_shapes=[
            pltpu.VMEM((4, 512, 256), LOW),
            pltpu.VMEM((4, 1024, 128), LOW),
            pltpu.VMEM((1152, 2048), LOW),
            pltpu.VMEM((4, 128, 1024), LOW),
            pltpu.VMEM((2, 1024, 128), FULL),
            pltpu.VMEM((2, 1024, 128), FULL),
            pltpu.VMEM((2048, 768), LOW),
            pltpu.VMEM((2, 1, 1024), FULL),
            pltpu.VMEM((2, 1024, 1), FULL),
            pltpu.VMEM((4,) + half, LOW),
            pltpu.VMEM((4,) + half, LOW),
            pltpu.VMEM(half, FULL),
            pltpu.VMEM(half, LOW),
            pltpu.VMEM(half, LOW),
            pltpu.VMEM(half, LOW),
            pltpu.VMEM((1152, 768), LOW),
            pltpu.VMEM((2, 4, 144, 512), LOW),
            pltpu.VMEM((144, UNIT), FULL),
            pltpu.VMEM((72, UNIT), FULL),
            pltpu.VMEM((4, 104, 128), FULL),
            pltpu.VMEM((3, 3, 104, 128), FULL),
            pltpu.SemaphoreType.DMA((count,)),
            pltpu.SemaphoreType.DMA((count,)),
            pltpu.SemaphoreType.DMA((64,)),
        ]
        + shapes,
        compiler_params=pltpu.CompilerParams(
            collective_id=1, has_side_effects=True, vmem_limit_bytes=61 << 20
        ),
        name="backward_attention",
    )(
        upstream, *heads, ids, ids_other, logsum, *grids, weights, n1t, tokens, middle_grad, gain, sums_hidden,
        sums, peak,
    )


def normalize(values, gain, shift):
    centre = values - jnp.mean(values, axis=-1, keepdims=True)
    inverse = lax.rsqrt(jnp.mean(centre * centre, axis=-1, keepdims=True) + EPSILON)
    return centre * inverse * gain + shift


def per_device(
    tokens,
    picture,
    cotangent,
    gain_one,
    shift_one,
    query_weight,
    query_bias,
    key_weight,
    value_weight,
    value_bias,
    out_weight,
    out_bias,
    gain_two,
    shift_two,
    up_weight,
    up_bias,
    down_weight,
    down_bias,
):
    width = tokens.shape[1]
    t = lax.axis_index("tensor")
    core = lax.axis_index("dp") % 2
    gain_first = gain_one.astype(FULL)

    out_t = out_weight.astype(FULL).T
    down_t = down_weight.astype(FULL).T
    up = up_weight.astype(FULL)
    halves = []
    for h in range(2):
        cols = slice(h * 72, (h + 1) * 72)
        first = h * (MAIN + TAIL)
        main, rest = slice(first, first + 128), slice(first + 128, first + MAIN)
        tail = slice(first + MAIN, first + MAIN + TAIL)
        halves.append(
            jnp.concatenate(
                [
                    query_weight[:, cols].astype(FULL),
                    key_weight[:, cols].astype(FULL),
                    value_weight[:, cols].astype(FULL),
                    jnp.zeros((72, 40), FULL),
                    out_t[:, cols],
                    up[:, tail],
                    down_t[:, tail],
                    jnp.zeros((72, 30), FULL),
                    up[:, main],
                    down_t[:, main],
                    up[:, rest],
                    down_t[:, rest],
                ],
                axis=1,
            )
        )
    pack = jnp.stack(halves)

    inputs = tokens.astype(FULL)
    normed = normalize(inputs, gain_first, shift_one.astype(FULL))
    normed_mine = normed.astype(LOW)
    half = lax.dynamic_slice_in_dim(picture, (t // 4) * 1024, 1024)
    ids = jnp.where(half >= 0, half, -1 - jnp.arange(1024, dtype=jnp.int32)).astype(FULL)
    def halves_of(vector, size):
        return lax.dynamic_index_in_dim(
            vector.astype(FULL).reshape(8, 2, size), core, axis=1, keepdims=False
        )

    query_b, value_b = halves_of(query_bias, 72), halves_of(value_bias, 72)
    head_bias = jnp.pad(
        jnp.stack([query_b, jnp.zeros((8, 72), FULL), value_b], axis=1), ((0, 0), (0, 0), (0, 56))
    ).reshape(2, 4, 384)
    proj_bias = lax.dynamic_index_in_dim(head_bias, t % 4, axis=1, keepdims=False).reshape(1, 768)
    up_b = halves_of(up_bias, MAIN + TAIL)
    hidden_bias = jnp.concatenate(
        [
            up_b[:, :128].reshape(1024),
            up_b[:, 128:MAIN].reshape(1024),
            up_b[:, MAIN:].reshape(8 * TAIL),
            jnp.zeros((24,), FULL),
        ]
    ).reshape(1, HIDDEN)

    consts = jnp.concatenate(
        [
            jnp.stack([out_bias, gain_two, shift_two, down_bias]).astype(FULL),
            jnp.zeros((4, width), FULL),
        ]
    )
    result, middle_grad, mixed_grad, *rest = forward(
        pack, normed_mine, cotangent, ids.reshape(8, 128), proj_bias, tokens, consts, hidden_bias
    )
    grids, (rows_one_t, weights, ids_other) = rest[:3], rest[3:6]
    heads, (logsum, peak, sums_hidden, sums) = rest[6:9], rest[9:]
    input_grad, grads, totals = backward(
        mixed_grad,
        heads,
        ids.reshape(8, 128),
        ids_other,
        logsum,
        grids,
        weights,
        rows_one_t,
        tokens,
        middle_grad,
        gain_first.reshape(1, width),
        sums_hidden,
        sums,
        peak,
    )

    def side(first, size):
        return jnp.concatenate([grads[0, :, first : first + size], grads[1, :, first : first + size]], axis=1)

    def hidden_side(main, tail):
        return jnp.concatenate(
            [
                grads[0, :, main : main + 128],
                grads[0, :, main + 256 : main + 384],
                grads[0, :, tail : tail + TAIL],
                grads[1, :, main : main + 128],
                grads[1, :, main + 256 : main + 384],
                grads[1, :, tail : tail + TAIL],
            ],
            axis=1,
        )

    query_w, key_w, value_w = side(0, 72), side(72, 72), side(144, 72)
    out_w = side(256, 72).T
    up_w = hidden_side(384, 256 + 72)
    down_w = hidden_side(512, 256 + 72 + TAIL).T
    heads = totals[:, :24].reshape(2, 8, 3, 128)[..., :HEAD_DIM]
    query_b_grad = heads[:, :, 0].transpose(1, 0, 2).reshape(width)
    value_b_grad = heads[:, :, 2].transpose(1, 0, 2).reshape(width)
    flat = totals[:, 24:95].reshape(2, 71 * 128)
    up_b_grad = (
        jnp.concatenate(
            [
                flat[:, :1024].reshape(2, 8, 128),
                flat[:, 1024:2048].reshape(2, 8, 128),
                flat[:, 2048 : 2048 + 8 * TAIL].reshape(2, 8, TAIL),
            ],
            axis=2,
        )
        .transpose(1, 0, 2)
        .reshape(-1)
    )
    summed = (flat[0] + flat[1])[HIDDEN:].reshape(6, width)
    high = jnp.maximum(totals[0, 96, :16], totals[1, 96, :16])
    factor = jnp.sqrt(CLIP_LIMIT / jnp.maximum(high, CLIP_LIMIT))
    column_factor = jnp.repeat(lax.dynamic_slice_in_dim(factor, 2 * t, 2), HEAD_DIM)
    clipped_query = query_weight.astype(FULL) * column_factor[None, :]
    clipped_key = key_weight.astype(FULL) * column_factor[None, :]
    return (
        result,
        input_grad,
        query_w,
        key_w,
        value_w,
        out_w,
        up_w,
        down_w,
        query_b_grad,
        value_b_grad,
        up_b_grad,
        summed[0],
        summed[1],
        summed[2],
        summed[3],
        summed[4],
        summed[5],
        clipped_query,
        clipped_key,
    )


def solution(mesh):
    in_specs = (
        P(("dp", "tensor"), None),
        P("dp"),
        P(("dp", "tensor"), None),
        P(),
        P(),
        P("dp", "tensor"),
        P(),
        P("dp", "tensor"),
        P("dp", "tensor"),
        P(),
        P("tensor", "dp"),
        P(),
        P(),
        P(),
        P("dp", "tensor"),
        P(),
        P("tensor", "dp"),
        P(),
    )
    out_specs = (
        P(("dp", "tensor"), None),
        P(("dp", "tensor"), None),
        P("dp", "tensor"),
        P("dp", "tensor"),
        P("dp", "tensor"),
        P("tensor", "dp"),
        P("dp", "tensor"),
        P("tensor", "dp"),
        P(),
        P(),
        P(),
        P(),
        P(),
        P(),
        P(),
        P(),
        P(),
        P("dp", "tensor"),
        P("dp", "tensor"),
    )
    return jax.shard_map(
        per_device, mesh=mesh, in_specs=in_specs, out_specs=out_specs, check_vma=False
    )
```

```python
import functools

import jax
import jax.numpy as jnp
import numpy as np
from jax import lax
from jax.experimental import pallas as pl
from jax.experimental.pallas import tpu as pltpu
from jax.sharding import PartitionSpec as P

HEAD_DIM = 72
EPSILON = 1e-06
CLIP_LIMIT = 2.0
LOWEST = -1e30
SCALE = HEAD_DIM**-0.5

MESH = pl.DeviceIdType.MESH
LOW = jnp.bfloat16
FULL = jnp.float32

STARTS = (0, 256, 384, 640)
WIDTHS = (256, 128, 256, 256)
STREAMS = ((0, 1), (2,))
UNIT = 896
MAIN = 256
TAIL = 13
HIDDEN = 8 * MAIN + 128
PARTS = ((0, 80, "xy"), (80, 64, "yx"))
PARTS_BEHIND = (
    ((0, 64, "zyx"), (64, 48, "zxy"), (112, 32, "yxz")),
    ((0, 48, "zyx"), (48, 64, "zxy"), (112, 32, "yxz")),
)
PARTS_BACK = ((0, 64, "zyx"), (64, 64, "zxy"), (128, 16, "yxz"))
STEPS = (1, 3, 2)
ALL = "xyz"


def place():
    d, t = lax.axis_index("dp"), lax.axis_index("tensor")
    return {"x": (d // 2) % 4, "y": (t // 4) * 2 + d // 8, "z": t % 4, "core": d % 2}


def device(at):
    return ((at["y"] % 2) * 8 + at["x"] * 2 + at["core"], (at["y"] // 2) * 4 + at["z"])


def moved(at, axis, step):
    other = dict(at)
    other[axis] = 1 - at["core"] if axis == "core" else (at[axis] + step) % 4
    return other


def greet(partners):
    barrier = pltpu.get_barrier_semaphore()
    for partner in partners:
        pl.semaphore_signal(barrier, inc=1, device_id=device(partner), device_id_type=MESH)
    pl.semaphore_wait(barrier, len(partners))


class Copies:
    def __init__(self, send, receive):
        self.send, self.receive, self.used = send, receive, 0

    def start(self, source, target, partner):
        copy = pltpu.make_async_remote_copy(
            src_ref=source,
            dst_ref=target,
            send_sem=self.send.at[self.used],
            recv_sem=self.receive.at[self.used],
            device_id=device(partner),
            device_id_type=MESH,
        )
        self.used += 1
        copy.start()
        return copy


def lanes(first, size):
    return pl.ds(first if isinstance(first, int) else pl.multiple_of(first, 128), size)


def spots(held, have, at, width, rows, half=None):
    zs, ys = (4 if "z" in held else 1), at["y"] if "y" in held else 0
    x_at = pl.ds(0, 4) if "x" in have else pl.ds(at["x"] if "x" in held else 0, 1)
    y_at = pl.ds(0, 2) if "y" in have else pl.ds(ys % 2, 1)
    z = at["z"] if "z" in held else 0
    if "y" in have and "z" in have:
        ranges = [(0, 8 * width)]
    elif "y" in have:
        ranges = [((h * zs + z) * width, width) for h in (0, 1)]
    elif "z" in have:
        ranges = [((ys // 2) * zs * width, 4 * width)]
    else:
        ranges = [(((ys // 2) * zs + z) * width, width)]
    if half is not None:
        if len(ranges) == 2:
            ranges = [ranges[half]]
        elif "x" in have:
            x_at = pl.ds(2 * half, 2)
        elif "y" in have:
            y_at = pl.ds(half, 1)
        else:
            ((first, size),) = ranges
            ranges = [(first + half * (size // 2), size // 2)]
    return [(y_at, x_at, pl.ds(*rows), lanes(*r)) for r in ranges]


def rect_shape(have, width, rows):
    ys, xs, zs = 2 if "y" in have else 1, 4 if "x" in have else 1, 4 if "z" in have else 1
    return (ys, xs, rows, ys * zs * width)


class Gather:
    def __init__(self, copies, at, grids, widths, part, held=ALL):
        self.copies, self.at, self.grids, self.widths = copies, at, grids, widths
        self.rows, self.order, self.held = part[:2], part[2], held
        self.arriving, self.sent = [], []

    def views(self, grid, width, have, at, half=None):
        return [grid.at[spot] for spot in spots(self.held, have, at, width, self.rows, half)]

    def send(self, have, owner, partner, half=None):
        started = []
        for grid, width in zip(self.grids, self.widths):
            for view in self.views(grid, width, have, owner, half):
                started.append(self.copies.start(view, view, partner))
        self.sent += started
        return started

    def settle(self):
        for copy in self.arriving:
            copy.wait_recv()
        self.arriving = []

    def first(self):
        for step in STEPS:
            self.arriving += self.send("", self.at, moved(self.at, self.order[0], step))

    def ring(self, phase):
        self.settle()
        axis, have = self.order[phase], self.order[:phase]
        self.after = self.send(have, self.at, moved(self.at, axis, 1))
        self.before = self.send(have, self.at, moved(self.at, axis, 3))

    def forward(self, phase):
        axis, have = self.order[phase], self.order[:phase]
        up, down = moved(self.at, axis, 1), moved(self.at, axis, 3)
        for copy in self.after:
            copy.wait_recv()
        self.arriving += self.send(have, down, up, 0)
        for copy in self.before:
            copy.wait_recv()
        self.arriving += self.send(have, up, down, 1)


def add_into(target, terms, shape):
    @pl.loop(0, shape[0] * shape[1] * (shape[2] // 16))
    def _(n):
        block = n // (shape[2] // 16)
        spot = (
            block // shape[1],
            block % shape[1],
            pl.ds(pl.multiple_of((n % (shape[2] // 16)) * 16, 16), 16),
            slice(None),
        )
        total = terms[0][spot].astype(FULL)
        for term in terms[1:]:
            total = total + term[spot].astype(FULL)
        target[spot] = total.astype(target.dtype)


def half_shape(have, shape):
    ys, xs, rows, cols = shape
    if "y" in have and "z" not in have:
        return (ys, xs, rows, cols // 2)
    if "x" in have:
        return (ys, 2, rows, cols)
    if "y" in have:
        return (1, xs, rows, cols)
    return (ys, xs, rows, cols // 2)


class Scatter:
    @staticmethod
    def shapes(widths, part, loaded):
        _, rows, order = part
        shapes = []
        for phase in range(len(order) - 1):
            have = order[: len(order) - 1 - phase]
            for _ in range(5 if loaded and phase == 0 else 4):
                shapes += [pltpu.VMEM(rect_shape(have, w, rows), LOW) for w in widths]
        shapes += [pltpu.VMEM((3, 1, 1, rows, w), LOW) for w in widths]
        return shapes

    def __init__(self, copies, at, grids, widths, part, buffers, held=ALL, local=None):
        self.copies, self.at, self.grids, self.widths = copies, at, grids, widths
        self.rows, self.order = part[:2], part[2]
        self.rings = len(self.order) - 1
        self.held = [held] + [self.order[: self.rings - phase] for phase in range(self.rings)]
        self.local = local
        self.sent = []

        def take():
            taken, buffers[:] = buffers[: len(widths)], buffers[len(widths) :]
            return taken

        self.near, self.low, self.high, self.own = [], [], [], []
        for phase in range(self.rings):
            for group in (self.near, self.low, self.high, self.own):
                group.append(take())
            if phase == 0 and local:
                self.mix = [take()]
        self.direct = take()

    def have(self, phase):
        return self.order[: self.rings - phase]

    def source(self, phase, a, at, half=None):
        grid = self.grids[a] if phase == 0 else self.own[phase - 1][a]
        rows = self.rows if phase == 0 else (0, self.rows[1])
        found = spots(self.held[phase], self.have(phase), at, self.widths[a], rows, half)
        return [grid.at[spot] for spot in found]

    def target(self, phase, buffer, a, half=None):
        have = self.have(phase)
        found = spots(have, have, self.at, self.widths[a], (0, self.rows[1]), half)
        return [buffer[phase][a].at[spot] for spot in found]

    def push(self, sources, targets, partner):
        started = [self.copies.start(s, t, partner) for s, t in zip(sources, targets)]
        self.sent += started
        return started

    def begin(self, phase):
        axis = self.order[self.rings - phase]
        up, down, far = (moved(self.at, axis, step) for step in STEPS)
        self.arriving, self.loading = [], []
        for a in range(len(self.grids)):
            for half, partner in ((0, up), (1, down)):
                self.arriving += self.push(
                    self.source(phase, a, far, half),
                    self.target(phase, self.near, a, half),
                    partner,
                )
        if phase == 0 and self.local:
            for a in range(len(self.grids)):
                pairs = list(
                    zip(
                        self.source(0, a, up, 0) + self.source(0, a, down, 1),
                        self.target(0, self.mix, a, 0) + self.target(0, self.mix, a, 1),
                    )
                )
                pairs += list(zip(self.source(0, a, self.at), self.target(0, self.own, a)))
                for view, target in pairs:
                    copy = pltpu.make_async_copy(view, target, self.local[0].at[self.local[1]])
                    self.local[1] += 1
                    copy.start()
                    self.loading.append(copy)

    def relay(self, phase):
        axis, have = self.order[self.rings - phase], self.have(phase)
        up, down, _ = (moved(self.at, axis, step) for step in STEPS)
        for copy in self.loading:
            copy.wait()
        for copy in self.arriving:
            copy.wait_recv()
        self.arriving = []
        for a in range(len(self.grids)):
            shape = half_shape(have, rect_shape(have, self.widths[a], self.rows[1]))
            for half, partner in ((0, up), (1, down)):
                (near,) = self.target(phase, self.near, a, half)
                if phase == 0 and self.local:
                    (view,) = self.target(phase, self.mix, a, half)
                else:
                    (view,) = self.source(phase, a, partner, half)
                add_into(near, [view, near], shape)
                buffer = self.low if half == 0 else self.high
                self.arriving += self.push(
                    [near] + self.source(phase, a, partner, 1 - half),
                    self.target(phase, buffer, a, half) + self.target(phase, buffer, a, 1 - half),
                    partner,
                )

    def finish(self, phase):
        have = self.have(phase)
        for copy in self.arriving:
            copy.wait_recv()
        for a in range(len(self.grids)):
            for low, high, own, source in zip(
                self.target(phase, self.low, a),
                self.target(phase, self.high, a),
                self.target(phase, self.own, a),
                self.source(phase, a, self.at),
            ):
                shape = rect_shape(have, self.widths[a], self.rows[1])
                if "y" in have and "z" not in have:
                    shape = half_shape(have, shape)
                add_into(own, [own if phase == 0 and self.local else source, low, high], shape)

    def last(self):
        self.arriving = []
        for k, step in enumerate(STEPS):
            partner = moved(self.at, self.order[0], step)
            for a in range(len(self.grids)):
                self.arriving += self.push(
                    self.source(self.rings, a, partner), [self.direct[a].at[k]], partner
                )

    def result(self, out, starts):
        for copy in self.arriving:
            copy.wait_recv()
        for a, start in enumerate(starts):
            (mine,) = self.source(self.rings, a, self.at)
            total = mine[0, 0].astype(FULL)
            for k in range(3):
                total = total + self.direct[a][k, 0, 0].astype(FULL)
            out[pl.ds(*self.rows), start : start + self.widths[a]] = total


def hbm():
    return pl.BlockSpec(memory_space=pltpu.HBM)


def anywhere():
    return pl.BlockSpec(memory_space=pl.ANY)


def vmem():
    return pl.BlockSpec(memory_space=pltpu.VMEM)


def picker():
    row = lax.broadcasted_iota(jnp.int32, (256, 384), 0)
    lane = lax.broadcasted_iota(jnp.int32, (256, 384), 1)
    hit = ((lane & 127) < HEAD_DIM) & (row == (lane >> 7) * HEAD_DIM + (lane & 127))
    return jnp.where(hit, 1.0, 0.0).astype(LOW)


def dot(left, right):
    return jnp.dot(left, right, preferred_element_type=FULL)


def dot_rows(left, right):
    return lax.dot_general(left, right, (((0,), (0,)), ((), ())), preferred_element_type=FULL)


def dot_cols(left, right):
    return lax.dot_general(left, right, (((1,), (1,)), ((), ())), preferred_element_type=FULL)


def set_ids(ids, r, ids_row, ids_col):
    eye = lax.broadcasted_iota(jnp.int32, (128, 128), 0) == lax.broadcasted_iota(
        jnp.int32, (128, 128), 1
    )
    for k in range(8):
        piece = ids[8 * r + k : 8 * r + k + 1, :]
        ids_row[r, :, k * 128 : (k + 1) * 128] = piece
        ids_col[r, k * 128 : (k + 1) * 128, :] = jnp.sum(
            jnp.where(eye, piece, 0.0), axis=1, keepdims=True
        )


def selector(offset):
    row = lax.broadcasted_iota(jnp.int32, (1024, 128), 0)
    lane = lax.broadcasted_iota(jnp.int32, (1024, 128), 1)
    inner = (row & 127) - offset
    hit = (inner >= 0) & (inner < TAIL) & (lane == (row >> 7) * TAIL + inner)
    return jnp.where(hit, 1.0, 0.0).astype(LOW)


def smooth(inner):
    root = 0.7978845608028654
    square = inner * inner
    wave = jnp.tanh(root * inner * (1.0 + 0.044715 * square))
    up = 0.5 * (1.0 + wave)
    slope = up + 0.5 * inner * (1.0 - wave * wave) * root * (1.0 + 3 * 0.044715 * square)
    return inner * up, slope


def mean(values):
    return jnp.sum(values, axis=1, keepdims=True) * (1.0 / values.shape[1])


def column_sum(values):
    return jnp.sum(values.astype(FULL), axis=0, keepdims=True)


def shifted(values, amount, width):
    if values.shape[1] < width:
        pad = jnp.zeros((values.shape[0], width - values.shape[1]), FULL)
        values = jnp.concatenate([values, pad], axis=1)
    return pltpu.roll(values, amount, 1) if amount else values


def widened(values, width):
    pad = jnp.zeros((values.shape[0], width - values.shape[1]), FULL)
    return jnp.concatenate([values.astype(FULL), pad], axis=1)


def pack_half(half, query, key, value, out_t, up, down_t, pack):
    lane = lax.broadcasted_iota(jnp.int32, (72, 256), 1)
    total = jnp.zeros((72, 256), FULL)
    for k, weight in enumerate((query, key, value)):
        spot = HEAD_DIM * k
        block = pltpu.roll(weight, (spot - HEAD_DIM * half) % 256, 1)
        total = jnp.where((lane >= spot) & (lane < spot + HEAD_DIM), block, total)
    pack[half, :, 0:256] = total
    first = half * (MAIN + TAIL)
    lane = lax.broadcasted_iota(jnp.int32, (72, 128), 1)
    total = jnp.where(lane < HEAD_DIM, pltpu.roll(out_t, (-HEAD_DIM * half) % 256, 1)[:, :128], 0.0)
    for k, weight in enumerate((up, down_t)):
        spot = HEAD_DIM + TAIL * k
        block = pltpu.roll(weight, (spot - first - MAIN) % 640, 1)[:, :128]
        total = jnp.where((lane >= spot) & (lane < spot + TAIL), block, total)
        block = pltpu.roll(weight, (-first) % 640, 1) if half else weight
        pack[half, :, 384 + 128 * k : 512 + 128 * k] = block[:, :128]
        pack[half, :, 640 + 128 * k : 768 + 128 * k] = block[:, 128:256]
    pack[half, :, 256:384] = total


def set_biases(core, z, consts, up_bias, hidden_bias):
    lane = lax.broadcasted_iota(jnp.int32, (1, 128), 1)
    pieces = []
    for j in range(2):
        for k in (6, None, 7):
            total = jnp.zeros((1, 128), FULL)
            if k is not None:
                for head in range(16):
                    block = shifted(consts[k : k + 1, :], (-HEAD_DIM * head) % 1152, 1152)[:, :128]
                    total = jnp.where(head == 8 * j + 2 * z + core, block, total)
            pieces.append(jnp.where(lane < HEAD_DIM, total, 0.0))
    line = jnp.concatenate([up_bias[k : k + 1, :] for k in range(34)], axis=1)
    line = jnp.where(core == 0, line, pltpu.roll(line, 34 * 128 - MAIN - TAIL, 1))
    tails = jnp.zeros((1, 128), FULL)
    for t in range(8):
        row = shifted(line, (-2 * (MAIN + TAIL) * t) % (34 * 128), 34 * 128)
        hidden_bias[:, t * 128 : (t + 1) * 128] = row[:, 0:128]
        hidden_bias[:, 1024 + t * 128 : 1152 + t * 128] = row[:, 128:256]
        tail = shifted(row[:, 256:384], TAIL * t, 128)
        tails = jnp.where((lane >= TAIL * t) & (lane < TAIL * (t + 1)), tail, tails)
    hidden_bias[:, 2048:HIDDEN] = tails
    return jnp.concatenate(pieces, axis=1)


def forward_kernel(
    query, key, value, out_weight, up_weight, down_weight_t, consts, up_bias, picture, cot, tokens,
    result_out, middle_grad_out, dout, dffn_a, dffn_b, n1t_out, weights_out, q_out, k_out, v_out, heads_grad, both_ids,
    logsum, peak, sums_hidden, sums,
    both, unit, slab, go, ffn_a, ffn_b, n1_all, ids_row, ids_col, vt_s, out_s, top_s, cot_rows, mixed,
    ut, dt, n2, n2t, ct, acc2, acc3, xhat, bg, out1, out2, in1, in2, in3, ids, hidden_bias, pack, q_s, k_s, v_s,
    weights, result, middle_grad, mixed_grad, send, receive, local,
):
    at = place()
    core, z = at["core"], at["z"]
    sibling = moved(at, "core", 1)
    up, down, far = (moved(at, "z", step) for step in STEPS)
    grids = (go, ffn_a, ffn_b)
    cot_own = pltpu.make_async_copy(cot, cot_rows.at[pl.ds(0, 256)], local.at[1])
    cot_own.start()
    wide = [widened(w[...], 256) for w in (query, key, value)]
    wide.append(widened(out_weight[...].astype(FULL).T, 256))
    wide += [widened(w[...], 640) for w in (up_weight, down_weight_t)]
    for half in range(2):
        pack_half(half, *wide, pack)
    greet([sibling] + [moved(at, axis, step) for axis in ALL for step in STEPS])
    copies = Copies(send, receive)
    sent = []

    def start(source, target, partner):
        copy = copies.start(source, target, partner)
        sent.append(copy)
        return copy

    mine = pl.ds(pl.multiple_of(core * 72, 8), 72)
    first_copy = start(pack.at[1 - core], both.at[mine], sibling)
    half_row = pl.ds(pl.multiple_of((at["y"] // 2) * 8, 8), 8)
    numbers = picture[half_row, :]
    slot = lax.broadcasted_iota(jnp.int32, (8, 128), 0) * 128 + lax.broadcasted_iota(jnp.int32, (8, 128), 1)
    ids[...] = jnp.where(numbers >= 0, numbers, -1 - slot).astype(FULL)
    ids_copy = start(ids, both_ids.at[pl.ds(8, 8)], sibling)
    both_ids[0:8, :] = ids[...]
    out_bias, gain, shift, down_bias, gain_first, shift_first = (consts[k : k + 1, :] for k in range(6))

    def block(owner, r, first=0, size=256):
        return n1_all.at[owner["z"], pl.ds(r * 256 + first, size)]

    def ring_step(first):
        return [
            start(block(at, 0, first, 128), block(at, 0, first, 128), partner) for partner in (up, down)
        ]

    both[mine, :] = pack[core]
    values = tokens[...].astype(FULL)
    centre = values - mean(values)
    inverse = lax.rsqrt(mean(centre * centre) + EPSILON)
    n1_all[z, 0:256, :] = (centre * inverse * gain_first + shift_first).astype(LOW)
    ring = [ring_step(0)]
    other = {0: start(block(at, 0), block(at, 1), sibling)}
    cot_copy = start(cot, cot_rows.at[pl.ds(256, 256)], sibling)
    first_copy.wait_recv()
    unit[...] = both[...].astype(LOW)
    tensor = (at["y"] // 2) * 4 + z
    slab[at["y"] % 2, at["x"], :, lanes((at["y"] // 2) * 256, 256)] = unit[:, 0:256]
    for grid, first, width in zip(grids, STARTS[1:], WIDTHS[1:]):
        grid[at["y"] % 2, at["x"], :, lanes(tensor * width, width)] = unit[:, first : first + width]
    ahead = [Gather(copies, at, [slab], [256], part, "xy") for part in PARTS]
    behind = [
        [
            Gather(copies, at, [grids[n] for n in names], [WIDTHS[n + 1] for n in names], part)
            for part in parts
        ]
        for names, parts in zip(STREAMS, PARTS_BEHIND)
    ]

    def step(group, name, *phase):
        for g in group:
            getattr(g, name)(*phase)

    for group in behind:
        step(group, "first")
    ring.append(ring_step(128))
    step(ahead, "first")
    ids_copy.wait_recv()
    set_ids(ids, 0, ids_row, ids_col)
    set_ids(both_ids, 1, ids_row, ids_col)
    step(ahead, "ring", 1)
    bias = set_biases(core, z, consts, up_bias, hidden_bias)
    ring[0][0].wait_recv()
    halves = [start(block(down, 0, 0, 128), block(down, 0, 0, 128), up)]
    step(ahead, "forward", 1)
    step(behind[0], "ring", 1)
    step(behind[1], "ring", 1)
    step(ahead, "settle")
    for j in range(2):
        packed = slab[:, :, :, j * 256 : (j + 1) * 256].reshape(1152, 256)
        weights[:, j * 384 : (j + 1) * 384] = dot(packed, picker()).astype(LOW)

    def project(owner, r):
        rows = pl.ds(pl.multiple_of(owner["z"] * 256, 256), 256)
        product = (dot(n1_all[owner["z"], r * 256 : (r + 1) * 256, :], weights[...]) + bias).astype(LOW)
        for j in range(2):
            for k, target in enumerate((q_s, k_s, v_s)):
                first_lane = j * 384 + k * 128
                target[2 * r + j, rows, :] = product[:, first_lane : first_lane + 128]

    project(at, 0)
    ring[1][1].wait_recv()
    halves.append(start(block(up, 0, 128, 128), block(up, 0, 128, 128), down))
    ring[0][1].wait_recv()
    other[2] = start(block(up, 0), block(up, 1), sibling)
    ring[1][0].wait_recv()
    other[1] = start(block(down, 0), block(down, 1), sibling)
    step(behind[0], "forward", 1)
    other[0].wait_recv()
    project(at, 1)
    step(behind[1], "forward", 1)
    step(behind[0], "ring", 2)
    project(down, 0)
    project(up, 0)
    step(behind[1], "ring", 2)
    other[1].wait_recv()
    project(down, 1)
    other[2].wait_recv()
    project(up, 1)
    for copy in halves:
        copy.wait_recv()
    other[3] = start(block(far, 0), block(far, 1), sibling)
    project(far, 0)
    other[3].wait_recv()
    project(far, 1)
    stores = [
        pltpu.make_async_copy(source, target, local.at[16 + k])
        for k, (source, target) in enumerate(
            ((q_s, q_out), (k_s, k_out), (v_s, v_out), (weights, weights_out))
        )
    ]
    for copy in stores:
        copy.start()
    for n in range(4):
        vt_s[n] = v_s[n].T
    top_s[...] = jnp.full(top_s.shape, LOWEST, FULL)
    back = []
    for k, hop in enumerate(STEPS + (0,)):
        b = (z + hop) % 4
        rows = pl.ds(pl.multiple_of(b * 256, 256), 256)

        @pl.loop(0, 4)
        def _(n, b=b, rows=rows):
            r = n // 2
            scores = dot_cols(k_s[n], q_s[n, rows, :]) * SCALE
            query_ids = ids_row[r, :, rows]
            scores = jnp.where(ids_col[r] == query_ids, scores, LOWEST)
            top = jnp.max(scores, axis=0, keepdims=True)
            expo = jnp.exp(scores - top)
            total = jnp.sum(expo, axis=0, keepdims=True)
            weights_low = (expo * (1.0 / total)).astype(LOW)
            out_s[n, b] = dot(vt_s[n], weights_low).T.astype(LOW)
            logsum[n, :, rows] = top + jnp.log(total)
            top_s[n] = jnp.maximum(top_s[n], jnp.where(query_ids >= 0.0, top, LOWEST))

        for n in range(4):
            r, j = n // 2, n % 2
            source = out_s.at[n, b]
            spot = (pl.ds(r * 256, 256), lanes((4 * j + z) * 128, 128))
            if hop:
                back.append(start(source, mixed.at[spot], moved(at, "z", hop)))
            else:
                copy = pltpu.make_async_copy(source, mixed.at[spot], local.at[2 + n])
                copy.start()
                stores.append(copy)
    row = lax.broadcasted_iota(jnp.int32, (8, 128), 0)
    high = [jnp.maximum(jnp.max(top_s[j]), jnp.max(top_s[2 + j])) for j in range(2)]
    peak[...] = jnp.where(row == 0, high[0], high[1])
    step(behind[0], "forward", 2)
    cot_own.wait()
    cot_copy.wait_recv()
    turned = []
    for k in range(4):
        if k >= 2:
            turned[k - 2].wait()
        buffer = (n2t, ct)[k % 2]
        buffer[...] = n1_all[k].T
        copy = pltpu.make_async_copy(buffer, n1t_out.at[:, pl.ds(512 * k, 512)], local.at[22 + k])
        copy.start()
        turned.append(copy)
    step(behind[1], "forward", 2)
    step(behind[0], "settle")
    for copy in turned[2:]:
        copy.wait()
    ct[...] = cot_rows[...].T
    ut[...] = dot(go[...].reshape(1152, 1024), selector(72)).astype(LOW)
    dt[...] = dot(go[...].reshape(1152, 1024), selector(72 + TAIL)).astype(LOW)
    acc2[...] = jnp.zeros(acc2.shape, FULL)
    acc3[...] = jnp.zeros(acc3.shape, FULL)
    for copy in back:
        copy.wait_recv()
    for copy in stores:
        copy.wait()
    stores = []

    def store(source, target, semaphore):
        copy = pltpu.make_async_copy(source, target, local.at[semaphore])
        copy.start()
        stores.append(copy)


    upper_half, lower_half = slice(0, 256), slice(256, 512)
    quarters = [slice(k * 256, (k + 1) * 256) for k in range(4)]

    def branch_part(rows):
        return dot_cols(mixed[rows, :], go[...].reshape(1152, 1024))

    out1[...] = branch_part(lower_half).astype(LOW)
    branch = copies.start(out1, in1, sibling)
    middle = branch_part(upper_half) + tokens[...].astype(FULL) + out_bias
    branch.wait_recv()
    middle = middle + in1[...].astype(FULL)
    result[...] = middle + down_bias
    centre = middle - mean(middle)
    inverse = lax.rsqrt(mean(centre * centre) + EPSILON)
    scaled = centre * inverse
    xhat[...] = scaled
    n2[upper_half, :] = (scaled * gain + shift).astype(LOW)
    normed = start(n2.at[pl.ds(0, 256)], n2.at[pl.ds(256, 256)], sibling)
    normed.wait_recv()
    n2t[...] = n2[...].T

    def hidden_block(u, d, block_bias):
        active, slope = smooth(dot(n2[...], u) + block_bias)
        upper = (dot(cot_rows[...], d) * slope).astype(LOW)
        active = active.astype(LOW)
        acc2[...] += dot_cols(active, d)
        acc3[...] += dot_cols(upper, u)
        return active, upper

    def grad_copy(ref, out, f, first):
        cols = lanes(f * 512, 512)
        return pltpu.make_async_copy(ref.at[:, :, :, cols], out.at[:, :, :, cols], local.at[first + f])

    streams = ((ffn_a, dffn_a, 7), (ffn_b, dffn_b, 11))
    for k, (ref, out, first) in enumerate(streams):
        step(behind[k], "settle")
        for g in behind[k]:
            for copy in g.sent:
                copy.wait_send()

        @pl.loop(0, 4)
        def _(f, k=k, ref=ref, out=out, first=first):
            def piece(n):
                return lanes(f * 512 + n * 128, 128)

            def columns(n):
                return jnp.concatenate(
                    [ref[:, :, :, piece(m)].reshape(1152, 128) for m in (n, n + 2)], axis=1
                )

            hidden_cols = lanes(k * 1024 + f * 256, 256)
            active, upper = hidden_block(columns(0), columns(1), hidden_bias[:, hidden_cols])
            sums_hidden[:, hidden_cols] = column_sum(upper)
            for n, grad in enumerate((dot(n2t[...], upper).astype(LOW), dot(ct[...], active).astype(LOW))):
                ref[:, :, :, piece(n)] = grad[:, :128].reshape(2, 4, 144, 128)
                ref[:, :, :, piece(n + 2)] = grad[:, 128:].reshape(2, 4, 144, 128)
            grad_copy(ref, out, f, first).start()

    active, upper = hidden_block(ut[...], dt[...], hidden_bias[:, 2048:HIDDEN])
    sums_hidden[:, 2048:HIDDEN] = column_sum(upper)
    branch.wait_send()
    out1[...] = acc3[lower_half, :].astype(LOW)
    return_copy = start(out1, in3, sibling)
    out2[...] = acc2[lower_half, :].astype(LOW)
    forth = start(out2, in2, sibling)
    up_tail = dot_cols(upper, selector(72)).astype(LOW)
    down_tail = dot_cols(active, selector(72 + TAIL)).astype(LOW)
    upstream = cot_rows[upper_half, :].astype(FULL)
    return_copy.wait_recv()
    normed_grad = acc3[upper_half, :] + in3[...].astype(FULL)
    scaled = xhat[...]
    along = normed_grad * gain
    grad = upstream + inverse * (along - mean(along) - scaled * mean(along * scaled))
    middle_grad[...] = grad
    store(middle_grad, middle_grad_out, 20)
    low = grad.astype(LOW)
    bg[upper_half, :] = low
    branch_grad = start(bg.at[pl.ds(0, 256)], bg.at[pl.ds(256, 256)], sibling)
    sums[0:1, :] = column_sum(low)
    sums[1:2, :] = column_sum(upstream)
    sums[2:3, :] = column_sum(normed_grad * scaled)
    sums[3:4, :] = column_sum(normed_grad)
    sums[4:8, :] = jnp.zeros((4, 1152), FULL)
    forth.wait_recv()
    result[...] += acc2[upper_half, :] + in2[...].astype(FULL)
    store(result, result_out, 21)
    branch_grad.wait_recv()
    for cols in quarters:
        mixed_grad[:, cols] = dot(bg[...], go[:, :, :, cols].reshape(1152, 256)).astype(LOW)
    heads_back = []
    for j in range(2):
        spot = pl.ds(j * 128, 128)
        for partner in (up, down, far):
            source = mixed_grad.at[:, lanes((4 * j + partner["z"]) * 128, 128)]
            heads_back.append(start(source, heads_grad.at[z, :, spot], partner))
        heads_grad[z, :, spot] = mixed_grad[:, lanes((4 * j + z) * 128, 128)]
    for cols in quarters:
        go[:, :, :, cols] = (
            (
                dot(n2t[...], up_tail[:, cols])
                + dot(ct[...], down_tail[:, cols])
                + dot_rows(bg[...], mixed[:, cols])
            )
            .astype(LOW)
            .reshape(2, 4, 144, 256)
        )
    last = pltpu.make_async_copy(go, dout, local.at[15])
    last.start()
    for ref, out, first in streams:
        for n in range(4):
            grad_copy(ref, out, n, first).wait()
    last.wait()
    for copy in stores:
        copy.wait()
    for copy in heads_back:
        copy.wait_recv()
    for copy in sent + [copy for g in ahead for copy in g.sent]:
        copy.wait_send()


def forward(weights, consts, up_bias, picture, cot, tokens):
    count = 12 + 12 + 5 + 6 + 2 * 15 + 3 * 45
    grids = [(2, 4, 144, 8 * w) for w in WIDTHS[1:]]
    rows, half = (512, 1152), (256, 1152)
    return pl.pallas_call(
        forward_kernel,
        out_shape=[
            jax.ShapeDtypeStruct(half, FULL),
            jax.ShapeDtypeStruct(half, FULL),
        ]
        + [jax.ShapeDtypeStruct(grid, LOW) for grid in grids]
        + [
            jax.ShapeDtypeStruct((1152, 2048), LOW),
            jax.ShapeDtypeStruct((1152, 768), LOW),
        ]
        + [jax.ShapeDtypeStruct((4, 1024, 128), LOW)] * 3
        + [
            jax.ShapeDtypeStruct((4, 512, 256), LOW),
            jax.ShapeDtypeStruct((16, 128), FULL),
            jax.ShapeDtypeStruct((4, 1, 1024), FULL),
            jax.ShapeDtypeStruct((8, 128), FULL),
            jax.ShapeDtypeStruct((1, HIDDEN), FULL),
            jax.ShapeDtypeStruct((8, 1152), FULL),
        ],
        in_specs=[vmem()] * 9 + [anywhere(), vmem()],
        out_specs=[hbm()] * 10 + [vmem()] * 6,
        scratch_shapes=[
            pltpu.VMEM((144, UNIT), FULL),
            pltpu.VMEM((144, UNIT), LOW),
            pltpu.VMEM((2, 4, 144, 512), LOW),
        ]
        + [pltpu.VMEM(grid, LOW) for grid in grids]
        + [
            pltpu.VMEM((4, 512, 1152), LOW),
            pltpu.VMEM((2, 1, 1024), FULL),
            pltpu.VMEM((2, 1024, 1), FULL),
            pltpu.VMEM((4, 128, 1024), LOW),
            pltpu.VMEM((4, 4, 256, 128), LOW),
            pltpu.VMEM((4, 1, 256), FULL),
            pltpu.VMEM(rows, LOW),
            pltpu.VMEM((512, 1024), LOW),
            pltpu.VMEM((1152, 128), LOW),
            pltpu.VMEM((1152, 128), LOW),
            pltpu.VMEM(rows, LOW),
            pltpu.VMEM((1152, 512), LOW),
            pltpu.VMEM((1152, 512), LOW),
            pltpu.VMEM(rows, FULL),
            pltpu.VMEM(rows, FULL),
            pltpu.VMEM(half, FULL),
            pltpu.VMEM(rows, LOW),
        ]
        + [pltpu.VMEM(half, LOW)] * 5
        + [
            pltpu.VMEM((8, 128), FULL),
            pltpu.VMEM((1, HIDDEN), FULL),
            pltpu.VMEM((2, 72, UNIT), FULL),
        ]
        + [pltpu.VMEM((4, 1024, 128), LOW)] * 3
        + [
            pltpu.VMEM((1152, 768), LOW),
            pltpu.VMEM(half, FULL),
            pltpu.VMEM(half, FULL),
            pltpu.VMEM((512, 1024), LOW),
            pltpu.SemaphoreType.DMA((count,)),
            pltpu.SemaphoreType.DMA((count,)),
            pltpu.SemaphoreType.DMA((26,)),
        ],
        compiler_params=pltpu.CompilerParams(
            collective_id=0, has_side_effects=True, vmem_limit_bytes=60 << 20
        ),
        name="forward_attention",
    )(*weights, consts, up_bias, picture, cot, tokens)


def backward_kernel(
    grad, q, k, v, consts, both_ids, logsum, dout, dffn_a, dffn_b, weights, n1t, tokens,
    middle, sums_hidden, sums, peak, token_grad, out, totals, *rest
):
    (
        q_s, k_s, v_s, w_s, middle_grad, g_s, n1t_s, kt_s, dk_s, dv_s, proj_grad, ids_row, ids_col, part_out, part_in,
        part_own, near, low, high, dslab, unit, other, line, near_lines, send, receive, local,
    ) = rest[:27]
    buffers = list(rest[27:])
    at = place()
    z, core = at["z"], at["core"]
    sibling = moved(at, "core", 1)
    up, down, far = [moved(at, "z", step) for step in STEPS]
    loads = [
        pltpu.make_async_copy(source, target, local.at[n])
        for n, (source, target) in enumerate(
            ((k, k_s), (q, q_s), (v, v_s), (weights, w_s), (n1t, n1t_s), (middle, middle_grad))
        )
    ]
    for copy in loads:
        copy.start()
    greet([sibling] + [moved(at, axis, step) for axis in ALL for step in STEPS])
    copies = Copies(send, receive)
    sent = []

    def start(source, target, partner):
        copy = copies.start(source, target, partner)
        sent.append(copy)
        return copy

    counter = [local, 7]
    behind = [
        Scatter(copies, at, [dout, dffn_a, dffn_b], WIDTHS[1:], part, buffers, ALL, counter)
        for part in PARTS_BACK
    ]
    last = [Scatter(copies, at, [dslab], [256], part, buffers, "xy") for part in PARTS]
    for s in behind:
        s.begin(0)
    set_ids(both_ids, 0, ids_row, ids_col)
    set_ids(both_ids, 1, ids_row, ids_col)
    values = tokens[...].astype(FULL)
    centre = values - mean(values)
    inverse = lax.rsqrt(mean(centre * centre) + EPSILON)
    token_grad[...] = centre * inverse
    for copy in loads[:3]:
        copy.wait()
    for n in range(4):
        kt_s[n] = k_s[n].T
    lane = lax.broadcasted_iota(jnp.int32, (256, 128), 1)
    for r in range(2):
        for j in range(2):
            for b in range(4):
                block = grad[b, r * 256 : (r + 1) * 256, j * 128 : (j + 1) * 128]
                g_s[2 * r + j, b * 256 : (b + 1) * 256, :] = jnp.where(
                    lane < HEAD_DIM, block.astype(FULL), 0.0
                ).astype(LOW)

    def heads_back(r):
        dk_s[...] = jnp.zeros(dk_s.shape, FULL)
        dv_s[...] = jnp.zeros(dv_s.shape, FULL)

        @pl.loop(0, 4)
        def _(b):
            rows = pl.ds(pl.multiple_of(b * 256, 256), 256)
            spot = pl.ds(pl.multiple_of(b * 512 + r * 256, 256), 256)
            allowed = ids_col[r] == ids_row[r, :, rows]
            for j in range(2):
                n = 2 * r + j
                query, upper = q_s[n, rows, :], g_s[n, rows, :]
                scores = dot_cols(k_s[n], query) * SCALE
                probs = jnp.where(allowed, jnp.exp(scores - logsum[n, :, rows]), 0.0)
                dv_s[j] += dot(probs.astype(LOW), upper)
                prob_grad = dot_cols(v_s[n], upper)
                centre = jnp.sum(probs * prob_grad, axis=0, keepdims=True)
                score_grad = (probs * (prob_grad - centre)).astype(LOW)
                proj_grad[spot, j * 384 : j * 384 + 128] = (
                    (dot(kt_s[n], score_grad) * SCALE).T.astype(LOW)
                )
                dk_s[j] += dot(score_grad, query)

        for j in range(2):
            for b in range(4):
                spot = slice(b * 512 + r * 256, b * 512 + (r + 1) * 256)
                rows = slice(b * 256, (b + 1) * 256)
                proj_grad[spot, j * 384 + 128 : j * 384 + 256] = (dk_s[j, rows, :] * SCALE).astype(LOW)
                proj_grad[spot, j * 384 + 256 : j * 384 + 384] = dv_s[j, rows, :].astype(LOW)

    def part(owner, r):
        spot = pl.ds(pl.multiple_of(owner["z"] * 512 + r * 256, 256), 256)
        return dot_cols(proj_grad[spot, :], w_s[...])

    heads_back(1)
    for copy in loads[3:]:
        copy.wait()
    swapped = []
    for owner in (far, up, down, at):
        n = owner["z"]
        part_out[n] = part(owner, 1).astype(LOW)
        swapped.append(copies.start(part_out.at[n], part_in.at[n], sibling))
    for s in behind:
        s.relay(0)
    heads_back(0)

    def summed(owner, copy):
        copy.wait()
        return part(owner, 0) + part_in[owner["z"]].astype(FULL)

    half_a, half_b = pl.ds(0, 128), pl.ds(128, 128)
    part_out[far["z"]] = summed(far, swapped[0]).astype(LOW)
    arriving = [
        start(part_out.at[far["z"], half_a], near.at[half_a], up),
        start(part_out.at[far["z"], half_b], near.at[half_b], down),
    ]
    part_out[up["z"]] = summed(up, swapped[1]).astype(LOW)
    part_out[down["z"]] = summed(down, swapped[2]).astype(LOW)
    part_own[...] = summed(at, swapped[3])
    for copy in arriving:
        copy.wait_recv()
    near[0:128, :] = (near[0:128, :].astype(FULL) + part_out[up["z"], 0:128, :].astype(FULL)).astype(LOW)
    near[128:256, :] = (
        near[128:256, :].astype(FULL) + part_out[down["z"], 128:256, :].astype(FULL)
    ).astype(LOW)
    arriving = [
        start(near.at[half_a], low.at[half_a], up),
        start(part_out.at[up["z"], half_b], low.at[half_b], up),
        start(near.at[half_b], high.at[half_b], down),
        start(part_out.at[down["z"], half_a], high.at[half_a], down),
    ]
    for n in range(3):
        cols = slice(n * 256, (n + 1) * 256)
        w_s[:, cols] = dot(n1t_s[...], proj_grad[:, cols]).astype(LOW)
    for j in range(2):
        dslab[:, :, :, j * 256 : (j + 1) * 256] = (
            dot_cols(w_s[:, j * 384 : (j + 1) * 384], picker()).astype(LOW).reshape(2, 4, 144, 256)
        )
    for s in last:
        s.begin(0)
    projected = column_sum(proj_grad[...])
    for s in behind:
        s.finish(0)
        s.begin(1)
    for s in last:
        s.relay(0)
    for copy in arriving:
        copy.wait_recv()
    normed_grad = part_own[...] + low[...].astype(FULL) + high[...].astype(FULL)
    scaled = token_grad[...]
    along = normed_grad * consts[4:5, :]
    token_grad[...] = middle_grad[...] + inverse * (
        along - mean(along) - scaled * mean(along * scaled)
    )
    for t in range(8):
        for n in range(3):
            first = (t // 4) * 384 + n * 128
            line[0, 3 * t + n : 3 * t + n + 1, :] = jnp.where(
                z == t % 4, projected[:, first : first + 128], 0.0
            )
    row = 24
    for piece in (
        sums_hidden[...],
        sums[0:1, :],
        sums[1:2, :],
        column_sum(normed_grad * scaled),
        column_sum(normed_grad),
        sums[2:3, :],
        sums[3:4, :],
        jnp.zeros((1, 128), FULL),
    ):
        for n in range(piece.shape[1] // 128):
            line[0, row : row + 1, :] = piece[:, n * 128 : (n + 1) * 128]
            row += 1
    head = lax.broadcasted_iota(jnp.int32, (8, 128), 1) - (2 * z + core)
    line[0, 96:104, :] = jnp.where(
        head == 0, peak[0:1, 0:1], jnp.where(head == 8, peak[1:2, 0:1], LOWEST)
    )

    def send_line(phase):
        return [
            start(line.at[phase], near_lines.at[phase, n], moved(at, ALL[phase], step))
            for n, step in enumerate(STEPS)
        ]

    def add_line(phase, begun):
        for copy in begun:
            copy.wait_recv()
        parts = [line[phase]] + [near_lines[phase, n] for n in range(3)]
        line[phase + 1, 0:96, :] = (parts[0][:96] + parts[1][:96]) + (parts[2][:96] + parts[3][:96])
        line[phase + 1, 96:104, :] = jnp.maximum(
            jnp.maximum(parts[0][96:], parts[1][96:]), jnp.maximum(parts[2][96:], parts[3][96:])
        )

    arriving = send_line(0)
    for s in behind:
        s.relay(1)
    add_line(0, arriving)
    arriving = send_line(1)
    for s in behind:
        s.finish(1)
        s.last()
    for s in last:
        s.finish(0)
        s.last()
    add_line(1, arriving)
    arriving = send_line(2)
    for s in behind:
        s.result(unit, STARTS[1:])
    for s in last:
        s.result(unit, [0])
    mine = pl.ds(pl.multiple_of(core * 72, 8), 72)
    theirs = pl.ds(pl.multiple_of((1 - core) * 72, 8), 72)
    late = start(unit.at[theirs], other, sibling)
    add_line(2, arriving)
    line_copy = start(line.at[3], totals.at[core], sibling)
    totals[core] = line[3]
    out[core] = unit[mine, :]
    late.wait_recv()
    out[1 - core] = other[...]
    line_copy.wait_recv()
    for copy in sent + [copy for s in behind + last for copy in s.sent]:
        copy.wait_send()


def backward(heads_grad, heads, consts, both_ids, logsum, grids, weights, n1t, tokens, middle_grad, sums_hidden, sums, peak):
    count = 4 + 6 + 9 + 2 + 3 * 45 + 2 * 15
    shapes = []
    for part in PARTS_BACK:
        shapes += Scatter.shapes(WIDTHS[1:], part, True)
    for part in PARTS:
        shapes += Scatter.shapes([256], part, False)
    half = (256, 1152)
    return pl.pallas_call(
        backward_kernel,
        out_shape=[
            jax.ShapeDtypeStruct(half, FULL),
            jax.ShapeDtypeStruct((2, 72, UNIT), FULL),
            jax.ShapeDtypeStruct((2, 104, 128), FULL),
        ],
        in_specs=[vmem()] + [anywhere()] * 3 + [vmem()] * 3 + [anywhere()] * 5 + [vmem(), anywhere()] + [vmem()] * 3,
        out_specs=[vmem()] * 3,
        scratch_shapes=[
            pltpu.VMEM((4, 1024, 128), LOW),
            pltpu.VMEM((4, 1024, 128), LOW),
            pltpu.VMEM((4, 1024, 128), LOW),
            pltpu.VMEM((1152, 768), LOW),
            pltpu.VMEM(half, FULL),
            pltpu.VMEM((4, 1024, 128), LOW),
            pltpu.VMEM((1152, 2048), LOW),
            pltpu.VMEM((4, 128, 1024), LOW),
            pltpu.VMEM((2, 1024, 128), FULL),
            pltpu.VMEM((2, 1024, 128), FULL),
            pltpu.VMEM((2048, 768), LOW),
            pltpu.VMEM((2, 1, 1024), FULL),
            pltpu.VMEM((2, 1024, 1), FULL),
            pltpu.VMEM((4,) + half, LOW),
            pltpu.VMEM((4,) + half, LOW),
            pltpu.VMEM(half, FULL),
            pltpu.VMEM(half, LOW),
            pltpu.VMEM(half, LOW),
            pltpu.VMEM(half, LOW),
            pltpu.VMEM((2, 4, 144, 512), LOW),
            pltpu.VMEM((144, UNIT), FULL),
            pltpu.VMEM((72, UNIT), FULL),
            pltpu.VMEM((4, 104, 128), FULL),
            pltpu.VMEM((3, 3, 104, 128), FULL),
            pltpu.SemaphoreType.DMA((count,)),
            pltpu.SemaphoreType.DMA((count,)),
            pltpu.SemaphoreType.DMA((64,)),
        ]
        + shapes,
        compiler_params=pltpu.CompilerParams(
            collective_id=1, has_side_effects=True, vmem_limit_bytes=60 << 20
        ),
        name="backward_attention",
    )(
        heads_grad, *heads, consts, both_ids, logsum, *grids, weights, n1t, tokens, middle_grad, sums_hidden, sums,
        peak,
    )


def finish_kernel(
    grads, totals, query_weight, key_weight, result_in, token_in,
    result, token_grad, query_w, key_w, value_w, out_w, up_w, down_w_t, query_b, value_b, up_b, *rest
):
    vectors, (query_clip, key_clip, held, local) = rest[:6], rest[6:]
    loads = [
        pltpu.make_async_copy(result_in, held.at[0], local.at[0]),
        pltpu.make_async_copy(token_in, held.at[1], local.at[1]),
    ]
    stores = [
        pltpu.make_async_copy(held.at[0], result, local.at[2]),
        pltpu.make_async_copy(held.at[1], token_grad, local.at[3]),
    ]
    for copy in loads:
        copy.start()
    tensor = lax.axis_index("tensor")
    lane = lax.broadcasted_iota(jnp.int32, (72, 256), 1)

    def heads(start):
        first, second = (shifted(grads[c, :, 0:384], (384 - start) % 384, 384)[:, :128] for c in range(2))
        return jnp.where(lane < HEAD_DIM, shifted(first, 0, 256), shifted(second, HEAD_DIM, 256))

    query_w[...] = heads(0)[:, :144]
    key_w[...] = heads(72)[:, :144]
    value_w[...] = heads(144)[:, :144]
    out_w[...] = heads(256).T[:144, :]
    wide = lax.broadcasted_iota(jnp.int32, (72, 640), 1)

    def hidden(main, tail):
        total = jnp.zeros((72, 640), FULL)
        for c in range(2):
            last = shifted(grads[c, :, 256:384], (128 - tail) % 128, 128)
            base = c * (MAIN + TAIL)
            block = jnp.concatenate(
                [grads[c, :, main : main + 128], grads[c, :, main + 256 : main + 384], last], axis=1
            )
            inside = (wide >= base) & (wide < base + MAIN + TAIL)
            total = jnp.where(inside, shifted(block, base, 640), total)
        return total

    up_w[...] = hidden(384, 72)[:, :538]
    down_w_t[...] = hidden(512, 72 + TAIL)[:, :538]
    for load, copy in zip(loads, stores):
        load.wait()
        copy.start()

    def line_up(target, pieces, size, width):
        lane = lax.broadcasted_iota(jnp.int32, (1, width), 1)
        total = jnp.zeros((1, width), FULL)
        for n, piece in enumerate(pieces):
            inside = (lane >= size * n) & (lane < size * (n + 1))
            total = jnp.where(inside, shifted(piece, size * n, width), total)
        for k in range(width // 128):
            target[k : k + 1, :] = total[:, 128 * k : 128 * (k + 1)]

    order = [(t, c) for t in range(8) for c in range(2)]
    line_up(query_b, [totals[c, 3 * t : 3 * t + 1, :] for t, c in order], HEAD_DIM, 1152)
    line_up(value_b, [totals[c, 3 * t + 2 : 3 * t + 3, :] for t, c in order], HEAD_DIM, 1152)
    line_up(
        up_b,
        [
            jnp.concatenate(
                [
                    totals[c, 24 + t : 25 + t, :],
                    totals[c, 32 + t : 33 + t, :],
                    shifted(totals[c, 40:41, :], (128 - TAIL * t) % 128, 128),
                ],
                axis=1,
            )
            for t, c in order
        ],
        MAIN + TAIL,
        34 * 128,
    )
    for n in range(6):
        rows = slice(41 + 9 * n, 50 + 9 * n)
        vectors[n][...] = totals[0, rows, :] + totals[1, rows, :]
    peak = jnp.maximum(totals[0, 96:97, :], totals[1, 96:97, :])
    factor = jnp.sqrt(CLIP_LIMIT / jnp.maximum(peak, CLIP_LIMIT))
    spot = lax.broadcasted_iota(jnp.int32, (1, 128), 1)
    low, high = (
        jnp.sum(jnp.where(spot == 2 * tensor + c, factor, 0.0), axis=1, keepdims=True) for c in range(2)
    )
    scale = jnp.where(lax.broadcasted_iota(jnp.int32, (1, 144), 1) < HEAD_DIM, low, high)
    query_clip[...] = query_weight[...].astype(FULL) * scale
    key_clip[...] = key_weight[...].astype(FULL) * scale
    for copy in stores:
        copy.wait()


def finish(grads, totals, query_weight, key_weight, result, token_grad):
    shapes = [(256, 1152)] * 2 + [(72, 144)] * 3 + [(144, 72), (72, 538), (72, 538)]
    shapes += [(9, 128)] * 2 + [(34, 128)] + [(9, 128)] * 6 + [(72, 144)] * 2
    return pl.pallas_call(
        finish_kernel,
        out_shape=[jax.ShapeDtypeStruct(shape, FULL) for shape in shapes],
        in_specs=[vmem()] * 4 + [hbm()] * 2,
        out_specs=[hbm()] * 2 + [vmem()] * 17,
        scratch_shapes=[pltpu.VMEM((2, 256, 1152), FULL), pltpu.SemaphoreType.DMA((4,))],
        compiler_params=pltpu.CompilerParams(vmem_limit_bytes=48 << 20),
        name="finish_outputs",
    )(grads, totals, query_weight, key_weight, result, token_grad)


def per_device(
    tokens,
    picture,
    cotangent,
    gain_one,
    shift_one,
    query_weight,
    query_bias,
    key_weight,
    value_weight,
    value_bias,
    out_weight,
    out_bias,
    gain_two,
    shift_two,
    up_weight,
    up_bias,
    down_weight,
    down_bias,
):
    row = lax.broadcasted_iota(jnp.int32, (8, tokens.shape[1]), 0)
    consts = jnp.zeros(row.shape, LOW)
    vectors = (out_bias, gain_two, shift_two, down_bias, gain_one, shift_one, query_bias, value_bias)
    for k, vector in enumerate(vectors):
        consts = jnp.where(row == k, vector[None, :], consts)
    consts = consts.astype(FULL)
    weights = (query_weight, key_weight, value_weight, out_weight, up_weight, down_weight.T)
    result, middle_grad, *rest = forward(
        weights, consts, jnp.pad(up_bias.astype(FULL), (0, 48)).reshape(34, 128), picture.reshape(16, 128), cotangent, tokens
    )
    grids, (rows_one_t, head_weights), heads = rest[:3], rest[3:5], rest[5:8]
    heads_grad, both_ids, logsum, peak, sums_hidden, sums = rest[8:]
    input_grad, grads, totals = backward(
        heads_grad,
        heads,
        consts,
        both_ids,
        logsum,
        grids,
        head_weights,
        rows_one_t,
        tokens,
        middle_grad,
        sums_hidden,
        sums,
        peak,
    )
    outputs = finish(grads, totals, query_weight, key_weight, result, input_grad)
    return (
        *outputs[:7],
        outputs[7].T,
        *(vector.reshape(-1) for vector in outputs[8:10]),
        outputs[10].reshape(-1)[: 8 * 538],
        *(vector.reshape(-1) for vector in outputs[11:17]),
        *outputs[17:],
    )


def solution(mesh):
    in_specs = (
        P(("dp", "tensor"), None),
        P("dp"),
        P(("dp", "tensor"), None),
        P(),
        P(),
        P("dp", "tensor"),
        P(),
        P("dp", "tensor"),
        P("dp", "tensor"),
        P(),
        P("tensor", "dp"),
        P(),
        P(),
        P(),
        P("dp", "tensor"),
        P(),
        P("tensor", "dp"),
        P(),
    )
    out_specs = (
        P(("dp", "tensor"), None),
        P(("dp", "tensor"), None),
        P("dp", "tensor"),
        P("dp", "tensor"),
        P("dp", "tensor"),
        P("tensor", "dp"),
        P("dp", "tensor"),
        P("tensor", "dp"),
        P(),
        P(),
        P(),
        P(),
        P(),
        P(),
        P(),
        P(),
        P(),
        P("dp", "tensor"),
        P("dp", "tensor"),
    )
    return jax.shard_map(
        per_device, mesh=mesh, in_specs=in_specs, out_specs=out_specs, check_vma=False
    )
```

```python
import functools

import jax
import jax.numpy as jnp
import numpy as np
from jax import lax
from jax.experimental import pallas as pl
from jax.experimental.pallas import tpu as pltpu
from jax.sharding import PartitionSpec as P

HEAD_DIM = 72
EPSILON = 1e-06
CLIP_LIMIT = 2.0
LOWEST = -1e30
SCALE = HEAD_DIM**-0.5

MESH = pl.DeviceIdType.MESH
LOW = jnp.bfloat16
FULL = jnp.float32

STARTS = (0, 256, 384, 640)
WIDTHS = (256, 128, 256, 256)
STREAMS = ((0, 1), (2,))
UNIT = 896
MAIN = 256
TAIL = 13
HIDDEN = 8 * MAIN + 128
PARTS = ((0, 80, "xy"), (80, 64, "yx"))
PARTS_BEHIND = (
    ((0, 64, "zyx"), (64, 48, "zxy"), (112, 32, "yxz")),
    ((0, 48, "zyx"), (48, 64, "zxy"), (112, 32, "yxz")),
)
PARTS_BACK = ((0, 64, "zyx"), (64, 64, "zxy"), (128, 16, "yxz"))
STEPS = (1, 3, 2)
ALL = "xyz"


def place():
    d, t = lax.axis_index("dp"), lax.axis_index("tensor")
    return {"x": (d // 2) % 4, "y": (t // 4) * 2 + d // 8, "z": t % 4, "core": d % 2}


def device(at):
    return ((at["y"] % 2) * 8 + at["x"] * 2 + at["core"], (at["y"] // 2) * 4 + at["z"])


def moved(at, axis, step):
    other = dict(at)
    other[axis] = 1 - at["core"] if axis == "core" else (at[axis] + step) % 4
    return other


def greet(partners, between=None):
    barrier = pltpu.get_barrier_semaphore()
    for partner in partners:
        pl.semaphore_signal(barrier, inc=1, device_id=device(partner), device_id_type=MESH)
    if between:
        between()
    pl.semaphore_wait(barrier, len(partners))


class Copies:
    def __init__(self, send, receive):
        self.send, self.receive, self.used = send, receive, 0

    def start(self, source, target, partner):
        copy = pltpu.make_async_remote_copy(
            src_ref=source,
            dst_ref=target,
            send_sem=self.send.at[self.used],
            recv_sem=self.receive.at[self.used],
            device_id=device(partner),
            device_id_type=MESH,
        )
        self.used += 1
        copy.start()
        return copy


def lanes(first, size):
    return pl.ds(first if isinstance(first, int) else pl.multiple_of(first, 128), size)


def spots(held, have, at, width, rows, half=None):
    zs, ys = (4 if "z" in held else 1), at["y"] if "y" in held else 0
    x_at = pl.ds(0, 4) if "x" in have else pl.ds(at["x"] if "x" in held else 0, 1)
    y_at = pl.ds(0, 2) if "y" in have else pl.ds(ys % 2, 1)
    z = at["z"] if "z" in held else 0
    if "y" in have and "z" in have:
        ranges = [(0, 8 * width)]
    elif "y" in have:
        ranges = [((h * zs + z) * width, width) for h in (0, 1)]
    elif "z" in have:
        ranges = [((ys // 2) * zs * width, 4 * width)]
    else:
        ranges = [(((ys // 2) * zs + z) * width, width)]
    if half is not None:
        if len(ranges) == 2:
            ranges = [ranges[half]]
        elif "x" in have:
            x_at = pl.ds(2 * half, 2)
        elif "y" in have:
            y_at = pl.ds(half, 1)
        else:
            ((first, size),) = ranges
            ranges = [(first + half * (size // 2), size // 2)]
    return [(y_at, x_at, pl.ds(*rows), lanes(*r)) for r in ranges]


def rect_shape(have, width, rows):
    ys, xs, zs = 2 if "y" in have else 1, 4 if "x" in have else 1, 4 if "z" in have else 1
    return (ys, xs, rows, ys * zs * width)


class Gather:
    def __init__(self, copies, at, grids, widths, part, held=ALL):
        self.copies, self.at, self.grids, self.widths = copies, at, grids, widths
        self.rows, self.order, self.held = part[:2], part[2], held
        self.arriving, self.sent = [], []

    def views(self, grid, width, have, at, half=None):
        return [grid.at[spot] for spot in spots(self.held, have, at, width, self.rows, half)]

    def send(self, have, owner, partner, half=None):
        started = []
        for grid, width in zip(self.grids, self.widths):
            for view in self.views(grid, width, have, owner, half):
                started.append(self.copies.start(view, view, partner))
        self.sent += started
        return started

    def settle(self):
        for copy in self.arriving:
            copy.wait_recv()
        self.arriving = []

    def first(self):
        for step in STEPS:
            self.arriving += self.send("", self.at, moved(self.at, self.order[0], step))

    def ring(self, phase):
        self.settle()
        axis, have = self.order[phase], self.order[:phase]
        self.after = self.send(have, self.at, moved(self.at, axis, 1))
        self.before = self.send(have, self.at, moved(self.at, axis, 3))

    def forward(self, phase):
        axis, have = self.order[phase], self.order[:phase]
        up, down = moved(self.at, axis, 1), moved(self.at, axis, 3)
        for copy in self.after:
            copy.wait_recv()
        self.arriving += self.send(have, down, up, 0)
        for copy in self.before:
            copy.wait_recv()
        self.arriving += self.send(have, up, down, 1)


def add_into(target, terms, shape):
    @pl.loop(0, shape[0] * shape[1] * (shape[2] // 16))
    def _(n):
        block = n // (shape[2] // 16)
        spot = (
            block // shape[1],
            block % shape[1],
            pl.ds(pl.multiple_of((n % (shape[2] // 16)) * 16, 16), 16),
            slice(None),
        )
        total = terms[0][spot].astype(FULL)
        for term in terms[1:]:
            total = total + term[spot].astype(FULL)
        target[spot] = total.astype(target.dtype)


def half_shape(have, shape):
    ys, xs, rows, cols = shape
    if "y" in have and "z" not in have:
        return (ys, xs, rows, cols // 2)
    if "x" in have:
        return (ys, 2, rows, cols)
    if "y" in have:
        return (1, xs, rows, cols)
    return (ys, xs, rows, cols // 2)


class Scatter:
    @staticmethod
    def shapes(widths, part, loaded):
        _, rows, order = part
        shapes = []
        for phase in range(len(order) - 1):
            have = order[: len(order) - 1 - phase]
            for _ in range(5 if loaded and phase == 0 else 4):
                shapes += [pltpu.VMEM(rect_shape(have, w, rows), LOW) for w in widths]
        shapes += [pltpu.VMEM((3, 1, 1, rows, w), LOW) for w in widths]
        return shapes

    def __init__(self, copies, at, grids, widths, part, buffers, held=ALL, local=None):
        self.copies, self.at, self.grids, self.widths = copies, at, grids, widths
        self.rows, self.order = part[:2], part[2]
        self.rings = len(self.order) - 1
        self.held = [held] + [self.order[: self.rings - phase] for phase in range(self.rings)]
        self.local = local
        self.sent = []

        def take():
            taken, buffers[:] = buffers[: len(widths)], buffers[len(widths) :]
            return taken

        self.near, self.low, self.high, self.own = [], [], [], []
        for phase in range(self.rings):
            for group in (self.near, self.low, self.high, self.own):
                group.append(take())
            if phase == 0 and local:
                self.mix = [take()]
        self.direct = take()

    def have(self, phase):
        return self.order[: self.rings - phase]

    def source(self, phase, a, at, half=None):
        grid = self.grids[a] if phase == 0 else self.own[phase - 1][a]
        rows = self.rows if phase == 0 else (0, self.rows[1])
        found = spots(self.held[phase], self.have(phase), at, self.widths[a], rows, half)
        return [grid.at[spot] for spot in found]

    def target(self, phase, buffer, a, half=None):
        have = self.have(phase)
        found = spots(have, have, self.at, self.widths[a], (0, self.rows[1]), half)
        return [buffer[phase][a].at[spot] for spot in found]

    def push(self, sources, targets, partner):
        started = [self.copies.start(s, t, partner) for s, t in zip(sources, targets)]
        self.sent += started
        return started

    def begin(self, phase):
        axis = self.order[self.rings - phase]
        up, down, far = (moved(self.at, axis, step) for step in STEPS)
        self.arriving, self.loading = [], []
        for a in range(len(self.grids)):
            for half, partner in ((0, up), (1, down)):
                self.arriving += self.push(
                    self.source(phase, a, far, half),
                    self.target(phase, self.near, a, half),
                    partner,
                )
        if phase == 0 and self.local:
            for a in range(len(self.grids)):
                pairs = list(
                    zip(
                        self.source(0, a, up, 0) + self.source(0, a, down, 1),
                        self.target(0, self.mix, a, 0) + self.target(0, self.mix, a, 1),
                    )
                )
                pairs += list(zip(self.source(0, a, self.at), self.target(0, self.own, a)))
                for view, target in pairs:
                    copy = pltpu.make_async_copy(view, target, self.local[0].at[self.local[1]])
                    self.local[1] += 1
                    copy.start()
                    self.loading.append(copy)

    def relay(self, phase):
        axis, have = self.order[self.rings - phase], self.have(phase)
        up, down, _ = (moved(self.at, axis, step) for step in STEPS)
        for copy in self.loading:
            copy.wait()
        for copy in self.arriving:
            copy.wait_recv()
        self.arriving = []
        for a in range(len(self.grids)):
            shape = half_shape(have, rect_shape(have, self.widths[a], self.rows[1]))
            for half, partner in ((0, up), (1, down)):
                (near,) = self.target(phase, self.near, a, half)
                if phase == 0 and self.local:
                    (view,) = self.target(phase, self.mix, a, half)
                else:
                    (view,) = self.source(phase, a, partner, half)
                add_into(near, [view, near], shape)
                buffer = self.low if half == 0 else self.high
                self.arriving += self.push(
                    [near] + self.source(phase, a, partner, 1 - half),
                    self.target(phase, buffer, a, half) + self.target(phase, buffer, a, 1 - half),
                    partner,
                )

    def finish(self, phase):
        have = self.have(phase)
        for copy in self.arriving:
            copy.wait_recv()
        for a in range(len(self.grids)):
            for low, high, own, source in zip(
                self.target(phase, self.low, a),
                self.target(phase, self.high, a),
                self.target(phase, self.own, a),
                self.source(phase, a, self.at),
            ):
                shape = rect_shape(have, self.widths[a], self.rows[1])
                if "y" in have and "z" not in have:
                    shape = half_shape(have, shape)
                add_into(own, [own if phase == 0 and self.local else source, low, high], shape)

    def last(self):
        self.arriving = []
        for k, step in enumerate(STEPS):
            partner = moved(self.at, self.order[0], step)
            for a in range(len(self.grids)):
                self.arriving += self.push(
                    self.source(self.rings, a, partner), [self.direct[a].at[k]], partner
                )

    def result(self, out, starts):
        for copy in self.arriving:
            copy.wait_recv()
        for a, start in enumerate(starts):
            (mine,) = self.source(self.rings, a, self.at)
            total = mine[0, 0].astype(FULL)
            for k in range(3):
                total = total + self.direct[a][k, 0, 0].astype(FULL)
            out[pl.ds(*self.rows), start : start + self.widths[a]] = total


def hbm():
    return pl.BlockSpec(memory_space=pltpu.HBM)


def anywhere():
    return pl.BlockSpec(memory_space=pl.ANY)


def vmem():
    return pl.BlockSpec(memory_space=pltpu.VMEM)


def picker():
    row = lax.broadcasted_iota(jnp.int32, (256, 384), 0)
    lane = lax.broadcasted_iota(jnp.int32, (256, 384), 1)
    hit = ((lane & 127) < HEAD_DIM) & (row == (lane >> 7) * HEAD_DIM + (lane & 127))
    return jnp.where(hit, 1.0, 0.0).astype(LOW)


def dot(left, right):
    return jnp.dot(left, right, preferred_element_type=FULL)


def dot_rows(left, right):
    return lax.dot_general(left, right, (((0,), (0,)), ((), ())), preferred_element_type=FULL)


def dot_cols(left, right):
    return lax.dot_general(left, right, (((1,), (1,)), ((), ())), preferred_element_type=FULL)


def set_ids(ids, r, ids_row, ids_col):
    eye = lax.broadcasted_iota(jnp.int32, (128, 128), 0) == lax.broadcasted_iota(
        jnp.int32, (128, 128), 1
    )
    for k in range(8):
        piece = ids[8 * r + k : 8 * r + k + 1, :]
        ids_row[r, :, k * 128 : (k + 1) * 128] = piece
        ids_col[r, k * 128 : (k + 1) * 128, :] = jnp.sum(
            jnp.where(eye, piece, 0.0), axis=1, keepdims=True
        )


def selector(offset):
    row = lax.broadcasted_iota(jnp.int32, (1024, 128), 0)
    lane = lax.broadcasted_iota(jnp.int32, (1024, 128), 1)
    inner = (row & 127) - offset
    hit = (inner >= 0) & (inner < TAIL) & (lane == (row >> 7) * TAIL + inner)
    return jnp.where(hit, 1.0, 0.0).astype(LOW)


def smooth(inner):
    root = 0.7978845608028654
    square = inner * inner
    wave = jnp.tanh(root * inner * (1.0 + 0.044715 * square))
    up = 0.5 * (1.0 + wave)
    slope = up + 0.5 * inner * (1.0 - wave * wave) * root * (1.0 + 3 * 0.044715 * square)
    return inner * up, slope


def mean(values):
    return jnp.sum(values, axis=1, keepdims=True) * (1.0 / values.shape[1])


def column_sum(values):
    return jnp.sum(values.astype(FULL), axis=0, keepdims=True)


def shifted(values, amount, width):
    if values.shape[1] < width:
        pad = jnp.zeros((values.shape[0], width - values.shape[1]), FULL)
        values = jnp.concatenate([values, pad], axis=1)
    return pltpu.roll(values, amount, 1) if amount else values


def widened(values, width):
    pad = jnp.zeros((values.shape[0], width - values.shape[1]), FULL)
    return jnp.concatenate([values.astype(FULL), pad], axis=1)


def pack_half(half, query, key, value, out_t, up, down_t, pack):
    lane = lax.broadcasted_iota(jnp.int32, (72, 256), 1)
    total = jnp.zeros((72, 256), FULL)
    for k, weight in enumerate((query, key, value)):
        spot = HEAD_DIM * k
        block = pltpu.roll(weight, (spot - HEAD_DIM * half) % 256, 1)
        total = jnp.where((lane >= spot) & (lane < spot + HEAD_DIM), block, total)
    pack[half, :, 0:256] = total
    first = half * (MAIN + TAIL)
    lane = lax.broadcasted_iota(jnp.int32, (72, 128), 1)
    total = jnp.where(lane < HEAD_DIM, pltpu.roll(out_t, (-HEAD_DIM * half) % 256, 1)[:, :128], 0.0)
    for k, weight in enumerate((up, down_t)):
        spot = HEAD_DIM + TAIL * k
        block = pltpu.roll(weight, (spot - first - MAIN) % 640, 1)[:, :128]
        total = jnp.where((lane >= spot) & (lane < spot + TAIL), block, total)
        block = pltpu.roll(weight, (-first) % 640, 1) if half else weight
        pack[half, :, 384 + 128 * k : 512 + 128 * k] = block[:, :128]
        pack[half, :, 640 + 128 * k : 768 + 128 * k] = block[:, 128:256]
    pack[half, :, 256:384] = total


def set_biases(core, z, consts, up_bias, hidden_bias):
    lane = lax.broadcasted_iota(jnp.int32, (1, 128), 1)
    pieces = []
    for j in range(2):
        for k in (6, None, 7):
            total = jnp.zeros((1, 128), FULL)
            if k is not None:
                for head in range(16):
                    block = shifted(consts[k : k + 1, :], (-HEAD_DIM * head) % 1152, 1152)[:, :128]
                    total = jnp.where(head == 8 * j + 2 * z + core, block, total)
            pieces.append(jnp.where(lane < HEAD_DIM, total, 0.0))
    line = jnp.concatenate([up_bias[k : k + 1, :] for k in range(34)], axis=1)
    line = jnp.where(core == 0, line, pltpu.roll(line, 34 * 128 - MAIN - TAIL, 1))
    tails = jnp.zeros((1, 128), FULL)
    for t in range(8):
        row = shifted(line, (-2 * (MAIN + TAIL) * t) % (34 * 128), 34 * 128)
        hidden_bias[:, t * 128 : (t + 1) * 128] = row[:, 0:128]
        hidden_bias[:, 1024 + t * 128 : 1152 + t * 128] = row[:, 128:256]
        tail = shifted(row[:, 256:384], TAIL * t, 128)
        tails = jnp.where((lane >= TAIL * t) & (lane < TAIL * (t + 1)), tail, tails)
    hidden_bias[:, 2048:HIDDEN] = tails
    return jnp.concatenate(pieces, axis=1)


def forward_kernel(
    query, key, value, out_weight, up_weight, down_weight_t, consts, up_bias, picture, cot, tokens,
    result_out, middle_grad_out, dout, dffn_a, dffn_b, n1t_out, weights_out, q_out, k_out, v_out, heads_grad, both_ids,
    logsum, peak, sums_hidden, sums,
    both, unit, slab, go, ffn_a, ffn_b, n1_all, ids_row, ids_col, vt_s, out_s, top_s, cot_rows, mixed,
    ut, dt, n2, n2t, ct, acc2, acc3, xhat, bg, out1, out2, in1, in2, in3, ids, hidden_bias, pack, q_s, k_s, v_s,
    weights, result, middle_grad, mixed_grad, send, receive, local,
):
    at = place()
    core, z = at["core"], at["z"]
    sibling = moved(at, "core", 1)
    up, down, far = (moved(at, "z", step) for step in STEPS)
    grids = (go, ffn_a, ffn_b)
    cot_own = pltpu.make_async_copy(cot, cot_rows.at[pl.ds(0, 256)], local.at[1])
    cot_own.start()

    def pack_weights():
        wide = [widened(w[...], 256) for w in (query, key, value)]
        wide.append(widened(out_weight[...].astype(FULL).T, 256))
        wide += [widened(w[...], 640) for w in (up_weight, down_weight_t)]
        for half in range(2):
            pack_half(half, *wide, pack)

    greet([sibling] + [moved(at, axis, step) for axis in ALL for step in STEPS], pack_weights)
    copies = Copies(send, receive)
    sent = []

    def start(source, target, partner):
        copy = copies.start(source, target, partner)
        sent.append(copy)
        return copy

    mine = pl.ds(pl.multiple_of(core * 72, 8), 72)
    first_copy = start(pack.at[1 - core], both.at[mine], sibling)
    half_row = pl.ds(pl.multiple_of((at["y"] // 2) * 8, 8), 8)
    numbers = picture[half_row, :]
    slot = lax.broadcasted_iota(jnp.int32, (8, 128), 0) * 128 + lax.broadcasted_iota(jnp.int32, (8, 128), 1)
    ids[...] = jnp.where(numbers >= 0, numbers, -1 - slot).astype(FULL)
    ids_copy = start(ids, both_ids.at[pl.ds(8, 8)], sibling)
    both_ids[0:8, :] = ids[...]
    out_bias, gain, shift, down_bias, gain_first, shift_first = (consts[k : k + 1, :] for k in range(6))

    def block(owner, r, first=0, size=256):
        return n1_all.at[owner["z"], pl.ds(r * 256 + first, size)]

    def ring_step(first):
        return [
            start(block(at, 0, first, 128), block(at, 0, first, 128), partner) for partner in (up, down)
        ]

    both[mine, :] = pack[core]
    values = tokens[...].astype(FULL)
    centre = values - mean(values)
    inverse = lax.rsqrt(mean(centre * centre) + EPSILON)
    n1_all[z, 0:256, :] = (centre * inverse * gain_first + shift_first).astype(LOW)
    ring = [ring_step(0)]
    other = {0: start(block(at, 0), block(at, 1), sibling)}
    cot_copy = start(cot, cot_rows.at[pl.ds(256, 256)], sibling)
    first_copy.wait_recv()
    unit[...] = both[...].astype(LOW)
    tensor = (at["y"] // 2) * 4 + z
    slab[at["y"] % 2, at["x"], :, lanes((at["y"] // 2) * 256, 256)] = unit[:, 0:256]
    for grid, first, width in zip(grids, STARTS[1:], WIDTHS[1:]):
        grid[at["y"] % 2, at["x"], :, lanes(tensor * width, width)] = unit[:, first : first + width]
    ahead = [Gather(copies, at, [slab], [256], part, "xy") for part in PARTS]
    behind = [
        [
            Gather(copies, at, [grids[n] for n in names], [WIDTHS[n + 1] for n in names], part)
            for part in parts
        ]
        for names, parts in zip(STREAMS, PARTS_BEHIND)
    ]

    def step(group, name, *phase):
        for g in group:
            getattr(g, name)(*phase)

    step(ahead, "first")
    for group in behind:
        step(group[2:] + group[:2], "first")
    ring.append(ring_step(128))
    ids_copy.wait_recv()
    set_ids(ids, 0, ids_row, ids_col)
    set_ids(both_ids, 1, ids_row, ids_col)
    step(ahead, "ring", 1)
    bias = set_biases(core, z, consts, up_bias, hidden_bias)
    ring[0][0].wait_recv()
    halves = [start(block(down, 0, 0, 128), block(down, 0, 0, 128), up)]
    step(ahead, "forward", 1)
    step(behind[0], "ring", 1)
    step(behind[1], "ring", 1)
    step(ahead, "settle")
    for j in range(2):
        packed = slab[:, :, :, j * 256 : (j + 1) * 256].reshape(1152, 256)
        weights[:, j * 384 : (j + 1) * 384] = dot(packed, picker()).astype(LOW)

    def project(owner, r):
        rows = pl.ds(pl.multiple_of(owner["z"] * 256, 256), 256)
        product = (dot(n1_all[owner["z"], r * 256 : (r + 1) * 256, :], weights[...]) + bias).astype(LOW)
        for j in range(2):
            for k, target in enumerate((q_s, k_s, v_s)):
                first_lane = j * 384 + k * 128
                target[2 * r + j, rows, :] = product[:, first_lane : first_lane + 128]

    project(at, 0)
    ring[1][1].wait_recv()
    halves.append(start(block(up, 0, 128, 128), block(up, 0, 128, 128), down))
    ring[0][1].wait_recv()
    other[2] = start(block(up, 0), block(up, 1), sibling)
    ring[1][0].wait_recv()
    other[1] = start(block(down, 0), block(down, 1), sibling)
    step(behind[0], "forward", 1)
    other[0].wait_recv()
    project(at, 1)
    step(behind[1], "forward", 1)
    step(behind[0], "ring", 2)
    project(down, 0)
    project(up, 0)
    step(behind[1], "ring", 2)
    other[1].wait_recv()
    project(down, 1)
    other[2].wait_recv()
    project(up, 1)
    for copy in halves:
        copy.wait_recv()
    other[3] = start(block(far, 0), block(far, 1), sibling)
    project(far, 0)
    other[3].wait_recv()
    project(far, 1)
    stores = [
        pltpu.make_async_copy(source, target, local.at[16 + k])
        for k, (source, target) in enumerate(
            ((q_s, q_out), (k_s, k_out), (v_s, v_out), (weights, weights_out))
        )
    ]
    for copy in stores:
        copy.start()
    for n in range(4):
        vt_s[n] = v_s[n].T
    top_s[...] = jnp.full(top_s.shape, LOWEST, FULL)
    back = []
    for k, hop in enumerate(STEPS + (0,)):
        b = (z + hop) % 4
        rows = pl.ds(pl.multiple_of(b * 256, 256), 256)

        @pl.loop(0, 4)
        def _(n, b=b, rows=rows):
            r = n // 2
            scores = dot_cols(k_s[n], q_s[n, rows, :]) * SCALE
            query_ids = ids_row[r, :, rows]
            scores = jnp.where(ids_col[r] == query_ids, scores, LOWEST)
            top = jnp.max(scores, axis=0, keepdims=True)
            expo = jnp.exp(scores - top)
            total = jnp.sum(expo, axis=0, keepdims=True)
            weights_low = (expo * (1.0 / total)).astype(LOW)
            out_s[n, b] = dot(vt_s[n], weights_low).T.astype(LOW)
            logsum[n, :, rows] = top + jnp.log(total)
            top_s[n] = jnp.maximum(top_s[n], jnp.where(query_ids >= 0.0, top, LOWEST))

        for n in range(4):
            r, j = n // 2, n % 2
            source = out_s.at[n, b]
            spot = (pl.ds(r * 256, 256), lanes((4 * j + z) * 128, 128))
            if hop:
                back.append(start(source, mixed.at[spot], moved(at, "z", hop)))
            else:
                copy = pltpu.make_async_copy(source, mixed.at[spot], local.at[2 + n])
                copy.start()
                stores.append(copy)
    row = lax.broadcasted_iota(jnp.int32, (8, 128), 0)
    high = [jnp.maximum(jnp.max(top_s[j]), jnp.max(top_s[2 + j])) for j in range(2)]
    peak[...] = jnp.where(row == 0, high[0], high[1])
    step(behind[0], "forward", 2)
    cot_own.wait()
    cot_copy.wait_recv()
    turned = []
    for k in range(4):
        if k >= 2:
            turned[k - 2].wait()
        buffer = (n2t, ct)[k % 2]
        buffer[...] = n1_all[k].T
        copy = pltpu.make_async_copy(buffer, n1t_out.at[:, pl.ds(512 * k, 512)], local.at[22 + k])
        copy.start()
        turned.append(copy)
    step(behind[1], "forward", 2)
    step(behind[0], "settle")
    for copy in turned[2:]:
        copy.wait()
    ct[...] = cot_rows[...].T
    ut[...] = dot(go[...].reshape(1152, 1024), selector(72)).astype(LOW)
    dt[...] = dot(go[...].reshape(1152, 1024), selector(72 + TAIL)).astype(LOW)
    acc2[...] = jnp.zeros(acc2.shape, FULL)
    acc3[...] = jnp.zeros(acc3.shape, FULL)
    for copy in back:
        copy.wait_recv()
    for copy in stores:
        copy.wait()
    stores = []

    def store(source, target, semaphore):
        copy = pltpu.make_async_copy(source, target, local.at[semaphore])
        copy.start()
        stores.append(copy)


    upper_half, lower_half = slice(0, 256), slice(256, 512)
    quarters = [slice(k * 256, (k + 1) * 256) for k in range(4)]

    def branch_part(rows):
        return dot_cols(mixed[rows, :], go[...].reshape(1152, 1024))

    out1[...] = branch_part(lower_half).astype(LOW)
    branch = copies.start(out1, in1, sibling)
    middle = branch_part(upper_half) + tokens[...].astype(FULL) + out_bias
    branch.wait_recv()
    middle = middle + in1[...].astype(FULL)
    result[...] = middle + down_bias
    centre = middle - mean(middle)
    inverse = lax.rsqrt(mean(centre * centre) + EPSILON)
    scaled = centre * inverse
    xhat[...] = scaled
    n2[upper_half, :] = (scaled * gain + shift).astype(LOW)
    normed = start(n2.at[pl.ds(0, 256)], n2.at[pl.ds(256, 256)], sibling)
    normed.wait_recv()
    n2t[...] = n2[...].T

    def hidden_block(u, d, block_bias):
        active, slope = smooth(dot(n2[...], u) + block_bias)
        upper = (dot(cot_rows[...], d) * slope).astype(LOW)
        active = active.astype(LOW)
        acc2[...] += dot_cols(active, d)
        acc3[...] += dot_cols(upper, u)
        return active, upper

    def grad_copy(ref, out, f, first):
        cols = lanes(f * 512, 512)
        return pltpu.make_async_copy(ref.at[:, :, :, cols], out.at[:, :, :, cols], local.at[first + f])

    streams = ((ffn_a, dffn_a, 7), (ffn_b, dffn_b, 11))
    for k, (ref, out, first) in enumerate(streams):
        step(behind[k], "settle")
        for g in behind[k]:
            for copy in g.sent:
                copy.wait_send()

        @pl.loop(0, 4)
        def _(f, k=k, ref=ref, out=out, first=first):
            def piece(n):
                return lanes(f * 512 + n * 128, 128)

            def columns(n):
                return jnp.concatenate(
                    [ref[:, :, :, piece(m)].reshape(1152, 128) for m in (n, n + 2)], axis=1
                )

            hidden_cols = lanes(k * 1024 + f * 256, 256)
            active, upper = hidden_block(columns(0), columns(1), hidden_bias[:, hidden_cols])
            sums_hidden[:, hidden_cols] = column_sum(upper)
            for n, grad in enumerate((dot(n2t[...], upper).astype(LOW), dot(ct[...], active).astype(LOW))):
                ref[:, :, :, piece(n)] = grad[:, :128].reshape(2, 4, 144, 128)
                ref[:, :, :, piece(n + 2)] = grad[:, 128:].reshape(2, 4, 144, 128)
            grad_copy(ref, out, f, first).start()

    active, upper = hidden_block(ut[...], dt[...], hidden_bias[:, 2048:HIDDEN])
    sums_hidden[:, 2048:HIDDEN] = column_sum(upper)
    branch.wait_send()
    out1[...] = acc3[lower_half, :].astype(LOW)
    return_copy = start(out1, in3, sibling)
    out2[...] = acc2[lower_half, :].astype(LOW)
    forth = start(out2, in2, sibling)
    up_tail = dot_cols(upper, selector(72)).astype(LOW)
    down_tail = dot_cols(active, selector(72 + TAIL)).astype(LOW)
    upstream = cot_rows[upper_half, :].astype(FULL)
    return_copy.wait_recv()
    normed_grad = acc3[upper_half, :] + in3[...].astype(FULL)
    scaled = xhat[...]
    along = normed_grad * gain
    grad = upstream + inverse * (along - mean(along) - scaled * mean(along * scaled))
    middle_grad[...] = grad
    store(middle_grad, middle_grad_out, 20)
    low = grad.astype(LOW)
    bg[upper_half, :] = low
    branch_grad = start(bg.at[pl.ds(0, 256)], bg.at[pl.ds(256, 256)], sibling)
    sums[0:1, :] = column_sum(low)
    sums[1:2, :] = column_sum(upstream)
    sums[2:3, :] = column_sum(normed_grad * scaled)
    sums[3:4, :] = column_sum(normed_grad)
    sums[4:8, :] = jnp.zeros((4, 1152), FULL)
    forth.wait_recv()
    result[...] += acc2[upper_half, :] + in2[...].astype(FULL)
    store(result, result_out, 21)
    branch_grad.wait_recv()
    for cols in quarters:
        mixed_grad[:, cols] = dot(bg[...], go[:, :, :, cols].reshape(1152, 256)).astype(LOW)
    heads_back = []
    for j in range(2):
        spot = pl.ds(j * 128, 128)
        for partner in (up, down, far):
            source = mixed_grad.at[:, lanes((4 * j + partner["z"]) * 128, 128)]
            heads_back.append(start(source, heads_grad.at[z, :, spot], partner))
        heads_grad[z, :, spot] = mixed_grad[:, lanes((4 * j + z) * 128, 128)]
    for cols in quarters:
        go[:, :, :, cols] = (
            (
                dot(n2t[...], up_tail[:, cols])
                + dot(ct[...], down_tail[:, cols])
                + dot_rows(bg[...], mixed[:, cols])
            )
            .astype(LOW)
            .reshape(2, 4, 144, 256)
        )
    last = pltpu.make_async_copy(go, dout, local.at[15])
    last.start()
    for ref, out, first in streams:
        for n in range(4):
            grad_copy(ref, out, n, first).wait()
    last.wait()
    for copy in stores:
        copy.wait()
    for copy in heads_back:
        copy.wait_recv()
    for copy in sent + [copy for g in ahead for copy in g.sent]:
        copy.wait_send()


def forward(weights, consts, up_bias, picture, cot, tokens):
    count = 12 + 12 + 5 + 6 + 2 * 15 + 3 * 45
    grids = [(2, 4, 144, 8 * w) for w in WIDTHS[1:]]
    rows, half = (512, 1152), (256, 1152)
    return pl.pallas_call(
        forward_kernel,
        out_shape=[
            jax.ShapeDtypeStruct(half, FULL),
            jax.ShapeDtypeStruct(half, FULL),
        ]
        + [jax.ShapeDtypeStruct(grid, LOW) for grid in grids]
        + [
            jax.ShapeDtypeStruct((1152, 2048), LOW),
            jax.ShapeDtypeStruct((1152, 768), LOW),
        ]
        + [jax.ShapeDtypeStruct((4, 1024, 128), LOW)] * 3
        + [
            jax.ShapeDtypeStruct((4, 512, 256), LOW),
            jax.ShapeDtypeStruct((16, 128), FULL),
            jax.ShapeDtypeStruct((4, 1, 1024), FULL),
            jax.ShapeDtypeStruct((8, 128), FULL),
            jax.ShapeDtypeStruct((1, HIDDEN), FULL),
            jax.ShapeDtypeStruct((8, 1152), FULL),
        ],
        in_specs=[vmem()] * 9 + [anywhere(), vmem()],
        out_specs=[hbm()] * 10 + [vmem()] * 6,
        scratch_shapes=[
            pltpu.VMEM((144, UNIT), FULL),
            pltpu.VMEM((144, UNIT), LOW),
            pltpu.VMEM((2, 4, 144, 512), LOW),
        ]
        + [pltpu.VMEM(grid, LOW) for grid in grids]
        + [
            pltpu.VMEM((4, 512, 1152), LOW),
            pltpu.VMEM((2, 1, 1024), FULL),
            pltpu.VMEM((2, 1024, 1), FULL),
            pltpu.VMEM((4, 128, 1024), LOW),
            pltpu.VMEM((4, 4, 256, 128), LOW),
            pltpu.VMEM((4, 1, 256), FULL),
            pltpu.VMEM(rows, LOW),
            pltpu.VMEM((512, 1024), LOW),
            pltpu.VMEM((1152, 128), LOW),
            pltpu.VMEM((1152, 128), LOW),
            pltpu.VMEM(rows, LOW),
            pltpu.VMEM((1152, 512), LOW),
            pltpu.VMEM((1152, 512), LOW),
            pltpu.VMEM(rows, FULL),
            pltpu.VMEM(rows, FULL),
            pltpu.VMEM(half, FULL),
            pltpu.VMEM(rows, LOW),
        ]
        + [pltpu.VMEM(half, LOW)] * 5
        + [
            pltpu.VMEM((8, 128), FULL),
            pltpu.VMEM((1, HIDDEN), FULL),
            pltpu.VMEM((2, 72, UNIT), FULL),
        ]
        + [pltpu.VMEM((4, 1024, 128), LOW)] * 3
        + [
            pltpu.VMEM((1152, 768), LOW),
            pltpu.VMEM(half, FULL),
            pltpu.VMEM(half, FULL),
            pltpu.VMEM((512, 1024), LOW),
            pltpu.SemaphoreType.DMA((count,)),
            pltpu.SemaphoreType.DMA((count,)),
            pltpu.SemaphoreType.DMA((26,)),
        ],
        compiler_params=pltpu.CompilerParams(
            collective_id=0, has_side_effects=True, vmem_limit_bytes=60 << 20
        ),
        name="forward_attention",
    )(*weights, consts, up_bias, picture, cot, tokens)


def backward_kernel(
    grad, q, k, v, consts, both_ids, logsum, dout, dffn_a, dffn_b, weights, n1t, tokens,
    middle, sums_hidden, sums, peak, token_grad, out, totals, *rest
):
    (
        q_s, k_s, v_s, w_s, middle_grad, g_s, n1t_s, kt_s, dk_s, dv_s, proj_grad, ids_row, ids_col, part_out, part_in,
        part_own, near, low, high, dslab, unit, other, line, near_lines, send, receive, local,
    ) = rest[:27]
    buffers = list(rest[27:])
    at = place()
    z, core = at["z"], at["core"]
    sibling = moved(at, "core", 1)
    up, down, far = [moved(at, "z", step) for step in STEPS]
    loads = [
        pltpu.make_async_copy(source, target, local.at[n])
        for n, (source, target) in enumerate(
            ((k, k_s), (q, q_s), (v, v_s), (weights, w_s), (n1t, n1t_s), (middle, middle_grad))
        )
    ]
    for copy in loads:
        copy.start()
    greet([sibling] + [moved(at, axis, step) for axis in ALL for step in STEPS])
    copies = Copies(send, receive)
    sent = []

    def start(source, target, partner):
        copy = copies.start(source, target, partner)
        sent.append(copy)
        return copy

    counter, grids = [local, 7], (dout, dffn_a, dffn_b)
    behind = [
        Scatter(copies, at, [grids[n] for n in names], [WIDTHS[n + 1] for n in names], part, buffers, ALL, counter)
        for names in STREAMS
        for part in PARTS_BACK
    ]
    last = [Scatter(copies, at, [dslab], [256], part, buffers, "xy") for part in PARTS]
    for s in behind:
        s.begin(0)
    set_ids(both_ids, 0, ids_row, ids_col)
    set_ids(both_ids, 1, ids_row, ids_col)
    values = tokens[...].astype(FULL)
    centre = values - mean(values)
    inverse = lax.rsqrt(mean(centre * centre) + EPSILON)
    token_grad[...] = centre * inverse
    for copy in loads[:3]:
        copy.wait()
    for n in range(4):
        kt_s[n] = k_s[n].T
    lane = lax.broadcasted_iota(jnp.int32, (256, 128), 1)
    for r in range(2):
        for j in range(2):
            for b in range(4):
                block = grad[b, r * 256 : (r + 1) * 256, j * 128 : (j + 1) * 128]
                g_s[2 * r + j, b * 256 : (b + 1) * 256, :] = jnp.where(
                    lane < HEAD_DIM, block.astype(FULL), 0.0
                ).astype(LOW)

    def heads_back(r):
        dk_s[...] = jnp.zeros(dk_s.shape, FULL)
        dv_s[...] = jnp.zeros(dv_s.shape, FULL)

        @pl.loop(0, 4)
        def _(b):
            rows = pl.ds(pl.multiple_of(b * 256, 256), 256)
            spot = pl.ds(pl.multiple_of(b * 512 + r * 256, 256), 256)
            allowed = ids_col[r] == ids_row[r, :, rows]
            for j in range(2):
                n = 2 * r + j
                query, upper = q_s[n, rows, :], g_s[n, rows, :]
                scores = dot_cols(k_s[n], query) * SCALE
                probs = jnp.where(allowed, jnp.exp(scores - logsum[n, :, rows]), 0.0)
                dv_s[j] += dot(probs.astype(LOW), upper)
                prob_grad = dot_cols(v_s[n], upper)
                centre = jnp.sum(probs * prob_grad, axis=0, keepdims=True)
                score_grad = (probs * (prob_grad - centre)).astype(LOW)
                proj_grad[spot, j * 384 : j * 384 + 128] = (
                    (dot(kt_s[n], score_grad) * SCALE).T.astype(LOW)
                )
                dk_s[j] += dot(score_grad, query)

        for j in range(2):
            for b in range(4):
                spot = slice(b * 512 + r * 256, b * 512 + (r + 1) * 256)
                rows = slice(b * 256, (b + 1) * 256)
                proj_grad[spot, j * 384 + 128 : j * 384 + 256] = (dk_s[j, rows, :] * SCALE).astype(LOW)
                proj_grad[spot, j * 384 + 256 : j * 384 + 384] = dv_s[j, rows, :].astype(LOW)

    def part(owner, r):
        spot = pl.ds(pl.multiple_of(owner["z"] * 512 + r * 256, 256), 256)
        return dot_cols(proj_grad[spot, :], w_s[...])

    heads_back(1)
    for copy in loads[3:]:
        copy.wait()
    swapped = []
    for owner in (far, up, down, at):
        n = owner["z"]
        part_out[n] = part(owner, 1).astype(LOW)
        swapped.append(copies.start(part_out.at[n], part_in.at[n], sibling))
    for s in behind:
        s.relay(0)
    heads_back(0)

    def summed(owner, copy):
        copy.wait()
        return part(owner, 0) + part_in[owner["z"]].astype(FULL)

    half_a, half_b = pl.ds(0, 128), pl.ds(128, 128)
    part_out[far["z"]] = summed(far, swapped[0]).astype(LOW)
    arriving = [
        start(part_out.at[far["z"], half_a], near.at[half_a], up),
        start(part_out.at[far["z"], half_b], near.at[half_b], down),
    ]
    part_out[up["z"]] = summed(up, swapped[1]).astype(LOW)
    part_out[down["z"]] = summed(down, swapped[2]).astype(LOW)
    part_own[...] = summed(at, swapped[3])
    for copy in arriving:
        copy.wait_recv()
    near[0:128, :] = (near[0:128, :].astype(FULL) + part_out[up["z"], 0:128, :].astype(FULL)).astype(LOW)
    near[128:256, :] = (
        near[128:256, :].astype(FULL) + part_out[down["z"], 128:256, :].astype(FULL)
    ).astype(LOW)
    arriving = [
        start(near.at[half_a], low.at[half_a], up),
        start(part_out.at[up["z"], half_b], low.at[half_b], up),
        start(near.at[half_b], high.at[half_b], down),
        start(part_out.at[down["z"], half_a], high.at[half_a], down),
    ]
    for n in range(3):
        cols = slice(n * 256, (n + 1) * 256)
        w_s[:, cols] = dot(n1t_s[...], proj_grad[:, cols]).astype(LOW)
    for j in range(2):
        dslab[:, :, :, j * 256 : (j + 1) * 256] = (
            dot_cols(w_s[:, j * 384 : (j + 1) * 384], picker()).astype(LOW).reshape(2, 4, 144, 256)
        )
    for s in last:
        s.begin(0)
    projected = column_sum(proj_grad[...])
    for s in behind:
        s.finish(0)
        s.begin(1)
    for s in last:
        s.relay(0)
    for copy in arriving:
        copy.wait_recv()
    normed_grad = part_own[...] + low[...].astype(FULL) + high[...].astype(FULL)
    scaled = token_grad[...]
    along = normed_grad * consts[4:5, :]
    token_grad[...] = middle_grad[...] + inverse * (
        along - mean(along) - scaled * mean(along * scaled)
    )
    for t in range(8):
        for n in range(3):
            first = (t // 4) * 384 + n * 128
            line[0, 3 * t + n : 3 * t + n + 1, :] = jnp.where(
                z == t % 4, projected[:, first : first + 128], 0.0
            )
    row = 24
    for piece in (
        sums_hidden[...],
        sums[0:1, :],
        sums[1:2, :],
        column_sum(normed_grad * scaled),
        column_sum(normed_grad),
        sums[2:3, :],
        sums[3:4, :],
        jnp.zeros((1, 128), FULL),
    ):
        for n in range(piece.shape[1] // 128):
            line[0, row : row + 1, :] = piece[:, n * 128 : (n + 1) * 128]
            row += 1
    head = lax.broadcasted_iota(jnp.int32, (8, 128), 1) - (2 * z + core)
    line[0, 96:104, :] = jnp.where(
        head == 0, peak[0:1, 0:1], jnp.where(head == 8, peak[1:2, 0:1], LOWEST)
    )

    def send_line(phase):
        return [
            start(line.at[phase], near_lines.at[phase, n], moved(at, ALL[phase], step))
            for n, step in enumerate(STEPS)
        ]

    def add_line(phase, begun):
        for copy in begun:
            copy.wait_recv()
        parts = [line[phase]] + [near_lines[phase, n] for n in range(3)]
        line[phase + 1, 0:96, :] = (parts[0][:96] + parts[1][:96]) + (parts[2][:96] + parts[3][:96])
        line[phase + 1, 96:104, :] = jnp.maximum(
            jnp.maximum(parts[0][96:], parts[1][96:]), jnp.maximum(parts[2][96:], parts[3][96:])
        )

    arriving = send_line(0)
    for s in behind:
        s.relay(1)
    add_line(0, arriving)
    arriving = send_line(1)
    for s in behind:
        s.finish(1)
        s.last()
    for s in last:
        s.finish(0)
        s.last()
    add_line(1, arriving)
    arriving = send_line(2)
    for k, s in enumerate(behind):
        s.result(unit, [STARTS[n + 1] for n in STREAMS[k // 3]])
    for s in last:
        s.result(unit, [0])
    mine = pl.ds(pl.multiple_of(core * 72, 8), 72)
    theirs = pl.ds(pl.multiple_of((1 - core) * 72, 8), 72)
    late = start(unit.at[theirs], other, sibling)
    add_line(2, arriving)
    line_copy = start(line.at[3], totals.at[core], sibling)
    totals[core] = line[3]
    out[core] = unit[mine, :]
    late.wait_recv()
    out[1 - core] = other[...]
    line_copy.wait_recv()
    for copy in sent + [copy for s in behind + last for copy in s.sent]:
        copy.wait_send()


def backward(heads_grad, heads, consts, both_ids, logsum, grids, weights, n1t, tokens, middle_grad, sums_hidden, sums, peak):
    count = 4 + 6 + 9 + 2 + 3 * 45 + 2 * 15
    shapes = []
    for names in STREAMS:
        for part in PARTS_BACK:
            shapes += Scatter.shapes([WIDTHS[n + 1] for n in names], part, True)
    for part in PARTS:
        shapes += Scatter.shapes([256], part, False)
    half = (256, 1152)
    return pl.pallas_call(
        backward_kernel,
        out_shape=[
            jax.ShapeDtypeStruct(half, FULL),
            jax.ShapeDtypeStruct((2, 72, UNIT), FULL),
            jax.ShapeDtypeStruct((2, 104, 128), FULL),
        ],
        in_specs=[vmem()] + [anywhere()] * 3 + [vmem()] * 3 + [anywhere()] * 5 + [vmem(), anywhere()] + [vmem()] * 3,
        out_specs=[vmem()] * 3,
        scratch_shapes=[
            pltpu.VMEM((4, 1024, 128), LOW),
            pltpu.VMEM((4, 1024, 128), LOW),
            pltpu.VMEM((4, 1024, 128), LOW),
            pltpu.VMEM((1152, 768), LOW),
            pltpu.VMEM(half, FULL),
            pltpu.VMEM((4, 1024, 128), LOW),
            pltpu.VMEM((1152, 2048), LOW),
            pltpu.VMEM((4, 128, 1024), LOW),
            pltpu.VMEM((2, 1024, 128), FULL),
            pltpu.VMEM((2, 1024, 128), FULL),
            pltpu.VMEM((2048, 768), LOW),
            pltpu.VMEM((2, 1, 1024), FULL),
            pltpu.VMEM((2, 1024, 1), FULL),
            pltpu.VMEM((4,) + half, LOW),
            pltpu.VMEM((4,) + half, LOW),
            pltpu.VMEM(half, FULL),
            pltpu.VMEM(half, LOW),
            pltpu.VMEM(half, LOW),
            pltpu.VMEM(half, LOW),
            pltpu.VMEM((2, 4, 144, 512), LOW),
            pltpu.VMEM((144, UNIT), FULL),
            pltpu.VMEM((72, UNIT), FULL),
            pltpu.VMEM((4, 104, 128), FULL),
            pltpu.VMEM((3, 3, 104, 128), FULL),
            pltpu.SemaphoreType.DMA((count,)),
            pltpu.SemaphoreType.DMA((count,)),
            pltpu.SemaphoreType.DMA((64,)),
        ]
        + shapes,
        compiler_params=pltpu.CompilerParams(
            collective_id=1, has_side_effects=True, vmem_limit_bytes=60 << 20
        ),
        name="backward_attention",
    )(
        heads_grad, *heads, consts, both_ids, logsum, *grids, weights, n1t, tokens, middle_grad, sums_hidden, sums,
        peak,
    )


def finish_kernel(
    grads, totals, query_weight, key_weight, result_in, token_in,
    result, token_grad, query_w, key_w, value_w, out_w, up_w, down_w_t, query_b, value_b, up_b, *rest
):
    vectors, (query_clip, key_clip, held, local) = rest[:6], rest[6:]
    loads = [
        pltpu.make_async_copy(result_in, held.at[0], local.at[0]),
        pltpu.make_async_copy(token_in, held.at[1], local.at[1]),
    ]
    stores = [
        pltpu.make_async_copy(held.at[0], result, local.at[2]),
        pltpu.make_async_copy(held.at[1], token_grad, local.at[3]),
    ]
    for copy in loads:
        copy.start()
    tensor = lax.axis_index("tensor")
    lane = lax.broadcasted_iota(jnp.int32, (72, 256), 1)

    def heads(start):
        first, second = (shifted(grads[c, :, 0:384], (384 - start) % 384, 384)[:, :128] for c in range(2))
        return jnp.where(lane < HEAD_DIM, shifted(first, 0, 256), shifted(second, HEAD_DIM, 256))

    query_w[...] = heads(0)[:, :144]
    key_w[...] = heads(72)[:, :144]
    value_w[...] = heads(144)[:, :144]
    out_w[...] = heads(256).T[:144, :]
    wide = lax.broadcasted_iota(jnp.int32, (72, 640), 1)

    def hidden(main, tail):
        total = jnp.zeros((72, 640), FULL)
        for c in range(2):
            last = shifted(grads[c, :, 256:384], (128 - tail) % 128, 128)
            base = c * (MAIN + TAIL)
            block = jnp.concatenate(
                [grads[c, :, main : main + 128], grads[c, :, main + 256 : main + 384], last], axis=1
            )
            inside = (wide >= base) & (wide < base + MAIN + TAIL)
            total = jnp.where(inside, shifted(block, base, 640), total)
        return total

    up_w[...] = hidden(384, 72)[:, :538]
    down_w_t[...] = hidden(512, 72 + TAIL)[:, :538]
    for load, copy in zip(loads, stores):
        load.wait()
        copy.start()

    def line_up(target, pieces, size, width):
        lane = lax.broadcasted_iota(jnp.int32, (1, width), 1)
        total = jnp.zeros((1, width), FULL)
        for n, piece in enumerate(pieces):
            inside = (lane >= size * n) & (lane < size * (n + 1))
            total = jnp.where(inside, shifted(piece, size * n, width), total)
        for k in range(width // 128):
            target[k : k + 1, :] = total[:, 128 * k : 128 * (k + 1)]

    order = [(t, c) for t in range(8) for c in range(2)]
    line_up(query_b, [totals[c, 3 * t : 3 * t + 1, :] for t, c in order], HEAD_DIM, 1152)
    line_up(value_b, [totals[c, 3 * t + 2 : 3 * t + 3, :] for t, c in order], HEAD_DIM, 1152)
    line_up(
        up_b,
        [
            jnp.concatenate(
                [
                    totals[c, 24 + t : 25 + t, :],
                    totals[c, 32 + t : 33 + t, :],
                    shifted(totals[c, 40:41, :], (128 - TAIL * t) % 128, 128),
                ],
                axis=1,
            )
            for t, c in order
        ],
        MAIN + TAIL,
        34 * 128,
    )
    for n in range(6):
        rows = slice(41 + 9 * n, 50 + 9 * n)
        vectors[n][...] = totals[0, rows, :] + totals[1, rows, :]
    peak = jnp.maximum(totals[0, 96:97, :], totals[1, 96:97, :])
    factor = jnp.sqrt(CLIP_LIMIT / jnp.maximum(peak, CLIP_LIMIT))
    spot = lax.broadcasted_iota(jnp.int32, (1, 128), 1)
    low, high = (
        jnp.sum(jnp.where(spot == 2 * tensor + c, factor, 0.0), axis=1, keepdims=True) for c in range(2)
    )
    scale = jnp.where(lax.broadcasted_iota(jnp.int32, (1, 144), 1) < HEAD_DIM, low, high)
    query_clip[...] = query_weight[...].astype(FULL) * scale
    key_clip[...] = key_weight[...].astype(FULL) * scale
    for copy in stores:
        copy.wait()


def finish(grads, totals, query_weight, key_weight, result, token_grad):
    shapes = [(256, 1152)] * 2 + [(72, 144)] * 3 + [(144, 72), (72, 538), (72, 538)]
    shapes += [(9, 128)] * 2 + [(34, 128)] + [(9, 128)] * 6 + [(72, 144)] * 2
    return pl.pallas_call(
        finish_kernel,
        out_shape=[jax.ShapeDtypeStruct(shape, FULL) for shape in shapes],
        in_specs=[vmem()] * 4 + [hbm()] * 2,
        out_specs=[hbm()] * 2 + [vmem()] * 17,
        scratch_shapes=[pltpu.VMEM((2, 256, 1152), FULL), pltpu.SemaphoreType.DMA((4,))],
        compiler_params=pltpu.CompilerParams(vmem_limit_bytes=60 << 20),
        name="finish_outputs",
    )(grads, totals, query_weight, key_weight, result, token_grad)


def per_device(
    tokens,
    picture,
    cotangent,
    gain_one,
    shift_one,
    query_weight,
    query_bias,
    key_weight,
    value_weight,
    value_bias,
    out_weight,
    out_bias,
    gain_two,
    shift_two,
    up_weight,
    up_bias,
    down_weight,
    down_bias,
):
    row = lax.broadcasted_iota(jnp.int32, (8, tokens.shape[1]), 0)
    consts = jnp.zeros(row.shape, LOW)
    vectors = (out_bias, gain_two, shift_two, down_bias, gain_one, shift_one, query_bias, value_bias)
    for k, vector in enumerate(vectors):
        consts = jnp.where(row == k, vector[None, :], consts)
    consts = consts.astype(FULL)
    weights = (query_weight, key_weight, value_weight, out_weight, up_weight, down_weight.T)
    result, middle_grad, *rest = forward(
        weights, consts, jnp.pad(up_bias.astype(FULL), (0, 48)).reshape(34, 128), picture.reshape(16, 128), cotangent, tokens
    )
    grids, (rows_one_t, head_weights), heads = rest[:3], rest[3:5], rest[5:8]
    heads_grad, both_ids, logsum, peak, sums_hidden, sums = rest[8:]
    input_grad, grads, totals = backward(
        heads_grad,
        heads,
        consts,
        both_ids,
        logsum,
        grids,
        head_weights,
        rows_one_t,
        tokens,
        middle_grad,
        sums_hidden,
        sums,
        peak,
    )
    outputs = finish(grads, totals, query_weight, key_weight, result, input_grad)
    return (
        *outputs[:7],
        outputs[7].T,
        *(vector.reshape(-1) for vector in outputs[8:10]),
        outputs[10].reshape(-1)[: 8 * 538],
        *(vector.reshape(-1) for vector in outputs[11:17]),
        *outputs[17:],
    )


def solution(mesh):
    in_specs = (
        P(("dp", "tensor"), None),
        P("dp"),
        P(("dp", "tensor"), None),
        P(),
        P(),
        P("dp", "tensor"),
        P(),
        P("dp", "tensor"),
        P("dp", "tensor"),
        P(),
        P("tensor", "dp"),
        P(),
        P(),
        P(),
        P("dp", "tensor"),
        P(),
        P("tensor", "dp"),
        P(),
    )
    out_specs = (
        P(("dp", "tensor"), None),
        P(("dp", "tensor"), None),
        P("dp", "tensor"),
        P("dp", "tensor"),
        P("dp", "tensor"),
        P("tensor", "dp"),
        P("dp", "tensor"),
        P("tensor", "dp"),
        P(),
        P(),
        P(),
        P(),
        P(),
        P(),
        P(),
        P(),
        P(),
        P("dp", "tensor"),
        P("dp", "tensor"),
    )
    return jax.shard_map(
        per_device, mesh=mesh, in_specs=in_specs, out_specs=out_specs, check_vma=False
    )
```

```python
import functools

import jax
import jax.numpy as jnp
import numpy as np
from jax import lax
from jax.experimental import pallas as pl
from jax.experimental.pallas import tpu as pltpu
from jax.sharding import PartitionSpec as P

HEAD_DIM = 72
EPSILON = 1e-06
CLIP_LIMIT = 2.0
LOWEST = -1e30
SCALE = HEAD_DIM**-0.5

MESH = pl.DeviceIdType.MESH
LOW = jnp.bfloat16
FULL = jnp.float32

STARTS = (0, 256, 384, 640)
WIDTHS = (256, 128, 256, 256)
STREAMS = ((0, 1), (2,))
UNIT = 896
MAIN = 256
TAIL = 13
HIDDEN = 8 * MAIN + 128
PARTS = ((0, 80, "xy"), (80, 64, "yx"))
PARTS_BEHIND = (
    ((0, 64, "zyx"), (64, 48, "zxy"), (112, 32, "yxz")),
    ((0, 48, "zyx"), (48, 64, "zxy"), (112, 32, "yxz")),
)
PARTS_BACK = ((0, 64, "zyx"), (64, 64, "zxy"), (128, 16, "yxz"))
STEPS = (1, 3, 2)
ALL = "xyz"


def place():
    d, t = lax.axis_index("dp"), lax.axis_index("tensor")
    return {"x": (d // 2) % 4, "y": (t // 4) * 2 + d // 8, "z": t % 4, "core": d % 2}


def device(at):
    return ((at["y"] % 2) * 8 + at["x"] * 2 + at["core"], (at["y"] // 2) * 4 + at["z"])


def moved(at, axis, step):
    other = dict(at)
    other[axis] = 1 - at["core"] if axis == "core" else (at[axis] + step) % 4
    return other


def greet(partners, between=None):
    barrier = pltpu.get_barrier_semaphore()
    for partner in partners:
        pl.semaphore_signal(barrier, inc=1, device_id=device(partner), device_id_type=MESH)
    if between:
        between()
    pl.semaphore_wait(barrier, len(partners))


class Copies:
    def __init__(self, send, receive):
        self.send, self.receive, self.used = send, receive, 0

    def start(self, source, target, partner):
        copy = pltpu.make_async_remote_copy(
            src_ref=source,
            dst_ref=target,
            send_sem=self.send.at[self.used],
            recv_sem=self.receive.at[self.used],
            device_id=device(partner),
            device_id_type=MESH,
        )
        self.used += 1
        copy.start()
        return copy


def lanes(first, size):
    return pl.ds(first if isinstance(first, int) else pl.multiple_of(first, 128), size)


def spots(held, have, at, width, rows, half=None):
    zs, ys = (4 if "z" in held else 1), at["y"] if "y" in held else 0
    x_at = pl.ds(0, 4) if "x" in have else pl.ds(at["x"] if "x" in held else 0, 1)
    y_at = pl.ds(0, 2) if "y" in have else pl.ds(ys % 2, 1)
    z = at["z"] if "z" in held else 0
    if "y" in have and "z" in have:
        ranges = [(0, 8 * width)]
    elif "y" in have:
        ranges = [((h * zs + z) * width, width) for h in (0, 1)]
    elif "z" in have:
        ranges = [((ys // 2) * zs * width, 4 * width)]
    else:
        ranges = [(((ys // 2) * zs + z) * width, width)]
    if half is not None:
        if len(ranges) == 2:
            ranges = [ranges[half]]
        elif "x" in have:
            x_at = pl.ds(2 * half, 2)
        elif "y" in have:
            y_at = pl.ds(half, 1)
        else:
            ((first, size),) = ranges
            ranges = [(first + half * (size // 2), size // 2)]
    return [(y_at, x_at, pl.ds(*rows), lanes(*r)) for r in ranges]


def rect_shape(have, width, rows):
    ys, xs, zs = 2 if "y" in have else 1, 4 if "x" in have else 1, 4 if "z" in have else 1
    return (ys, xs, rows, ys * zs * width)


class Gather:
    def __init__(self, copies, at, grids, widths, part, held=ALL):
        self.copies, self.at, self.grids, self.widths = copies, at, grids, widths
        self.rows, self.order, self.held = part[:2], part[2], held
        self.arriving, self.sent = [], []

    def views(self, grid, width, have, at, half=None):
        return [grid.at[spot] for spot in spots(self.held, have, at, width, self.rows, half)]

    def send(self, have, owner, partner, half=None):
        started = []
        for grid, width in zip(self.grids, self.widths):
            for view in self.views(grid, width, have, owner, half):
                started.append(self.copies.start(view, view, partner))
        self.sent += started
        return started

    def settle(self):
        for copy in self.arriving:
            copy.wait_recv()
        self.arriving = []

    def first(self):
        for step in STEPS:
            self.arriving += self.send("", self.at, moved(self.at, self.order[0], step))

    def ring(self, phase):
        self.settle()
        axis, have = self.order[phase], self.order[:phase]
        self.after = self.send(have, self.at, moved(self.at, axis, 1))
        self.before = self.send(have, self.at, moved(self.at, axis, 3))

    def forward(self, phase):
        axis, have = self.order[phase], self.order[:phase]
        up, down = moved(self.at, axis, 1), moved(self.at, axis, 3)
        for copy in self.after:
            copy.wait_recv()
        self.arriving += self.send(have, down, up, 0)
        for copy in self.before:
            copy.wait_recv()
        self.arriving += self.send(have, up, down, 1)


def add_into(target, terms, shape):
    @pl.loop(0, shape[0] * shape[1] * (shape[2] // 16))
    def _(n):
        block = n // (shape[2] // 16)
        spot = (
            block // shape[1],
            block % shape[1],
            pl.ds(pl.multiple_of((n % (shape[2] // 16)) * 16, 16), 16),
            slice(None),
        )
        total = terms[0][spot].astype(FULL)
        for term in terms[1:]:
            total = total + term[spot].astype(FULL)
        target[spot] = total.astype(target.dtype)


def half_shape(have, shape):
    ys, xs, rows, cols = shape
    if "y" in have and "z" not in have:
        return (ys, xs, rows, cols // 2)
    if "x" in have:
        return (ys, 2, rows, cols)
    if "y" in have:
        return (1, xs, rows, cols)
    return (ys, xs, rows, cols // 2)


class Scatter:
    @staticmethod
    def shapes(widths, part, loaded):
        _, rows, order = part
        shapes = []
        for phase in range(len(order) - 1):
            have = order[: len(order) - 1 - phase]
            for _ in range(5 if loaded and phase == 0 else 4):
                shapes += [pltpu.VMEM(rect_shape(have, w, rows), LOW) for w in widths]
        shapes += [pltpu.VMEM((3, 1, 1, rows, w), LOW) for w in widths]
        return shapes

    def __init__(self, copies, at, grids, widths, part, buffers, held=ALL, local=None):
        self.copies, self.at, self.grids, self.widths = copies, at, grids, widths
        self.rows, self.order = part[:2], part[2]
        self.rings = len(self.order) - 1
        self.held = [held] + [self.order[: self.rings - phase] for phase in range(self.rings)]
        self.local = local
        self.sent = []

        def take():
            taken, buffers[:] = buffers[: len(widths)], buffers[len(widths) :]
            return taken

        self.near, self.low, self.high, self.own = [], [], [], []
        for phase in range(self.rings):
            for group in (self.near, self.low, self.high, self.own):
                group.append(take())
            if phase == 0 and local:
                self.mix = [take()]
        self.direct = take()

    def have(self, phase):
        return self.order[: self.rings - phase]

    def source(self, phase, a, at, half=None):
        grid = self.grids[a] if phase == 0 else self.own[phase - 1][a]
        rows = self.rows if phase == 0 else (0, self.rows[1])
        found = spots(self.held[phase], self.have(phase), at, self.widths[a], rows, half)
        return [grid.at[spot] for spot in found]

    def target(self, phase, buffer, a, half=None):
        have = self.have(phase)
        found = spots(have, have, self.at, self.widths[a], (0, self.rows[1]), half)
        return [buffer[phase][a].at[spot] for spot in found]

    def push(self, sources, targets, partner):
        started = [self.copies.start(s, t, partner) for s, t in zip(sources, targets)]
        self.sent += started
        return started

    def begin(self, phase):
        axis = self.order[self.rings - phase]
        up, down, far = (moved(self.at, axis, step) for step in STEPS)
        self.arriving, self.loading = [], []
        for a in range(len(self.grids)):
            for half, partner in ((0, up), (1, down)):
                self.arriving += self.push(
                    self.source(phase, a, far, half),
                    self.target(phase, self.near, a, half),
                    partner,
                )
        if phase == 0 and self.local:
            for a in range(len(self.grids)):
                pairs = list(
                    zip(
                        self.source(0, a, up, 0) + self.source(0, a, down, 1),
                        self.target(0, self.mix, a, 0) + self.target(0, self.mix, a, 1),
                    )
                )
                pairs += list(zip(self.source(0, a, self.at), self.target(0, self.own, a)))
                for view, target in pairs:
                    copy = pltpu.make_async_copy(view, target, self.local[0].at[self.local[1]])
                    self.local[1] += 1
                    copy.start()
                    self.loading.append(copy)

    def relay(self, phase):
        axis, have = self.order[self.rings - phase], self.have(phase)
        up, down, _ = (moved(self.at, axis, step) for step in STEPS)
        for copy in self.loading:
            copy.wait()
        for copy in self.arriving:
            copy.wait_recv()
        self.arriving = []
        for a in range(len(self.grids)):
            shape = half_shape(have, rect_shape(have, self.widths[a], self.rows[1]))
            for half, partner in ((0, up), (1, down)):
                (near,) = self.target(phase, self.near, a, half)
                if phase == 0 and self.local:
                    (view,) = self.target(phase, self.mix, a, half)
                else:
                    (view,) = self.source(phase, a, partner, half)
                add_into(near, [view, near], shape)
                buffer = self.low if half == 0 else self.high
                self.arriving += self.push(
                    [near] + self.source(phase, a, partner, 1 - half),
                    self.target(phase, buffer, a, half) + self.target(phase, buffer, a, 1 - half),
                    partner,
                )

    def finish(self, phase):
        have = self.have(phase)
        for copy in self.arriving:
            copy.wait_recv()
        for a in range(len(self.grids)):
            for low, high, own, source in zip(
                self.target(phase, self.low, a),
                self.target(phase, self.high, a),
                self.target(phase, self.own, a),
                self.source(phase, a, self.at),
            ):
                shape = rect_shape(have, self.widths[a], self.rows[1])
                if "y" in have and "z" not in have:
                    shape = half_shape(have, shape)
                add_into(own, [own if phase == 0 and self.local else source, low, high], shape)

    def last(self):
        self.arriving = []
        for k, step in enumerate(STEPS):
            partner = moved(self.at, self.order[0], step)
            for a in range(len(self.grids)):
                self.arriving += self.push(
                    self.source(self.rings, a, partner), [self.direct[a].at[k]], partner
                )

    def result(self, out, starts):
        for copy in self.arriving:
            copy.wait_recv()
        for a, start in enumerate(starts):
            (mine,) = self.source(self.rings, a, self.at)
            total = mine[0, 0].astype(FULL)
            for k in range(3):
                total = total + self.direct[a][k, 0, 0].astype(FULL)
            out[pl.ds(*self.rows), start : start + self.widths[a]] = total


def hbm():
    return pl.BlockSpec(memory_space=pltpu.HBM)


def anywhere():
    return pl.BlockSpec(memory_space=pl.ANY)


def vmem():
    return pl.BlockSpec(memory_space=pltpu.VMEM)


def picker():
    row = lax.broadcasted_iota(jnp.int32, (256, 384), 0)
    lane = lax.broadcasted_iota(jnp.int32, (256, 384), 1)
    hit = ((lane & 127) < HEAD_DIM) & (row == (lane >> 7) * HEAD_DIM + (lane & 127))
    return jnp.where(hit, 1.0, 0.0).astype(LOW)


def dot(left, right):
    return jnp.dot(left, right, preferred_element_type=FULL)


def dot_rows(left, right):
    return lax.dot_general(left, right, (((0,), (0,)), ((), ())), preferred_element_type=FULL)


def dot_cols(left, right):
    return lax.dot_general(left, right, (((1,), (1,)), ((), ())), preferred_element_type=FULL)


def set_ids(ids, r, ids_row, ids_col):
    eye = lax.broadcasted_iota(jnp.int32, (128, 128), 0) == lax.broadcasted_iota(
        jnp.int32, (128, 128), 1
    )
    for k in range(8):
        piece = ids[8 * r + k : 8 * r + k + 1, :]
        ids_row[r, :, k * 128 : (k + 1) * 128] = piece
        ids_col[r, k * 128 : (k + 1) * 128, :] = jnp.sum(
            jnp.where(eye, piece, 0.0), axis=1, keepdims=True
        )


def selector(offset):
    row = lax.broadcasted_iota(jnp.int32, (1024, 128), 0)
    lane = lax.broadcasted_iota(jnp.int32, (1024, 128), 1)
    inner = (row & 127) - offset
    hit = (inner >= 0) & (inner < TAIL) & (lane == (row >> 7) * TAIL + inner)
    return jnp.where(hit, 1.0, 0.0).astype(LOW)


def smooth(inner):
    root = 0.7978845608028654
    square = inner * inner
    wave = jnp.tanh(root * inner * (1.0 + 0.044715 * square))
    up = 0.5 * (1.0 + wave)
    slope = up + 0.5 * inner * (1.0 - wave * wave) * root * (1.0 + 3 * 0.044715 * square)
    return inner * up, slope


def mean(values):
    return jnp.sum(values, axis=1, keepdims=True) * (1.0 / values.shape[1])


def column_sum(values):
    return jnp.sum(values.astype(FULL), axis=0, keepdims=True)


def shifted(values, amount, width):
    if values.shape[1] < width:
        pad = jnp.zeros((values.shape[0], width - values.shape[1]), FULL)
        values = jnp.concatenate([values, pad], axis=1)
    return pltpu.roll(values, amount, 1) if amount else values


def widened(values, width):
    pad = jnp.zeros((values.shape[0], width - values.shape[1]), FULL)
    return jnp.concatenate([values.astype(FULL), pad], axis=1)


def pack_half(half, query, key, value, out_t, up, down_t, pack):
    lane = lax.broadcasted_iota(jnp.int32, (72, 256), 1)
    total = jnp.zeros((72, 256), FULL)
    for k, weight in enumerate((query, key, value)):
        spot = HEAD_DIM * k
        block = pltpu.roll(weight, (spot - HEAD_DIM * half) % 256, 1)
        total = jnp.where((lane >= spot) & (lane < spot + HEAD_DIM), block, total)
    pack[half, :, 0:256] = total
    first = half * (MAIN + TAIL)
    lane = lax.broadcasted_iota(jnp.int32, (72, 128), 1)
    total = jnp.where(lane < HEAD_DIM, pltpu.roll(out_t, (-HEAD_DIM * half) % 256, 1)[:, :128], 0.0)
    for k, weight in enumerate((up, down_t)):
        spot = HEAD_DIM + TAIL * k
        block = pltpu.roll(weight, (spot - first - MAIN) % 640, 1)[:, :128]
        total = jnp.where((lane >= spot) & (lane < spot + TAIL), block, total)
        block = pltpu.roll(weight, (-first) % 640, 1) if half else weight
        pack[half, :, 384 + 128 * k : 512 + 128 * k] = block[:, :128]
        pack[half, :, 640 + 128 * k : 768 + 128 * k] = block[:, 128:256]
    pack[half, :, 256:384] = total


def set_biases(core, z, consts, up_bias, hidden_bias):
    lane = lax.broadcasted_iota(jnp.int32, (1, 128), 1)
    pieces = []
    for j in range(2):
        for k in (6, None, 7):
            total = jnp.zeros((1, 128), FULL)
            if k is not None:
                for head in range(16):
                    block = shifted(consts[k : k + 1, :], (-HEAD_DIM * head) % 1152, 1152)[:, :128]
                    total = jnp.where(head == 8 * j + 2 * z + core, block, total)
            pieces.append(jnp.where(lane < HEAD_DIM, total, 0.0))
    line = jnp.concatenate([up_bias[k : k + 1, :] for k in range(34)], axis=1)
    line = jnp.where(core == 0, line, pltpu.roll(line, 34 * 128 - MAIN - TAIL, 1))
    tails = jnp.zeros((1, 128), FULL)
    for t in range(8):
        row = shifted(line, (-2 * (MAIN + TAIL) * t) % (34 * 128), 34 * 128)
        hidden_bias[:, t * 128 : (t + 1) * 128] = row[:, 0:128]
        hidden_bias[:, 1024 + t * 128 : 1152 + t * 128] = row[:, 128:256]
        tail = shifted(row[:, 256:384], TAIL * t, 128)
        tails = jnp.where((lane >= TAIL * t) & (lane < TAIL * (t + 1)), tail, tails)
    hidden_bias[:, 2048:HIDDEN] = tails
    return jnp.concatenate(pieces, axis=1)


def forward_kernel(
    query, key, value, out_weight, up_weight, down_weight_t, consts, up_bias, picture, cot, tokens,
    result_out, middle_grad_out, dout, dffn_a, dffn_b, n1t_out, weights_out, q_out, k_out, v_out, heads_grad, both_ids,
    logsum, peak, sums_hidden, sums,
    both, unit, slab, go, ffn_a, ffn_b, n1_all, ids_row, ids_col, vt_s, out_s, top_s, cot_rows, mixed,
    ut, dt, n2, n2t, ct, acc2, acc3, xhat, bg, out1, out2, in1, in2, in3, ids, hidden_bias, pack, q_s, k_s, v_s,
    weights, result, middle_grad, mixed_grad, send, receive, local,
):
    at = place()
    core, z = at["core"], at["z"]
    sibling = moved(at, "core", 1)
    up, down, far = (moved(at, "z", step) for step in STEPS)
    grids = (go, ffn_a, ffn_b)
    cot_own = pltpu.make_async_copy(cot, cot_rows.at[pl.ds(0, 256)], local.at[1])
    cot_own.start()

    def pack_weights():
        wide = [widened(w[...], 256) for w in (query, key, value)]
        wide.append(widened(out_weight[...].astype(FULL).T, 256))
        wide += [widened(w[...], 640) for w in (up_weight, down_weight_t)]
        for half in range(2):
            pack_half(half, *wide, pack)

    greet([sibling] + [moved(at, axis, step) for axis in ALL for step in STEPS], pack_weights)
    copies = Copies(send, receive)
    sent = []

    def start(source, target, partner):
        copy = copies.start(source, target, partner)
        sent.append(copy)
        return copy

    mine = pl.ds(pl.multiple_of(core * 72, 8), 72)
    first_copy = start(pack.at[1 - core], both.at[mine], sibling)
    half_row = pl.ds(pl.multiple_of((at["y"] // 2) * 8, 8), 8)
    numbers = picture[half_row, :]
    slot = lax.broadcasted_iota(jnp.int32, (8, 128), 0) * 128 + lax.broadcasted_iota(jnp.int32, (8, 128), 1)
    ids[...] = jnp.where(numbers >= 0, numbers, -1 - slot).astype(FULL)
    ids_copy = start(ids, both_ids.at[pl.ds(8, 8)], sibling)
    both_ids[0:8, :] = ids[...]
    out_bias, gain, shift, down_bias, gain_first, shift_first = (consts[k : k + 1, :] for k in range(6))

    def block(owner, r, first=0, size=256):
        return n1_all.at[owner["z"], pl.ds(r * 256 + first, size)]

    def ring_step(first):
        return [
            start(block(at, 0, first, 128), block(at, 0, first, 128), partner) for partner in (up, down)
        ]

    both[mine, :] = pack[core]
    values = tokens[...].astype(FULL)
    centre = values - mean(values)
    inverse = lax.rsqrt(mean(centre * centre) + EPSILON)
    n1_all[z, 0:256, :] = (centre * inverse * gain_first + shift_first).astype(LOW)
    ring = [ring_step(0)]
    other = {0: start(block(at, 0), block(at, 1), sibling)}
    cot_copy = start(cot, cot_rows.at[pl.ds(256, 256)], sibling)
    first_copy.wait_recv()
    unit[...] = both[...].astype(LOW)
    tensor = (at["y"] // 2) * 4 + z
    slab[at["y"] % 2, at["x"], :, lanes((at["y"] // 2) * 256, 256)] = unit[:, 0:256]
    for grid, first, width in zip(grids, STARTS[1:], WIDTHS[1:]):
        grid[at["y"] % 2, at["x"], :, lanes(tensor * width, width)] = unit[:, first : first + width]
    ahead = [Gather(copies, at, [slab], [256], part, "xy") for part in PARTS]
    behind = [
        [
            Gather(copies, at, [grids[n] for n in names], [WIDTHS[n + 1] for n in names], part)
            for part in parts
        ]
        for names, parts in zip(STREAMS, PARTS_BEHIND)
    ]

    def step(group, name, *phase):
        for g in group:
            getattr(g, name)(*phase)

    step(ahead, "first")
    for group in behind:
        step(group[2:] + group[:2], "first")
    ring.append(ring_step(128))
    ids_copy.wait_recv()
    set_ids(ids, 0, ids_row, ids_col)
    set_ids(both_ids, 1, ids_row, ids_col)
    step(ahead, "ring", 1)
    bias = set_biases(core, z, consts, up_bias, hidden_bias)
    ring[0][0].wait_recv()
    halves = [start(block(down, 0, 0, 128), block(down, 0, 0, 128), up)]
    step(ahead, "forward", 1)
    step(behind[0], "ring", 1)
    step(behind[1], "ring", 1)
    step(ahead, "settle")
    for j in range(2):
        packed = slab[:, :, :, j * 256 : (j + 1) * 256].reshape(1152, 256)
        weights[:, j * 384 : (j + 1) * 384] = dot(packed, picker()).astype(LOW)

    def project(owner, r):
        rows = pl.ds(pl.multiple_of(owner["z"] * 256, 256), 256)
        product = (dot(n1_all[owner["z"], r * 256 : (r + 1) * 256, :], weights[...]) + bias).astype(LOW)
        for j in range(2):
            for k, target in enumerate((q_s, k_s, v_s)):
                first_lane = j * 384 + k * 128
                target[2 * r + j, rows, :] = product[:, first_lane : first_lane + 128]

    project(at, 0)
    ring[1][1].wait_recv()
    halves.append(start(block(up, 0, 128, 128), block(up, 0, 128, 128), down))
    ring[0][1].wait_recv()
    other[2] = start(block(up, 0), block(up, 1), sibling)
    ring[1][0].wait_recv()
    other[1] = start(block(down, 0), block(down, 1), sibling)
    step(behind[0], "forward", 1)
    other[0].wait_recv()
    project(at, 1)
    step(behind[1], "forward", 1)
    step(behind[0], "ring", 2)
    project(down, 0)
    project(up, 0)
    step(behind[1], "ring", 2)
    other[1].wait_recv()
    project(down, 1)
    other[2].wait_recv()
    project(up, 1)
    for copy in halves:
        copy.wait_recv()
    other[3] = start(block(far, 0), block(far, 1), sibling)
    project(far, 0)
    other[3].wait_recv()
    project(far, 1)
    stores = [
        pltpu.make_async_copy(source, target, local.at[16 + k])
        for k, (source, target) in enumerate(
            ((q_s, q_out), (k_s, k_out), (v_s, v_out), (weights, weights_out))
        )
    ]
    for copy in stores:
        copy.start()
    for n in range(4):
        vt_s[n] = v_s[n].T
    top_s[...] = jnp.full(top_s.shape, LOWEST, FULL)
    back = []
    for k, hop in enumerate(STEPS + (0,)):
        b = (z + hop) % 4
        rows = pl.ds(pl.multiple_of(b * 256, 256), 256)

        @pl.loop(0, 4)
        def _(n, b=b, rows=rows):
            r = n // 2
            scores = dot_cols(k_s[n], q_s[n, rows, :]) * SCALE
            query_ids = ids_row[r, :, rows]
            scores = jnp.where(ids_col[r] == query_ids, scores, LOWEST)
            top = jnp.max(scores, axis=0, keepdims=True)
            expo = jnp.exp(scores - top)
            total = jnp.sum(expo, axis=0, keepdims=True)
            weights_low = (expo * (1.0 / total)).astype(LOW)
            out_s[n, b] = dot(vt_s[n], weights_low).T.astype(LOW)
            logsum[n, :, rows] = top + jnp.log(total)
            top_s[n] = jnp.maximum(top_s[n], jnp.where(query_ids >= 0.0, top, LOWEST))

        for n in range(4):
            r, j = n // 2, n % 2
            source = out_s.at[n, b]
            spot = (pl.ds(r * 256, 256), lanes((4 * j + z) * 128, 128))
            if hop:
                back.append(start(source, mixed.at[spot], moved(at, "z", hop)))
            else:
                copy = pltpu.make_async_copy(source, mixed.at[spot], local.at[2 + n])
                copy.start()
                stores.append(copy)
    row = lax.broadcasted_iota(jnp.int32, (8, 128), 0)
    high = [jnp.maximum(jnp.max(top_s[j]), jnp.max(top_s[2 + j])) for j in range(2)]
    peak[...] = jnp.where(row == 0, high[0], high[1])
    step(behind[0], "forward", 2)
    cot_own.wait()
    cot_copy.wait_recv()
    turned = []
    for k in range(4):
        if k >= 2:
            turned[k - 2].wait()
        buffer = (n2t, ct)[k % 2]
        buffer[...] = n1_all[k].T
        copy = pltpu.make_async_copy(buffer, n1t_out.at[:, pl.ds(512 * k, 512)], local.at[22 + k])
        copy.start()
        turned.append(copy)
    step(behind[1], "forward", 2)
    step(behind[0], "settle")
    for copy in turned[2:]:
        copy.wait()
    ct[...] = cot_rows[...].T
    ut[...] = dot(go[...].reshape(1152, 1024), selector(72)).astype(LOW)
    dt[...] = dot(go[...].reshape(1152, 1024), selector(72 + TAIL)).astype(LOW)
    acc2[...] = jnp.zeros(acc2.shape, FULL)
    acc3[...] = jnp.zeros(acc3.shape, FULL)
    for copy in back:
        copy.wait_recv()
    for copy in stores:
        copy.wait()
    stores = []

    def store(source, target, semaphore):
        copy = pltpu.make_async_copy(source, target, local.at[semaphore])
        copy.start()
        stores.append(copy)


    upper_half, lower_half = slice(0, 256), slice(256, 512)
    quarters = [slice(k * 256, (k + 1) * 256) for k in range(4)]

    def branch_part(rows):
        return dot_cols(mixed[rows, :], go[...].reshape(1152, 1024))

    out1[...] = branch_part(lower_half).astype(LOW)
    branch = copies.start(out1, in1, sibling)
    middle = branch_part(upper_half) + tokens[...].astype(FULL) + out_bias
    branch.wait_recv()
    middle = middle + in1[...].astype(FULL)
    result[...] = middle + down_bias
    centre = middle - mean(middle)
    inverse = lax.rsqrt(mean(centre * centre) + EPSILON)
    scaled = centre * inverse
    xhat[...] = scaled
    n2[upper_half, :] = (scaled * gain + shift).astype(LOW)
    normed = start(n2.at[pl.ds(0, 256)], n2.at[pl.ds(256, 256)], sibling)
    normed.wait_recv()
    n2t[...] = n2[...].T

    def hidden_block(u, d, block_bias):
        active, slope = smooth(dot(n2[...], u) + block_bias)
        upper = (dot(cot_rows[...], d) * slope).astype(LOW)
        active = active.astype(LOW)
        acc2[...] += dot_cols(active, d)
        acc3[...] += dot_cols(upper, u)
        return active, upper

    def grad_copy(ref, out, f, first):
        cols = lanes(f * 512, 512)
        return pltpu.make_async_copy(ref.at[:, :, :, cols], out.at[:, :, :, cols], local.at[first + f])

    streams = ((ffn_a, dffn_a, 7), (ffn_b, dffn_b, 11))
    for k, (ref, out, first) in enumerate(streams):
        step(behind[k], "settle")
        for g in behind[k]:
            for copy in g.sent:
                copy.wait_send()

        @pl.loop(0, 4)
        def _(f, k=k, ref=ref, out=out, first=first):
            def piece(n):
                return lanes(f * 512 + n * 128, 128)

            def columns(n):
                return jnp.concatenate(
                    [ref[:, :, :, piece(m)].reshape(1152, 128) for m in (n, n + 2)], axis=1
                )

            hidden_cols = lanes(k * 1024 + f * 256, 256)
            active, upper = hidden_block(columns(0), columns(1), hidden_bias[:, hidden_cols])
            sums_hidden[:, hidden_cols] = column_sum(upper)
            for n, grad in enumerate((dot(n2t[...], upper).astype(LOW), dot(ct[...], active).astype(LOW))):
                ref[:, :, :, piece(n)] = grad[:, :128].reshape(2, 4, 144, 128)
                ref[:, :, :, piece(n + 2)] = grad[:, 128:].reshape(2, 4, 144, 128)
            grad_copy(ref, out, f, first).start()

    active, upper = hidden_block(ut[...], dt[...], hidden_bias[:, 2048:HIDDEN])
    sums_hidden[:, 2048:HIDDEN] = column_sum(upper)
    branch.wait_send()
    out1[...] = acc3[lower_half, :].astype(LOW)
    return_copy = start(out1, in3, sibling)
    out2[...] = acc2[lower_half, :].astype(LOW)
    forth = start(out2, in2, sibling)
    up_tail = dot_cols(upper, selector(72)).astype(LOW)
    down_tail = dot_cols(active, selector(72 + TAIL)).astype(LOW)
    upstream = cot_rows[upper_half, :].astype(FULL)
    return_copy.wait_recv()
    normed_grad = acc3[upper_half, :] + in3[...].astype(FULL)
    scaled = xhat[...]
    along = normed_grad * gain
    grad = upstream + inverse * (along - mean(along) - scaled * mean(along * scaled))
    middle_grad[...] = grad
    store(middle_grad, middle_grad_out, 20)
    low = grad.astype(LOW)
    bg[upper_half, :] = low
    branch_grad = start(bg.at[pl.ds(0, 256)], bg.at[pl.ds(256, 256)], sibling)
    sums[0:1, :] = column_sum(low)
    sums[1:2, :] = column_sum(upstream)
    sums[2:3, :] = column_sum(normed_grad * scaled)
    sums[3:4, :] = column_sum(normed_grad)
    sums[4:8, :] = jnp.zeros((4, 1152), FULL)
    forth.wait_recv()
    result[...] += acc2[upper_half, :] + in2[...].astype(FULL)
    store(result, result_out, 21)
    branch_grad.wait_recv()
    for cols in quarters:
        mixed_grad[:, cols] = dot(bg[...], go[:, :, :, cols].reshape(1152, 256)).astype(LOW)
    heads_back = []
    for j in range(2):
        spot = pl.ds(j * 128, 128)
        for partner in (up, down, far):
            source = mixed_grad.at[:, lanes((4 * j + partner["z"]) * 128, 128)]
            heads_back.append(start(source, heads_grad.at[z, :, spot], partner))
        heads_grad[z, :, spot] = mixed_grad[:, lanes((4 * j + z) * 128, 128)]
    for cols in quarters:
        go[:, :, :, cols] = (
            (
                dot(n2t[...], up_tail[:, cols])
                + dot(ct[...], down_tail[:, cols])
                + dot_rows(bg[...], mixed[:, cols])
            )
            .astype(LOW)
            .reshape(2, 4, 144, 256)
        )
    last = pltpu.make_async_copy(go, dout, local.at[15])
    last.start()
    for ref, out, first in streams:
        for n in range(4):
            grad_copy(ref, out, n, first).wait()
    last.wait()
    for copy in stores:
        copy.wait()
    for copy in heads_back:
        copy.wait_recv()
    for copy in sent + [copy for g in ahead for copy in g.sent]:
        copy.wait_send()


def forward(weights, consts, up_bias, picture, cot, tokens):
    count = 12 + 12 + 5 + 6 + 2 * 15 + 3 * 45
    grids = [(2, 4, 144, 8 * w) for w in WIDTHS[1:]]
    rows, half = (512, 1152), (256, 1152)
    return pl.pallas_call(
        forward_kernel,
        out_shape=[
            jax.ShapeDtypeStruct(half, FULL),
            jax.ShapeDtypeStruct(half, FULL),
        ]
        + [jax.ShapeDtypeStruct(grid, LOW) for grid in grids]
        + [
            jax.ShapeDtypeStruct((1152, 2048), LOW),
            jax.ShapeDtypeStruct((1152, 768), LOW),
        ]
        + [jax.ShapeDtypeStruct((4, 1024, 128), LOW)] * 3
        + [
            jax.ShapeDtypeStruct((4, 512, 256), LOW),
            jax.ShapeDtypeStruct((16, 128), FULL),
            jax.ShapeDtypeStruct((4, 1, 1024), FULL),
            jax.ShapeDtypeStruct((8, 128), FULL),
            jax.ShapeDtypeStruct((1, HIDDEN), FULL),
            jax.ShapeDtypeStruct((8, 1152), FULL),
        ],
        in_specs=[vmem()] * 9 + [anywhere(), vmem()],
        out_specs=[hbm()] * 10 + [vmem()] * 6,
        scratch_shapes=[
            pltpu.VMEM((144, UNIT), FULL),
            pltpu.VMEM((144, UNIT), LOW),
            pltpu.VMEM((2, 4, 144, 512), LOW),
        ]
        + [pltpu.VMEM(grid, LOW) for grid in grids]
        + [
            pltpu.VMEM((4, 512, 1152), LOW),
            pltpu.VMEM((2, 1, 1024), FULL),
            pltpu.VMEM((2, 1024, 1), FULL),
            pltpu.VMEM((4, 128, 1024), LOW),
            pltpu.VMEM((4, 4, 256, 128), LOW),
            pltpu.VMEM((4, 1, 256), FULL),
            pltpu.VMEM(rows, LOW),
            pltpu.VMEM((512, 1024), LOW),
            pltpu.VMEM((1152, 128), LOW),
            pltpu.VMEM((1152, 128), LOW),
            pltpu.VMEM(rows, LOW),
            pltpu.VMEM((1152, 512), LOW),
            pltpu.VMEM((1152, 512), LOW),
            pltpu.VMEM(rows, FULL),
            pltpu.VMEM(rows, FULL),
            pltpu.VMEM(half, FULL),
            pltpu.VMEM(rows, LOW),
        ]
        + [pltpu.VMEM(half, LOW)] * 5
        + [
            pltpu.VMEM((8, 128), FULL),
            pltpu.VMEM((1, HIDDEN), FULL),
            pltpu.VMEM((2, 72, UNIT), FULL),
        ]
        + [pltpu.VMEM((4, 1024, 128), LOW)] * 3
        + [
            pltpu.VMEM((1152, 768), LOW),
            pltpu.VMEM(half, FULL),
            pltpu.VMEM(half, FULL),
            pltpu.VMEM((512, 1024), LOW),
            pltpu.SemaphoreType.DMA((count,)),
            pltpu.SemaphoreType.DMA((count,)),
            pltpu.SemaphoreType.DMA((26,)),
        ],
        compiler_params=pltpu.CompilerParams(
            collective_id=0, has_side_effects=True, vmem_limit_bytes=60 << 20
        ),
        name="forward_attention",
    )(*weights, consts, up_bias, picture, cot, tokens)


def backward_kernel(
    grad, q, k, v, consts, both_ids, logsum, dout, dffn_a, dffn_b, weights, n1t, tokens,
    middle, sums_hidden, sums, peak, token_grad, out, totals, *rest
):
    (
        q_s, k_s, v_s, w_s, middle_grad, g_s, n1t_s, kt_s, dk_s, dv_s, proj_grad, ids_row, ids_col, part_out, part_in,
        part_own, near, low, high, dslab, unit, other, line, near_lines, send, receive, local,
    ) = rest[:27]
    buffers = list(rest[27:])
    at = place()
    z, core = at["z"], at["core"]
    sibling = moved(at, "core", 1)
    up, down, far = [moved(at, "z", step) for step in STEPS]
    loads = [
        pltpu.make_async_copy(source, target, local.at[n])
        for n, (source, target) in enumerate(
            ((k, k_s), (q, q_s), (v, v_s), (weights, w_s), (n1t, n1t_s), (middle, middle_grad))
        )
    ]
    for copy in loads:
        copy.start()
    greet([sibling] + [moved(at, axis, step) for axis in ALL for step in STEPS])
    copies = Copies(send, receive)
    sent = []

    def start(source, target, partner):
        copy = copies.start(source, target, partner)
        sent.append(copy)
        return copy

    counter, grids = [local, 7], (dout, dffn_a, dffn_b)
    behind = [
        Scatter(copies, at, [grids[n] for n in names], [WIDTHS[n + 1] for n in names], part, buffers, ALL, counter)
        for names in STREAMS
        for part in PARTS_BACK
    ]
    last = [Scatter(copies, at, [dslab], [256], part, buffers, "xy") for part in PARTS]
    for s in behind:
        s.begin(0)
    set_ids(both_ids, 0, ids_row, ids_col)
    set_ids(both_ids, 1, ids_row, ids_col)
    for copy in loads[:3]:
        copy.wait()
    for n in range(4):
        kt_s[n] = k_s[n].T
    lane = lax.broadcasted_iota(jnp.int32, (256, 128), 1)
    for r in range(2):
        for j in range(2):
            for b in range(4):
                block = grad[b, r * 256 : (r + 1) * 256, j * 128 : (j + 1) * 128]
                g_s[2 * r + j, b * 256 : (b + 1) * 256, :] = jnp.where(
                    lane < HEAD_DIM, block.astype(FULL), 0.0
                ).astype(LOW)

    def heads_back(r):
        dk_s[...] = jnp.zeros(dk_s.shape, FULL)
        dv_s[...] = jnp.zeros(dv_s.shape, FULL)

        @pl.loop(0, 4)
        def _(b):
            rows = pl.ds(pl.multiple_of(b * 256, 256), 256)
            spot = pl.ds(pl.multiple_of(b * 512 + r * 256, 256), 256)
            allowed = ids_col[r] == ids_row[r, :, rows]
            for j in range(2):
                n = 2 * r + j
                query, upper = q_s[n, rows, :], g_s[n, rows, :]
                scores = dot_cols(k_s[n], query) * SCALE
                probs = jnp.where(allowed, jnp.exp(scores - logsum[n, :, rows]), 0.0)
                dv_s[j] += dot(probs.astype(LOW), upper)
                prob_grad = dot_cols(v_s[n], upper)
                centre = jnp.sum(probs * prob_grad, axis=0, keepdims=True)
                score_grad = (probs * (prob_grad - centre)).astype(LOW)
                proj_grad[spot, j * 384 : j * 384 + 128] = (
                    (dot(kt_s[n], score_grad) * SCALE).T.astype(LOW)
                )
                dk_s[j] += dot(score_grad, query)

        for j in range(2):
            for b in range(4):
                spot = slice(b * 512 + r * 256, b * 512 + (r + 1) * 256)
                rows = slice(b * 256, (b + 1) * 256)
                proj_grad[spot, j * 384 + 128 : j * 384 + 256] = (dk_s[j, rows, :] * SCALE).astype(LOW)
                proj_grad[spot, j * 384 + 256 : j * 384 + 384] = dv_s[j, rows, :].astype(LOW)

    def part(owner, r):
        spot = pl.ds(pl.multiple_of(owner["z"] * 512 + r * 256, 256), 256)
        return dot_cols(proj_grad[spot, :], w_s[...])

    heads_back(1)
    for copy in loads[3:]:
        copy.wait()
    swapped = []
    for owner in (far, up, down, at):
        n = owner["z"]
        part_out[n] = part(owner, 1).astype(LOW)
        swapped.append(copies.start(part_out.at[n], part_in.at[n], sibling))
    for s in behind:
        s.relay(0)
    heads_back(0)

    def summed(owner, copy):
        copy.wait()
        return part(owner, 0) + part_in[owner["z"]].astype(FULL)

    half_a, half_b = pl.ds(0, 128), pl.ds(128, 128)
    part_out[far["z"]] = summed(far, swapped[0]).astype(LOW)
    arriving = [
        start(part_out.at[far["z"], half_a], near.at[half_a], up),
        start(part_out.at[far["z"], half_b], near.at[half_b], down),
    ]
    part_out[up["z"]] = summed(up, swapped[1]).astype(LOW)
    part_out[down["z"]] = summed(down, swapped[2]).astype(LOW)
    part_own[...] = summed(at, swapped[3])
    for copy in arriving:
        copy.wait_recv()
    near[0:128, :] = (near[0:128, :].astype(FULL) + part_out[up["z"], 0:128, :].astype(FULL)).astype(LOW)
    near[128:256, :] = (
        near[128:256, :].astype(FULL) + part_out[down["z"], 128:256, :].astype(FULL)
    ).astype(LOW)
    arriving = [
        start(near.at[half_a], low.at[half_a], up),
        start(part_out.at[up["z"], half_b], low.at[half_b], up),
        start(near.at[half_b], high.at[half_b], down),
        start(part_out.at[down["z"], half_a], high.at[half_a], down),
    ]
    for n in range(3):
        cols = slice(n * 256, (n + 1) * 256)
        w_s[:, cols] = dot(n1t_s[...], proj_grad[:, cols]).astype(LOW)
    for j in range(2):
        dslab[:, :, :, j * 256 : (j + 1) * 256] = (
            dot_cols(w_s[:, j * 384 : (j + 1) * 384], picker()).astype(LOW).reshape(2, 4, 144, 256)
        )
    for s in last:
        s.begin(0)
    projected = column_sum(proj_grad[...])
    values = tokens[...].astype(FULL)
    centre = values - mean(values)
    inverse = lax.rsqrt(mean(centre * centre) + EPSILON)
    token_grad[...] = centre * inverse
    for s in behind:
        s.finish(0)
        s.begin(1)
    for s in last:
        s.relay(0)
    for copy in arriving:
        copy.wait_recv()
    normed_grad = part_own[...] + low[...].astype(FULL) + high[...].astype(FULL)
    scaled = token_grad[...]
    along = normed_grad * consts[4:5, :]
    token_grad[...] = middle_grad[...] + inverse * (
        along - mean(along) - scaled * mean(along * scaled)
    )
    for t in range(8):
        for n in range(3):
            first = (t // 4) * 384 + n * 128
            line[0, 3 * t + n : 3 * t + n + 1, :] = jnp.where(
                z == t % 4, projected[:, first : first + 128], 0.0
            )
    row = 24
    for piece in (
        sums_hidden[...],
        sums[0:1, :],
        sums[1:2, :],
        column_sum(normed_grad * scaled),
        column_sum(normed_grad),
        sums[2:3, :],
        sums[3:4, :],
        jnp.zeros((1, 128), FULL),
    ):
        for n in range(piece.shape[1] // 128):
            line[0, row : row + 1, :] = piece[:, n * 128 : (n + 1) * 128]
            row += 1
    head = lax.broadcasted_iota(jnp.int32, (8, 128), 1) - (2 * z + core)
    line[0, 96:104, :] = jnp.where(
        head == 0, peak[0:1, 0:1], jnp.where(head == 8, peak[1:2, 0:1], LOWEST)
    )

    def send_line(phase):
        return [
            start(line.at[phase], near_lines.at[phase, n], moved(at, ALL[phase], step))
            for n, step in enumerate(STEPS)
        ]

    def add_line(phase, begun):
        for copy in begun:
            copy.wait_recv()
        parts = [line[phase]] + [near_lines[phase, n] for n in range(3)]
        line[phase + 1, 0:96, :] = (parts[0][:96] + parts[1][:96]) + (parts[2][:96] + parts[3][:96])
        line[phase + 1, 96:104, :] = jnp.maximum(
            jnp.maximum(parts[0][96:], parts[1][96:]), jnp.maximum(parts[2][96:], parts[3][96:])
        )

    arriving = send_line(0)
    for s in behind:
        s.relay(1)
    add_line(0, arriving)
    arriving = send_line(1)
    for s in behind:
        s.finish(1)
        s.last()
    for s in last:
        s.finish(0)
        s.last()
    add_line(1, arriving)
    arriving = send_line(2)
    for k, s in enumerate(behind):
        s.result(unit, [STARTS[n + 1] for n in STREAMS[k // 3]])
    for s in last:
        s.result(unit, [0])
    mine = pl.ds(pl.multiple_of(core * 72, 8), 72)
    theirs = pl.ds(pl.multiple_of((1 - core) * 72, 8), 72)
    late = start(unit.at[theirs], other, sibling)
    add_line(2, arriving)
    line_copy = start(line.at[3], totals.at[core], sibling)
    totals[core] = line[3]
    out[core] = unit[mine, :]
    late.wait_recv()
    out[1 - core] = other[...]
    line_copy.wait_recv()
    for copy in sent + [copy for s in behind + last for copy in s.sent]:
        copy.wait_send()


def backward(heads_grad, heads, consts, both_ids, logsum, grids, weights, n1t, tokens, middle_grad, sums_hidden, sums, peak):
    count = 4 + 6 + 9 + 2 + 3 * 45 + 2 * 15
    shapes = []
    for names in STREAMS:
        for part in PARTS_BACK:
            shapes += Scatter.shapes([WIDTHS[n + 1] for n in names], part, True)
    for part in PARTS:
        shapes += Scatter.shapes([256], part, False)
    half = (256, 1152)
    return pl.pallas_call(
        backward_kernel,
        out_shape=[
            jax.ShapeDtypeStruct(half, FULL),
            jax.ShapeDtypeStruct((2, 72, UNIT), FULL),
            jax.ShapeDtypeStruct((2, 104, 128), FULL),
        ],
        in_specs=[vmem()] + [anywhere()] * 3 + [vmem()] * 3 + [anywhere()] * 5 + [vmem(), anywhere()] + [vmem()] * 3,
        out_specs=[vmem()] * 3,
        scratch_shapes=[
            pltpu.VMEM((4, 1024, 128), LOW),
            pltpu.VMEM((4, 1024, 128), LOW),
            pltpu.VMEM((4, 1024, 128), LOW),
            pltpu.VMEM((1152, 768), LOW),
            pltpu.VMEM(half, FULL),
            pltpu.VMEM((4, 1024, 128), LOW),
            pltpu.VMEM((1152, 2048), LOW),
            pltpu.VMEM((4, 128, 1024), LOW),
            pltpu.VMEM((2, 1024, 128), FULL),
            pltpu.VMEM((2, 1024, 128), FULL),
            pltpu.VMEM((2048, 768), LOW),
            pltpu.VMEM((2, 1, 1024), FULL),
            pltpu.VMEM((2, 1024, 1), FULL),
            pltpu.VMEM((4,) + half, LOW),
            pltpu.VMEM((4,) + half, LOW),
            pltpu.VMEM(half, FULL),
            pltpu.VMEM(half, LOW),
            pltpu.VMEM(half, LOW),
            pltpu.VMEM(half, LOW),
            pltpu.VMEM((2, 4, 144, 512), LOW),
            pltpu.VMEM((144, UNIT), FULL),
            pltpu.VMEM((72, UNIT), FULL),
            pltpu.VMEM((4, 104, 128), FULL),
            pltpu.VMEM((3, 3, 104, 128), FULL),
            pltpu.SemaphoreType.DMA((count,)),
            pltpu.SemaphoreType.DMA((count,)),
            pltpu.SemaphoreType.DMA((64,)),
        ]
        + shapes,
        compiler_params=pltpu.CompilerParams(
            collective_id=1, has_side_effects=True, vmem_limit_bytes=60 << 20
        ),
        name="backward_attention",
    )(
        heads_grad, *heads, consts, both_ids, logsum, *grids, weights, n1t, tokens, middle_grad, sums_hidden, sums,
        peak,
    )


def finish_kernel(
    grads, totals, query_weight, key_weight, result_in, token_in,
    result, token_grad, query_w, key_w, value_w, out_w, up_w, down_w_t, query_b, value_b, up_b, *rest
):
    vectors, (query_clip, key_clip, held, local) = rest[:6], rest[6:]
    loads = [
        pltpu.make_async_copy(result_in, held.at[0], local.at[0]),
        pltpu.make_async_copy(token_in, held.at[1], local.at[1]),
    ]
    stores = [
        pltpu.make_async_copy(held.at[0], result, local.at[2]),
        pltpu.make_async_copy(held.at[1], token_grad, local.at[3]),
    ]
    for copy in loads:
        copy.start()
    tensor = lax.axis_index("tensor")
    lane = lax.broadcasted_iota(jnp.int32, (72, 256), 1)

    def heads(start):
        first, second = (shifted(grads[c, :, 0:384], (384 - start) % 384, 384)[:, :128] for c in range(2))
        return jnp.where(lane < HEAD_DIM, shifted(first, 0, 256), shifted(second, HEAD_DIM, 256))

    query_w[...] = heads(0)[:, :144]
    key_w[...] = heads(72)[:, :144]
    value_w[...] = heads(144)[:, :144]
    out_w[...] = heads(256).T[:144, :]
    wide = lax.broadcasted_iota(jnp.int32, (72, 640), 1)

    def hidden(main, tail):
        total = jnp.zeros((72, 640), FULL)
        for c in range(2):
            last = shifted(grads[c, :, 256:384], (128 - tail) % 128, 128)
            base = c * (MAIN + TAIL)
            block = jnp.concatenate(
                [grads[c, :, main : main + 128], grads[c, :, main + 256 : main + 384], last], axis=1
            )
            inside = (wide >= base) & (wide < base + MAIN + TAIL)
            total = jnp.where(inside, shifted(block, base, 640), total)
        return total

    up_w[...] = hidden(384, 72)[:, :538]
    down_w_t[...] = hidden(512, 72 + TAIL)[:, :538]
    for load, copy in zip(loads, stores):
        load.wait()
        copy.start()

    def line_up(target, pieces, size, width):
        lane = lax.broadcasted_iota(jnp.int32, (1, width), 1)
        total = jnp.zeros((1, width), FULL)
        for n, piece in enumerate(pieces):
            inside = (lane >= size * n) & (lane < size * (n + 1))
            total = jnp.where(inside, shifted(piece, size * n, width), total)
        for k in range(width // 128):
            target[k : k + 1, :] = total[:, 128 * k : 128 * (k + 1)]

    order = [(t, c) for t in range(8) for c in range(2)]
    line_up(query_b, [totals[c, 3 * t : 3 * t + 1, :] for t, c in order], HEAD_DIM, 1152)
    line_up(value_b, [totals[c, 3 * t + 2 : 3 * t + 3, :] for t, c in order], HEAD_DIM, 1152)
    line_up(
        up_b,
        [
            jnp.concatenate(
                [
                    totals[c, 24 + t : 25 + t, :],
                    totals[c, 32 + t : 33 + t, :],
                    shifted(totals[c, 40:41, :], (128 - TAIL * t) % 128, 128),
                ],
                axis=1,
            )
            for t, c in order
        ],
        MAIN + TAIL,
        34 * 128,
    )
    for n in range(6):
        rows = slice(41 + 9 * n, 50 + 9 * n)
        vectors[n][...] = totals[0, rows, :] + totals[1, rows, :]
    peak = jnp.maximum(totals[0, 96:97, :], totals[1, 96:97, :])
    factor = jnp.sqrt(CLIP_LIMIT / jnp.maximum(peak, CLIP_LIMIT))
    spot = lax.broadcasted_iota(jnp.int32, (1, 128), 1)
    low, high = (
        jnp.sum(jnp.where(spot == 2 * tensor + c, factor, 0.0), axis=1, keepdims=True) for c in range(2)
    )
    scale = jnp.where(lax.broadcasted_iota(jnp.int32, (1, 144), 1) < HEAD_DIM, low, high)
    query_clip[...] = query_weight[...].astype(FULL) * scale
    key_clip[...] = key_weight[...].astype(FULL) * scale
    for copy in stores:
        copy.wait()


def finish(grads, totals, query_weight, key_weight, result, token_grad):
    shapes = [(256, 1152)] * 2 + [(72, 144)] * 3 + [(144, 72), (72, 538), (72, 538)]
    shapes += [(9, 128)] * 2 + [(34, 128)] + [(9, 128)] * 6 + [(72, 144)] * 2
    return pl.pallas_call(
        finish_kernel,
        out_shape=[jax.ShapeDtypeStruct(shape, FULL) for shape in shapes],
        in_specs=[vmem()] * 4 + [hbm()] * 2,
        out_specs=[hbm()] * 2 + [vmem()] * 17,
        scratch_shapes=[pltpu.VMEM((2, 256, 1152), FULL), pltpu.SemaphoreType.DMA((4,))],
        compiler_params=pltpu.CompilerParams(vmem_limit_bytes=60 << 20),
        name="finish_outputs",
    )(grads, totals, query_weight, key_weight, result, token_grad)


def per_device(
    tokens,
    picture,
    cotangent,
    gain_one,
    shift_one,
    query_weight,
    query_bias,
    key_weight,
    value_weight,
    value_bias,
    out_weight,
    out_bias,
    gain_two,
    shift_two,
    up_weight,
    up_bias,
    down_weight,
    down_bias,
):
    row = lax.broadcasted_iota(jnp.int32, (8, tokens.shape[1]), 0)
    consts = jnp.zeros(row.shape, LOW)
    vectors = (out_bias, gain_two, shift_two, down_bias, gain_one, shift_one, query_bias, value_bias)
    for k, vector in enumerate(vectors):
        consts = jnp.where(row == k, vector[None, :], consts)
    consts = consts.astype(FULL)
    weights = (query_weight, key_weight, value_weight, out_weight, up_weight, down_weight.T)
    result, middle_grad, *rest = forward(
        weights, consts, jnp.pad(up_bias.astype(FULL), (0, 48)).reshape(34, 128), picture.reshape(16, 128), cotangent, tokens
    )
    grids, (rows_one_t, head_weights), heads = rest[:3], rest[3:5], rest[5:8]
    heads_grad, both_ids, logsum, peak, sums_hidden, sums = rest[8:]
    input_grad, grads, totals = backward(
        heads_grad,
        heads,
        consts,
        both_ids,
        logsum,
        grids,
        head_weights,
        rows_one_t,
        tokens,
        middle_grad,
        sums_hidden,
        sums,
        peak,
    )
    outputs = finish(grads, totals, query_weight, key_weight, result, input_grad)
    return (
        *outputs[:7],
        outputs[7].T,
        *(vector.reshape(-1) for vector in outputs[8:10]),
        outputs[10].reshape(-1)[: 8 * 538],
        *(vector.reshape(-1) for vector in outputs[11:17]),
        *outputs[17:],
    )


def solution(mesh):
    in_specs = (
        P(("dp", "tensor"), None),
        P("dp"),
        P(("dp", "tensor"), None),
        P(),
        P(),
        P("dp", "tensor"),
        P(),
        P("dp", "tensor"),
        P("dp", "tensor"),
        P(),
        P("tensor", "dp"),
        P(),
        P(),
        P(),
        P("dp", "tensor"),
        P(),
        P("tensor", "dp"),
        P(),
    )
    out_specs = (
        P(("dp", "tensor"), None),
        P(("dp", "tensor"), None),
        P("dp", "tensor"),
        P("dp", "tensor"),
        P("dp", "tensor"),
        P("tensor", "dp"),
        P("dp", "tensor"),
        P("tensor", "dp"),
        P(),
        P(),
        P(),
        P(),
        P(),
        P(),
        P(),
        P(),
        P(),
        P("dp", "tensor"),
        P("dp", "tensor"),
    )
    return jax.shard_map(
        per_device, mesh=mesh, in_specs=in_specs, out_specs=out_specs, check_vma=False
    )
```
